32 devices in a mesh: dp: 8 (over z, y), mp: 4 (over x, core).
Axes of the slice: x: 2, y: 2, z: 4, core: 2. Of those that a mesh axis runs over, the one named last changes fastest.
Arguments:
- tokens_in: bfloat16 [8192, 768], P(('dp', 'mp')), may hold values from -6 to 6
- segments: int32 [8, 1024], P('dp'), may hold values from 0 to 15, never falling along the last dimension, each value on 1 to 128 neighbouring positions
- pairing: int32 [128], P('dp'), may hold values from 0 to 127, as said below
- drop_masks: int32 [2, 2, 8192, 768], P(None, None, ('dp', 'mp')), may hold values 0 or 1
- w_qkv: bfloat16 [2, 3, 768, 768], P(None, None, 'dp', 'mp'), may hold values from -0.21875 to 0.21875
- w_out: bfloat16 [2, 768, 768], P(None, ('mp', 'dp')), may hold values from -1.75 to 1.75
- w_in: bfloat16 [2, 768, 3072], P(None, 'dp', 'mp'), may hold values from -0.21875 to 0.21875
- w_back: bfloat16 [2, 3072, 768], P(None, ('mp', 'dp')), may hold values from -0.109375 to 0.109375
- b_in: bfloat16 [2, 3072], P(None, ('mp', 'dp')), may hold values from -0.59765625 to 0.59765625
- biases: bfloat16 [2, 6, 768], P(None, None, 'dp'), may hold values from -0.59765625 to 0.59765625
- gains: bfloat16 [2, 2, 768], P(None, None, 'dp'), may hold values from 0.5 to 1.5
- pool_w: bfloat16 [768, 768], P('dp'), may hold values from -0.21875 to 0.21875
- pool_b: bfloat16 [768], P('dp'), may hold values from -0.59765625 to 0.59765625
Outputs:
- loss: float32 [128], P('dp')
- alignment: float32 [128], P('dp')
- uniformity: float32 [128], P('dp')
- grad_x: float32 [8192, 768], P(('dp', 'mp'))
- grad_w_qkv: float32 [2, 3, 768, 768], P(None, None, 'dp', 'mp')
- grad_w_out: float32 [2, 768, 768], P(None, ('mp', 'dp'))
- grad_w_in: float32 [2, 768, 3072], P(None, 'dp', 'mp')
- grad_w_back: float32 [2, 3072, 768], P(None, ('mp', 'dp'))
- grad_b_in: float32 [2, 3072], P(None, ('mp', 'dp'))
- grad_biases: float32 [2, 6, 768], P(None, None, ('dp', 'mp'))
- grad_gains: float32 [2, 2, 768], P(None, None, ('dp', 'mp'))
- grad_pool_w: float32 [768, 768], P('dp')
- grad_pool_b: float32 [768], P('dp')
The draws below stay inside these ranges and needn't reach their ends.
Inputs may be any that keep to these rules, and one draw needn't show every extreme that they name: `segments`: along each row the segment numbers never fall, and each of the 16 numbers names a run of 1 to 128 positions. pairing[pairing[i]] = i and pairing[i] != i; pooled sentence i is sentence i % 16 of row i // 16.
All inputs are finite; a program needn't handle non-finite values. No bound on the sum of `drop_masks` on one device may be relied on, other than what follows from the above.
Results may differ from the reference program's by a relative error of at most 0.035.
Values may be sent and summed in bfloat16 or wider, within the bound.
A program may use at most 256 MiB of HBM per device.

```python
import math
import jax
import jax.numpy as jnp
import numpy as np
from jax import lax

D = 768
HEADS = 12
HEAD_DIM = 64
FF = 3072
LAYERS = 2
SEQ_LEN = 1024
SEGS = 16
SEG_MOST = 128
ROWS = 8
TOKENS = 8192
NPOOL = 128


def draw_pairing(key, part):
    key = jax.random.fold_in(key, 7)
    order = jax.random.permutation(key, NPOOL).astype(jnp.int32)
    couples = order.reshape(NPOOL // 2, 2)
    partner = jnp.zeros((NPOOL,), jnp.int32)
    partner = partner.at[couples[:, 0]].set(couples[:, 1])
    partner = partner.at[couples[:, 1]].set(couples[:, 0])
    return partner


def plant(values, key, low, top_value):
    spot = [jax.random.randint(jax.random.fold_in(key, axis), (), 0, length) for axis, length in enumerate(values.shape)]
    main_axis = values.shape.index(max(values.shape))
    neighbour = spot[:main_axis] + [(spot[main_axis] + 1) % values.shape[main_axis]] + spot[main_axis + 1:]
    return values.at[tuple(spot)].set(low).at[tuple(neighbour)].set(top_value)


def steps_of(stream_key, dims, split, smallest, high):
    gain, own = 1.0, jax.random.fold_in(stream_key, 6)
    for position, blocks in split:
        steps = jnp.exp(jax.random.uniform(jax.random.fold_in(own, position), (blocks,), jnp.float32, smallest / len(split), high / len(split)))
        gain = gain * jnp.repeat(steps, dims[position] // blocks).reshape([-1 if axis == position else 1 for axis in range(len(dims))])
    return gain


def length_profile(number_of, total, reach, skew):
    weights = [(1 << 20) // math.isqrt(standing ** skew) + 1 for standing in range(2, number_of + 1)]
    rest, given = total - reach - (number_of - 1), [1] * (number_of - 1)
    while rest > 0:
        candidates = [i for i in range(number_of - 1) if given[i] < reach]
        mass, budget = sum([weights[i] for i in candidates]), rest
        for i in candidates:
            addition = min(reach - given[i], max(1, budget * weights[i] // mass), rest)
            given[i] = given[i] + addition
            rest = rest - addition
    return np.array([reach] + given)


def ragged(key, amount, total, reach, slope):
    if amount == 2:
        one = jax.random.randint(key, (), max(1, total - reach), min(reach, total - 1) + 1)
        return jnp.stack([one, total - one])
    sizes = jnp.asarray(length_profile(amount, total, reach, slope), jnp.int32)
    pairs = (amount - 1) // 2
    giver, sink = sizes[1:1 + 2 * pairs:2], sizes[2:2 + 2 * pairs:2]
    margin = jnp.minimum(giver - 1, reach - sink)
    shifted = jax.random.randint(jax.random.fold_in(key, 1), (pairs,), 0, 1 << 20) % (margin + 1)
    sizes = sizes.at[1:1 + 2 * pairs:2].set(giver - shifted).at[2:2 + 2 * pairs:2].set(sink + shifted)
    return sizes[jax.random.permutation(jax.random.fold_in(key, 2), amount)]


def scatter_about(stream_key, dims, scale, most, cuts=(), kind=jnp.bfloat16):
    result = jax.random.normal(stream_key, dims, jnp.float32) * scale
    if len(cuts) > 0:
        result = steps_of(stream_key, dims, cuts, -0.22, 0.18) * result
    return jnp.clip(result, min=-most, max=most).astype(kind)


def setup_inputs(seed: int = 0) -> dict:
    seeds = jax.random.split(jax.random.key(seed), 14)
    return {
        "tokens_in": scatter_about(seeds[0], (TOKENS, D), 1.0, 6.0, ((0, 32),)),
        "segments": jax.vmap(lambda own: jnp.searchsorted(jnp.cumsum(ragged(own, SEGS, SEQ_LEN, SEG_MOST, 2)), jnp.arange(SEQ_LEN), side="right"))(jax.random.split(seeds[1], ROWS)).reshape((ROWS, SEQ_LEN)).astype(jnp.int32),
        "pairing": draw_pairing(jax.random.fold_in(seeds[13], 71), 0),
        "drop_masks": plant((jax.random.randint(seeds[3], (LAYERS, 2, TOKENS, D), 0, 10) < 9).astype(jnp.int32), jax.random.fold_in(seeds[3], 1), 0, 1),
        "w_qkv": scatter_about(seeds[4], (LAYERS, 3, D, D), D ** -0.5, 0.21875, ((2, 8), (3, 4))),
        "w_out": scatter_about(seeds[5], (LAYERS, D, D), (D // 64) ** -0.5, 1.75, ((1, 32),)),
        "w_in": scatter_about(seeds[6], (LAYERS, D, FF), D ** -0.5, 0.21875, ((1, 8), (2, 4))),
        "w_back": scatter_about(seeds[7], (LAYERS, FF, D), FF ** -0.5, 0.109375, ((1, 32),)),
        "b_in": scatter_about(seeds[8], (LAYERS, FF), 0.1, 0.59765625, ((1, 32),)),
        "biases": scatter_about(seeds[9], (LAYERS, 6, D), 0.1, 0.59765625, ((2, 8),)),
        "gains": jnp.clip(1.0 + 0.1 * jax.random.normal(seeds[10], (LAYERS, 2, D), jnp.float32), 0.5, 1.5).astype(jnp.bfloat16),
        "pool_w": scatter_about(seeds[11], (D, D), D ** -0.5, 0.21875, ((0, 8),)),
        "pool_b": scatter_about(seeds[12], (D,), 0.1, 0.59765625, ((0, 8),)),
    }


@jax.custom_vjp
def low(v):
    return lax.optimization_barrier(v.astype(jnp.bfloat16)).astype(jnp.float32)

@jax.custom_vjp
def low_back(v):
    return v

def low_keep(v):
    return (low(v), None)

def low_pass(kept, grad):
    return (grad,)

def back_keep(v):
    return (v, None)

def back_low(kept, grad):
    return (low(grad),)
low.defvjp(low_keep, low_pass)
low_back.defvjp(back_keep, back_low)
TEMP = 0.05
EPS = 1e-06
KEEP = 0.9

def matmul32(left_side, right_side):
    return jnp.dot(left_side, right_side, precision=lax.Precision.HIGHEST)

def layer_norm(values, gain_row, shift_row):
    center = lax.optimization_barrier(jnp.mean(values, -1, keepdims=True))
    spread = lax.rsqrt(lax.optimization_barrier(jnp.mean(values * values, -1, keepdims=True)) - center * center + EPS)
    return (values - center) * spread * gain_row + shift_row

def encoder_block(hidden_in, labels, keep_masks, weights):
    w_three, w_proj, w_up, w_down, bias_up, shifts, scales = weights
    rows_low = low(hidden_in)
    queries = low(low_back(matmul32(rows_low, w_three[0]) + shifts[0]))
    keys_all = low(low_back(matmul32(rows_low, w_three[1])))
    values = low(low_back(matmul32(rows_low, w_three[2]) + shifts[1]))
    shape3 = (SEQ_LEN, HEADS, HEAD_DIM)
    scores = jnp.einsum('qhd,khd->hqk', queries.reshape(shape3), keys_all.reshape(shape3), precision=lax.Precision.HIGHEST) * HEAD_DIM ** (-0.5)
    scores = low_back(scores)
    same_doc = labels[:, None] == labels[None, :]
    scores = jnp.where(same_doc[None], scores, -1000000000.0)
    row_peak = lax.optimization_barrier(jnp.max(scores, -1, keepdims=True))
    exponent = jnp.exp(scores - row_peak)
    soft_probs = low(exponent / lax.optimization_barrier(jnp.sum(exponent, -1, keepdims=True)))
    attended = jnp.einsum('hqk,khd->qhd', soft_probs, values.reshape(shape3), precision=lax.Precision.HIGHEST).reshape(SEQ_LEN, D)
    attended = low(low_back(attended))
    mixed_out = low_back(matmul32(attended, w_proj)) + shifts[2]
    middle = layer_norm(hidden_in + keep_masks[0] * mixed_out / KEEP, scales[0], shifts[3])
    hidden = low_back(matmul32(low(middle), w_up) + bias_up)
    active = low(jax.nn.gelu(hidden, approximate=False))
    branch = low_back(matmul32(active, w_down)) + shifts[4]
    return layer_norm(middle + keep_masks[1] * branch / KEEP, scales[1], shifts[5])

def reference(tokens_in, segments, pairing, drop_masks, w_qkv, w_out, w_in, w_back, b_in, biases, gains, pool_w, pool_b):
    floats = (tokens_in.astype(jnp.float32), w_qkv.astype(jnp.float32), w_out.astype(jnp.float32), w_in.astype(jnp.float32), w_back.astype(jnp.float32), b_in.astype(jnp.float32), biases.astype(jnp.float32), gains.astype(jnp.float32), pool_w.astype(jnp.float32), pool_b.astype(jnp.float32))

    def forward(tokens32, w_qkv32, w_out32, w_in32, w_back32, b_in32, biases32, gains32, pool_w32, pool_b32):

        def one_row(row_index):
            row_start = row_index * SEQ_LEN
            hidden = lax.dynamic_slice_in_dim(tokens32, row_start, SEQ_LEN, 0)
            labels = segments[row_index]
            keep_all = lax.dynamic_slice_in_dim(drop_masks, row_start, SEQ_LEN, 2).astype(jnp.float32)
            for layer_index in range(LAYERS):
                hidden = encoder_block(hidden, labels, keep_all[layer_index], (w_qkv32[layer_index], w_out32[layer_index], w_in32[layer_index], w_back32[layer_index], b_in32[layer_index], biases32[layer_index], gains32[layer_index]))
            numbers = jnp.arange(SEGS, dtype=jnp.int32)
            starts = lax.optimization_barrier(jnp.sum((labels[None, :] < numbers[:, None]).astype(jnp.int32), 1))
            before = low_back(matmul32(low(hidden[starts]), pool_w32) + pool_b32)
            pooled = jnp.tanh(before)
            return pooled * lax.rsqrt(lax.optimization_barrier(jnp.sum(pooled * pooled, -1, keepdims=True)) + EPS)
        unit_rows = lax.map(jax.checkpoint(one_row), jnp.arange(ROWS, dtype=jnp.int32)).reshape(NPOOL, D)
        unit_rows = low(unit_rows)
        gram_raw = low_back(jnp.dot(unit_rows, unit_rows.T, precision=lax.Precision.HIGHEST))
        logits = gram_raw / TEMP
        columns = jnp.arange(NPOOL, dtype=jnp.int32)
        self_mask = columns[None, :] == columns[:, None]
        pair_mask = columns[None, :] == pairing[:, None]
        masked = jnp.where(self_mask, -1000000000.0, logits)
        row_peak = lax.optimization_barrier(jnp.max(masked, 1, keepdims=True))
        totals = lax.optimization_barrier(jnp.sum(jnp.exp(masked - row_peak), 1))
        loss_rows = row_peak[:, 0] + jnp.log(totals) - lax.optimization_barrier(jnp.sum(jnp.where(pair_mask, logits, 0.0), 1))
        squares = lax.optimization_barrier(jnp.sum(unit_rows * unit_rows, 1))
        distance = squares[:, None] + squares[None, :] - 2.0 * gram_raw
        align_rows = lax.optimization_barrier(jnp.sum(jnp.where(pair_mask, distance, 0.0), 1))
        unif_rows = jnp.log(lax.optimization_barrier(jnp.sum(jnp.where(self_mask, 0.0, jnp.exp(-2.0 * distance)), 1)) / (NPOOL - 1))
        return (jnp.sum(loss_rows), (loss_rows, align_rows, unif_rows))
    loss_sum, back_fn, metrics = jax.vjp(forward, *floats, has_aux=True)
    gradients = back_fn(jnp.ones_like(loss_sum))
    return (metrics[0], metrics[1], metrics[2], gradients[0], gradients[1], gradients[2], gradients[3], gradients[4], gradients[5], gradients[6], gradients[7], gradients[8], gradients[9])
```

```python
import functools

import jax
import jax.numpy as jnp
from jax import lax
from jax.experimental import pallas as pl
from jax.experimental.pallas import tpu as pltpu
from jax.sharding import Mesh
from jax.sharding import PartitionSpec as P

HEAD_DIM = 64
SEGS = 16
TEMP = 0.05
EPS = 1e-06
KEEP = 0.9
HALO = 128
MESH = pl.DeviceIdType.MESH
ANY = pl.BlockSpec(memory_space=pl.ANY)
VMEM = pl.BlockSpec(memory_space=pltpu.VMEM)
BF = jnp.bfloat16
F32 = jnp.float32
NZ = 4
NY = 2


def contract(left_side, right_side, left_dim, right_dim):
    return lax.dot_general(
        left_side,
        right_side,
        (((left_dim,), (right_dim,)), ((), ())),
        preferred_element_type=F32,
    )


def mm(a, b):
    return jnp.dot(a, b, preferred_element_type=F32)


def position():
    return tuple(lax.axis_index(name) for name in ("z", "y", "x", "c"))


def neighbours():
    x, c = lax.axis_index("x"), lax.axis_index("c")
    m = 2 * x + c
    left = {"x": jnp.where(c == 1, x, x - 1), "c": 1 - c}
    right = {"x": jnp.where(c == 0, x, x + 1), "c": 1 - c}
    return m, left, right


def signal(sem, device):
    pl.semaphore_signal(sem, inc=1, device_id=device, device_id_type=MESH)


def gather_kernel(nblk, *refs):
    ins = refs[:nblk]
    tok = refs[nblk]
    outs = refs[nblk + 1 : 2 * nblk + 1]
    halo = refs[2 * nblk + 1]
    zsend, xsend, ysend, csend, recv, own_sem, hsend, hrecv = refs[2 * nblk + 2 :]
    z, y, x, c = position()
    m, left, right = neighbours()
    up, down = z < NZ - 1, z > 0
    xdev, ydev, cdev = {"x": 1 - x}, {"y": 1 - y}, {"c": 1 - c}
    diag_halo = (m == 1) | (m == 2)
    diag_dev = {"x": 1 - x, "c": 1 - c}

    bar = pltpu.get_barrier_semaphore()
    signal(bar, xdev)
    signal(bar, ydev)
    signal(bar, cdev)

    @pl.when(up)
    def _():
        signal(bar, {"z": z + 1})

    @pl.when(down)
    def _():
        signal(bar, {"z": z - 1})

    @pl.when(diag_halo)
    def _():
        signal(bar, diag_dev)

    pl.semaphore_wait(
        bar, 3 + up.astype(jnp.int32) + down.astype(jnp.int32) + diag_halo.astype(jnp.int32)
    )

    def copy(b, src, slot, device, sem):
        return pltpu.make_async_remote_copy(
            src_ref=src,
            dst_ref=outs[b].at[slot],
            send_sem=sem,
            recv_sem=recv.at[(b, *slot)],
            device_id=device,
            device_id_type=MESH,
        )

    def arrived(b, slot):
        ref = outs[b].at[slot]
        pltpu.make_async_copy(ref, ref, recv.at[(b, *slot)]).wait()

    def halo_copies():
        return (
            (m > 0, pltpu.make_async_remote_copy(
                src_ref=tok.at[0:HALO], dst_ref=halo.at[1], send_sem=hsend.at[0], recv_sem=hrecv.at[1],
                device_id=left, device_id_type=MESH)),
            (m < 3, pltpu.make_async_remote_copy(
                src_ref=tok.at[tok.shape[0] - HALO :], dst_ref=halo.at[0], send_sem=hsend.at[1],
                recv_sem=hrecv.at[0], device_id=right, device_id_type=MESH)),
        )

    def x_first(b):
        return b % 2 == 0

    def fan_out(b, src, slot, k):
        copy(b, src, slot, xdev, xsend.at[b, k]).start()
        copy(b, src, slot, ydev, ysend.at[b, k]).start()
        copy(b, src, slot, cdev, csend.at[b, 0, k]).start()

    def z_events(b):
        src = ins[b]
        mine = (x, c, z, y)

        @pl.when(up)
        def _():
            copy(b, src, mine, {"z": z + 1}, zsend.at[b, 0]).start()

        @pl.when(down)
        def _():
            copy(b, src, mine, {"z": z - 1}, zsend.at[b, 1]).start()

        fan_out(b, src, mine, 0)
        pltpu.make_async_copy(src, outs[b].at[mine], own_sem.at[b]).start()

    def z_relay(b, d):
        @pl.when(z >= d)
        def _():
            slot = (x, c, z - d, y)
            arrived(b, slot)

            @pl.when(up)
            def _():
                copy(b, outs[b].at[slot], slot, {"z": z + 1}, zsend.at[b, 2 * d]).start()

            fan_out(b, outs[b].at[slot], slot, NZ - d)

        @pl.when(z < NZ - d)
        def _():
            slot = (x, c, z + d, y)
            arrived(b, slot)

            @pl.when(down)
            def _():
                copy(b, outs[b].at[slot], slot, {"z": z - 1}, zsend.at[b, 2 * d + 1]).start()

            fan_out(b, outs[b].at[slot], slot, d)

    def xy_relay(b, k):
        zp = lax.rem(z + k, NZ)
        sx, sy = (1 - x, c, zp, y), (x, c, zp, 1 - y)
        arrived(b, sx)
        if x_first(b):
            copy(b, outs[b].at[sx], sx, ydev, ysend.at[b, NZ + k]).start()
        copy(b, outs[b].at[sx], sx, cdev, csend.at[b, 1, k]).start()
        arrived(b, sy)
        if not x_first(b):
            copy(b, outs[b].at[sy], sy, xdev, xsend.at[b, NZ + k]).start()
        copy(b, outs[b].at[sy], sy, cdev, csend.at[b, 2, k]).start()

    def corner(b, k):
        zp = lax.rem(z + k, NZ)
        sd = (1 - x, c, zp, 1 - y)
        arrived(b, sd)
        copy(b, outs[b].at[sd], sd, cdev, csend.at[b, 3, k]).start()

    for cond, cp in halo_copies():
        pl.when(cond)(cp.start)

    for t in range(nblk + 2):
        if t < nblk:
            z_events(t)
            for d in range(1, NZ):
                z_relay(t, d)
        if 0 <= t - 1 < nblk:
            for k in range(NZ):
                xy_relay(t - 1, k)
        if 0 <= t - 2 < nblk:
            for k in range(NZ):
                corner(t - 2, k)

    for b in range(nblk):
        src = ins[b]
        mine = (x, c, z, y)
        pltpu.make_async_copy(src, outs[b].at[mine], own_sem.at[b]).wait()
        for k in range(NZ):
            zp = lax.rem(z + k, NZ)
            for xp in (x, 1 - x):
                for yp in (y, 1 - y):
                    arrived(b, (xp, 1 - c, zp, yp))
            copy(b, src, mine, xdev, xsend.at[b, k]).wait_send()
            copy(b, src, mine, ydev, ysend.at[b, k]).wait_send()
            if x_first(b):
                copy(b, src, mine, ydev, ysend.at[b, NZ + k]).wait_send()
            else:
                copy(b, src, mine, xdev, xsend.at[b, NZ + k]).wait_send()
            for kind in range(4):
                copy(b, src, mine, cdev, csend.at[b, kind, k]).wait_send()
        for d in range(NZ):

            @pl.when(up & (z >= d))
            def _():
                copy(b, src, mine, {"z": z + 1}, zsend.at[b, 2 * d]).wait_send()

            @pl.when(down & (z < NZ - d))
            def _():
                copy(b, src, mine, {"z": z - 1}, zsend.at[b, 2 * d + 1]).wait_send()

    (has_left, to_left), (has_right, to_right) = halo_copies()
    pl.when(has_left)(to_left.wait_send)
    pl.when(has_right)(to_right.wait_send)
    pl.when(has_left)(to_right.wait_recv)
    pl.when(has_right)(to_left.wait_recv)


def gather_all(blocks, tokens):
    nblk = len(blocks)
    outs = [jax.ShapeDtypeStruct((2, 2, NZ, NY, *b.shape), b.dtype) for b in blocks]
    dma = pltpu.SemaphoreType.DMA
    res = pl.pallas_call(
        functools.partial(gather_kernel, nblk),
        out_shape=outs + [jax.ShapeDtypeStruct((2, HALO, tokens.shape[1]), tokens.dtype)],
        in_specs=[ANY] * (nblk + 1),
        out_specs=[ANY] * (nblk + 1),
        scratch_shapes=[
            dma((nblk, 2 * NZ)),
            dma((nblk, 2 * NZ)),
            dma((nblk, 2 * NZ)),
            dma((nblk, 4, NZ)),
            dma((nblk, 2, 2, NZ, NY)),
            dma((nblk,)),
            dma((2,)),
            dma((2,)),
        ],
        compiler_params=pltpu.CompilerParams(collective_id=1, has_side_effects=True),
        name="gather_params",
    )(*blocks, tokens)
    return res[:nblk], res[nblk]


def halo_kernel(a_ref, o_ref, ssem, rsem):
    m, left, right = neighbours()
    has_left, has_right = m > 0, m < 3
    bar = pltpu.get_barrier_semaphore()
    pl.when(has_left)(lambda: signal(bar, left))
    pl.when(has_right)(lambda: signal(bar, right))
    pl.semaphore_wait(bar, has_left.astype(jnp.int32) + has_right.astype(jnp.int32))
    to_left = pltpu.make_async_remote_copy(
        src_ref=a_ref.at[0], dst_ref=o_ref.at[1], send_sem=ssem.at[0], recv_sem=rsem.at[1],
        device_id=left, device_id_type=MESH)
    to_right = pltpu.make_async_remote_copy(
        src_ref=a_ref.at[1], dst_ref=o_ref.at[0], send_sem=ssem.at[1], recv_sem=rsem.at[0],
        device_id=right, device_id_type=MESH)
    pl.when(has_left)(to_left.start)
    pl.when(has_right)(to_right.start)

    @pl.when(~has_left)
    def _():
        o_ref[0] = jnp.zeros_like(o_ref[0])

    @pl.when(~has_right)
    def _():
        o_ref[1] = jnp.zeros_like(o_ref[1])

    pl.when(has_left)(to_left.wait_send)
    pl.when(has_right)(to_right.wait_send)
    pl.when(has_left)(to_right.wait_recv)
    pl.when(has_right)(to_left.wait_recv)


def swap_halos(to_left, to_right, cid):
    both = jnp.stack([to_left, to_right])
    dma = pltpu.SemaphoreType.DMA
    return pl.pallas_call(
        halo_kernel,
        out_shape=jax.ShapeDtypeStruct(both.shape, both.dtype),
        in_specs=[VMEM],
        out_specs=VMEM,
        scratch_shapes=[dma((2,)), dma((2,))],
        compiler_params=pltpu.CompilerParams(collective_id=cid, has_side_effects=True),
        name=f"halo_{cid}",
    )(both)


def pooled_kernel(a_ref, o_ref, part, s1, r1, s2, r2):
    z, y, x, c = position()
    mates = ({"x": 1 - x}, {"c": 1 - c}, {"x": 1 - x, "c": 1 - c})
    peers = []
    for k in range(NZ):
        for flip in range(NY):
            if k or flip:
                peers.append((k * NY + flip, k, flip))

    def peer(k, flip):
        return {"z": lax.rem(z + k, NZ), "y": y if flip == 0 else 1 - y}

    bar = pltpu.get_barrier_semaphore()
    for dev in mates:
        signal(bar, dev)
    for _, k, flip in peers:
        signal(bar, peer(k, flip))
    pl.semaphore_wait(bar, len(mates) + len(peers))
    first = [
        pltpu.make_async_remote_copy(
            src_ref=a_ref, dst_ref=part.at[i], send_sem=s1.at[i], recv_sem=r1.at[i],
            device_id=dev, device_id_type=MESH)
        for i, dev in enumerate(mates)
    ]
    for cp in first:
        cp.start()
    for cp in first:
        cp.wait()
    row = a_ref[...].astype(F32)
    for i in range(len(mates)):
        row = row + part[i].astype(F32)
    here = o_ref.at[z, y]
    here[...] = row.astype(BF)
    second = [
        pltpu.make_async_remote_copy(
            src_ref=here, dst_ref=here, send_sem=s2.at[i], recv_sem=r2.at[i],
            device_id=peer(k, flip), device_id_type=MESH)
        for i, k, flip in peers
    ]
    for cp in second:
        cp.start()
    for cp in second:
        cp.wait_send()
    for i, k, flip in peers:
        there = o_ref.at[lax.rem(z + NZ - k, NZ), y if flip == 0 else 1 - y]
        pltpu.make_async_copy(there, there, r2.at[i]).wait()


def share_pooled(rows):
    dma = pltpu.SemaphoreType.DMA
    return pl.pallas_call(
        pooled_kernel,
        out_shape=jax.ShapeDtypeStruct((NZ, NY, *rows.shape), rows.dtype),
        in_specs=[VMEM],
        out_specs=VMEM,
        scratch_shapes=[
            pltpu.VMEM((3, *rows.shape), rows.dtype),
            dma((3,)), dma((3,)), dma((NZ * NY,)), dma((NZ * NY,)),
        ],
        compiler_params=pltpu.CompilerParams(collective_id=9, has_side_effects=True),
        name="share_pooled",
    )(rows)


def reduce_kernel(nblk, *refs):
    ins = refs[:nblk]
    outs = refs[nblk : 2 * nblk]
    scr = refs[2 * nblk :]
    own, rc, p1x, p1y, p2x, p2y, q, zu, zd = (scr[i * nblk : (i + 1) * nblk] for i in range(9))
    csend, crecv, lsem, s1, r1, s2, r2, zs, zr = scr[9 * nblk :]
    z, y, x, c = position()
    up, down = z < NZ - 1, z > 0
    xdev, ydev, cdev = {"x": 1 - x}, {"y": 1 - y}, {"c": 1 - c}

    bar = pltpu.get_barrier_semaphore()
    signal(bar, xdev)
    signal(bar, ydev)
    signal(bar, cdev)
    pl.when(up)(lambda: signal(bar, {"z": z + 1}))
    pl.when(down)(lambda: signal(bar, {"z": z - 1}))
    pl.semaphore_wait(bar, 3 + up.astype(jnp.int32) + down.astype(jnp.int32))

    def remote(src, dst, ss, rs, dev):
        return pltpu.make_async_remote_copy(
            src_ref=src, dst_ref=dst, send_sem=ss, recv_sem=rs, device_id=dev, device_id_type=MESH)

    def add(a, b):
        return (a.astype(F32) + b.astype(F32)).astype(a.dtype)

    def core_copies(b):
        return [remote(ins[b].at[i, 1 - c], rc[b].at[i], csend.at[b, i], crecv.at[b, i], cdev) for i in range(2)]

    def local_copies(b):
        return [pltpu.make_async_copy(ins[b].at[i, c], own[b].at[i], lsem.at[b, i]) for i in range(2)]

    def half(b):
        return ins[b].shape[4] // 2

    def first_x(b):
        h = half(b)
        return remote(own[b].at[1 - x, :, :, 0:h], p1x[b], s1.at[b, 0], r1.at[b, 0], xdev)

    def first_y(b):
        h = half(b)
        return remote(own[b].at[:, :, 1 - y, h:], p1y[b], s1.at[b, 1], r1.at[b, 1], ydev)

    def second_y(b):
        h = half(b)
        return remote(own[b].at[x, :, 1 - y, 0:h], p2y[b], s2.at[b, 0], r2.at[b, 0], ydev)

    def second_x(b):
        h = half(b)
        return remote(own[b].at[1 - x, :, y, h:], p2x[b], s2.at[b, 1], r2.at[b, 1], xdev)

    def stage0(b):
        for cp in core_copies(b) + local_copies(b):
            cp.start()

    def stage1(b):
        for cp in core_copies(b):
            cp.wait_recv()
        for cp in local_copies(b):
            cp.wait()

        @pl.loop(0, NZ)
        def _(k):
            for i in range(2):
                own[b][i, k] = add(own[b][i, k], rc[b][i, k])

        first_x(b).start()
        first_y(b).start()

    def stage2(b):
        h = half(b)
        first_x(b).wait_recv()
        first_y(b).wait_recv()

        @pl.loop(0, NZ)
        def _(k):
            a = own[b].at[x, k, :, 0:h]
            a[...] = add(a[...], p1x[b][k])
            for i in range(2):
                a = own[b].at[i, k, y, h:]
                a[...] = add(a[...], p1y[b][i, k])

        second_y(b).start()
        second_x(b).start()

    def zcopy(b, j, upward):
        if upward:
            return remote(q[b].at[0, z + j], zu[b].at[z + j], zs.at[b, 0, j], zr.at[b, 0, j], {"z": z + 1})
        return remote(q[b].at[1, z - j], zd[b].at[z - j], zs.at[b, 1, j], zr.at[b, 1, j], {"z": z - 1})

    def zarrived(b, j, upward):
        if upward:
            ref = zu[b].at[z + j]
            pltpu.make_async_copy(ref, ref, zr.at[b, 0, j + 1]).wait()
        else:
            ref = zd[b].at[z - j]
            pltpu.make_async_copy(ref, ref, zr.at[b, 1, j + 1]).wait()

    def stage3(b):
        h = half(b)
        second_y(b).wait_recv()
        second_x(b).wait_recv()

        @pl.loop(0, NZ)
        def _(k):
            lo = add(own[b][x, k, y, 0:h], p2y[b][k])
            hi = add(own[b][x, k, y, h:], p2x[b][k])
            for d in range(2):
                q[b][d, k, 0:h] = lo
                q[b][d, k, h:] = hi

        for j in range(NZ - 1, 0, -1):

            @pl.when(z + j < NZ)
            def _():
                @pl.when(down)
                def _():
                    zarrived(b, j, True)
                    q[b][0, z + j] = add(q[b][0, z + j], zu[b][z + j])

                zcopy(b, j, True).start()

            @pl.when(z - j >= 0)
            def _():
                @pl.when(up)
                def _():
                    zarrived(b, j, False)
                    q[b][1, z - j] = add(q[b][1, z - j], zd[b][z - j])

                zcopy(b, j, False).start()

    def stage4(b):
        outs[b][...] = q[b][0, z].astype(F32)

        @pl.when(down)
        def _():
            zarrived(b, 0, True)
            outs[b][...] += zu[b][z].astype(F32)

        @pl.when(up)
        def _():
            zarrived(b, 0, False)
            outs[b][...] += zd[b][z].astype(F32)

    for t in range(nblk + 4):
        if t < nblk:
            stage0(t)
        if 0 <= t - 1 < nblk:
            stage1(t - 1)
        if 0 <= t - 2 < nblk:
            stage2(t - 2)
        if 0 <= t - 3 < nblk:
            stage3(t - 3)
        if 0 <= t - 4 < nblk:
            stage4(t - 4)

    for b in range(nblk):
        for cp in core_copies(b):
            cp.wait_send()
        for cp in (first_x(b), first_y(b), second_y(b), second_x(b)):
            cp.wait_send()
        for j in range(1, NZ):
            pl.when(z + j < NZ)(lambda: zcopy(b, j, True).wait_send())
            pl.when(z - j >= 0)(lambda: zcopy(b, j, False).wait_send())


def reduce_all(blocks):
    nblk = len(blocks)
    dma = pltpu.SemaphoreType.DMA

    def scratch(shape_of):
        return [pltpu.VMEM(shape_of(*b.shape[4:]), b.dtype) for b in blocks]

    return pl.pallas_call(
        functools.partial(reduce_kernel, nblk),
        out_shape=[jax.ShapeDtypeStruct(b.shape[4:], F32) for b in blocks],
        in_specs=[ANY] * nblk,
        out_specs=[VMEM] * nblk,
        scratch_shapes=scratch(lambda r, w: (2, NZ, NY, r, w))
        + scratch(lambda r, w: (2, NZ, NY, r, w))
        + scratch(lambda r, w: (NZ, NY, r // 2, w))
        + scratch(lambda r, w: (2, NZ, r // 2, w))
        + scratch(lambda r, w: (NZ, r // 2, w))
        + scratch(lambda r, w: (NZ, r // 2, w))
        + scratch(lambda r, w: (2, NZ, r, w))
        + scratch(lambda r, w: (NZ, r, w))
        + scratch(lambda r, w: (NZ, r, w))
        + [
            dma((nblk, 2)), dma((nblk, 2)), dma((nblk, 2)),
            dma((nblk, 2)), dma((nblk, 2)), dma((nblk, 2)), dma((nblk, 2)),
            dma((nblk, 2, NZ)), dma((nblk, 2, NZ)),
        ],
        compiler_params=pltpu.CompilerParams(
            collective_id=2, has_side_effects=True, vmem_limit_bytes=60 << 20
        ),
        name="reduce_grads",
    )(*blocks)


def gelu_exact(values):
    return jax.nn.gelu(values, approximate=False)


def norm_forward(residual, gain_row, shift_row):
    center = jnp.mean(residual, 1)
    spread = lax.rsqrt(jnp.mean(residual * residual, 1) - center * center + EPS)
    normed = (residual - center[:, None]) * spread[:, None]
    return (normed * gain_row + shift_row, normed, spread)


def norm_backward(grad_out, gain_row, normed, spread):
    scaled = grad_out * gain_row
    first_mean = jnp.mean(scaled, 1)
    second_mean = jnp.mean(scaled * normed, 1)
    grad_in = spread[:, None] * (scaled - first_mean[:, None] - normed * second_mean[:, None])
    return (grad_in, jnp.sum(grad_out * normed, 0), jnp.sum(grad_out, 0))


def heads_of(values):
    return values.reshape(values.shape[0], -1, HEAD_DIM)


def layer_forward(residual, halo, weights, keep_masks, same_doc):
    w_q, w_k, w_v, w_proj, w_up, w_down, bias_up, shifts, scales = weights
    own = residual.astype(BF)
    window = jnp.concatenate([halo[0], own, halo[1]], 0)
    queries = heads_of((mm(own, w_q) + shifts[0]).astype(BF))
    keys = heads_of(mm(window, w_k).astype(BF))
    values = heads_of((mm(window, w_v) + shifts[1]).astype(BF))
    scores = jnp.einsum("qhd,khd->hqk", queries, keys, preferred_element_type=F32) * HEAD_DIM**-0.5
    scores = jnp.where(same_doc[None], scores, -1000000000.0)
    row_peak = jnp.max(scores, -1, keepdims=True)
    exponent = jnp.exp(scores - row_peak)
    totals = jnp.sum(exponent, -1, keepdims=True)
    soft_probs = (exponent / totals).astype(BF)
    log_sums = row_peak + jnp.log(totals)
    attended = jnp.einsum("hqk,khd->qhd", soft_probs, values, preferred_element_type=F32)
    attended = attended.astype(BF).reshape(own.shape)
    mixed_out = mm(attended, w_proj) + shifts[2]
    middle, normed_one, spread_one = norm_forward(
        residual + keep_masks[0] * mixed_out / KEEP, scales[0], shifts[3]
    )
    middle_low = middle.astype(BF)
    hidden = mm(middle_low, w_up) + bias_up
    active = gelu_exact(hidden).astype(BF)
    branch = mm(active, w_down) + shifts[4]
    output, normed_two, spread_two = norm_forward(
        middle + keep_masks[1] * branch / KEEP, scales[1], shifts[5]
    )
    saved = (window, queries, keys, values, attended, log_sums, normed_one, spread_one,
             middle_low, hidden, active, normed_two, spread_two)
    return output, saved


def layer_backward(grad_out, weights, keep_masks, saved, same_doc, cid):
    w_q, w_k, w_v, w_proj, w_up, w_down, bias_up, shifts, scales = weights
    (window, queries, keys, values, attended, log_sums, normed_one, spread_one,
     middle_low, hidden, active, normed_two, spread_two) = saved
    rows = grad_out.shape[0]
    grad_two, gain_two, shift_two = norm_backward(grad_out, scales[1], normed_two, spread_two)
    grad_branch = grad_two * keep_masks[1] / KEEP
    bias_down = jnp.sum(grad_branch, 0)
    branch_low = grad_branch.astype(BF)
    grad_active = contract(branch_low, w_down, 1, 1)
    grad_down = contract(active, branch_low, 0, 0).astype(BF)
    grad_hidden = jax.vjp(gelu_exact, hidden)[1](grad_active)[0].astype(BF)
    grad_bias_up = jnp.sum(grad_hidden.astype(F32), 0)
    grad_up = contract(middle_low, grad_hidden, 0, 0).astype(BF)
    grad_middle = grad_two + contract(grad_hidden, w_up, 1, 1)
    grad_one, gain_one, shift_one = norm_backward(grad_middle, scales[0], normed_one, spread_one)
    grad_mixed = grad_one * keep_masks[0] / KEEP
    bias_proj = jnp.sum(grad_mixed, 0)
    mixed_low = grad_mixed.astype(BF)
    grad_proj = contract(attended, mixed_low, 0, 0).astype(BF)
    grad_att = heads_of(contract(mixed_low, w_proj, 1, 1).astype(BF))
    scores = jnp.einsum("qhd,khd->hqk", queries, keys, preferred_element_type=F32) * HEAD_DIM**-0.5
    scores = jnp.where(same_doc[None], scores, -1000000000.0)
    soft_probs = jnp.exp(scores - log_sums)
    grad_v = jnp.einsum("hqk,qhd->khd", soft_probs.astype(BF), grad_att, preferred_element_type=F32)
    grad_probs = jnp.einsum("qhd,khd->hqk", grad_att, values, preferred_element_type=F32)
    inner_sum = jnp.sum(soft_probs * grad_probs, -1, keepdims=True)
    grad_scores = (soft_probs * (grad_probs - inner_sum)).astype(BF)
    grad_q = jnp.einsum("hqk,khd->qhd", grad_scores, keys, preferred_element_type=F32) * HEAD_DIM**-0.5
    grad_k = jnp.einsum("hqk,qhd->khd", grad_scores, queries, preferred_element_type=F32) * HEAD_DIM**-0.5
    grad_q = grad_q.astype(BF).reshape(rows, -1)
    grad_k = grad_k.astype(BF).reshape(window.shape)
    grad_v = grad_v.astype(BF).reshape(window.shape)
    own = window[HALO : HALO + rows]
    grad_wq = contract(own, grad_q, 0, 0).astype(BF)
    grad_wk = contract(window, grad_k, 0, 0).astype(BF)
    grad_wv = contract(window, grad_v, 0, 0).astype(BF)
    grad_window = contract(grad_k, w_k, 1, 1) + contract(grad_v, w_v, 1, 1)
    edges = grad_window.astype(BF)
    swapped = swap_halos(edges[:HALO], edges[HALO + rows :], cid)
    grad_in = grad_one + contract(grad_q, w_q, 1, 1) + grad_window[HALO : HALO + rows]
    grad_in = grad_in + jnp.concatenate([swapped[0], swapped[1]], 0).astype(F32)
    bias_q = jnp.sum(grad_q.astype(F32), 0)
    bias_v = jnp.sum(grad_v.astype(F32), 0)
    grad_shifts = jnp.stack([bias_q, bias_v, bias_proj, shift_one, bias_down, shift_two])
    grad_scales = jnp.stack([gain_one, gain_two])
    return grad_in, (grad_wq, grad_wk, grad_wv, grad_proj, grad_up, grad_down, grad_bias_up, grad_shifts, grad_scales)


def unit_rows(values):
    return values * lax.rsqrt(jnp.sum(values * values, 1, keepdims=True) + EPS)


def per_device(tokens_in, segments, pairing, drop_masks, w_qkv, w_out, w_in, w_back, b_in, biases,
               gains, pool_w, pool_b):
    inner = lax.axis_size("g")
    layers = w_qkv.shape[0]
    width = tokens_in.shape[1]
    local_rows = tokens_in.shape[0]
    z, y, x, c = position()
    m = 2 * x + c
    dp = (z * NY + y) * inner + lax.axis_index("g")

    def group(arr, dim):
        return arr if inner == 1 else lax.all_gather(arr, "g", axis=dim, tiled=True)

    w_qkv, w_out, w_in, w_back = group(w_qkv, 2), group(w_out, 1), group(w_in, 1), group(w_back, 1)
    b_in, biases, gains = group(b_in, 1), group(biases, 2), group(gains, 2)
    pool_w, pool_b, pairing = group(pool_w, 0), group(pool_b, 0), group(pairing, 0)
    rows = w_in.shape[1]
    part = w_qkv.shape[3]
    rows_out = w_out.shape[1]
    fold = width // part
    spare = rows_out * width // (3 * rows)

    side = w_out.reshape(layers, rows_out * fold, 3, spare)
    main = jnp.moveaxis(w_qkv, 1, 2)
    block_a = jnp.concatenate([main, side], 3).reshape(layers, rows, -1)
    smalls = [b_in, biases.reshape(-1, rows), gains.reshape(-1, rows), pool_b[None]]
    smalls = jnp.concatenate([s.astype(F32) for s in smalls], 0)
    smalls = jnp.pad(smalls, ((0, 0), (0, 128 - rows)))
    pair_row = jnp.pad(pairing.astype(F32), (0, 128 - pairing.shape[0]))[None]
    smalls = jnp.concatenate([smalls, pair_row], 0)
    smalls = jnp.pad(smalls, ((0, 24 - smalls.shape[0]), (0, 0)))
    pool_pad = pool_w
    blocks = [smalls]
    for layer in range(layers):
        blocks += [block_a[layer], w_in[layer], w_back[layer]]
    blocks.append(pool_pad)
    full, halo = gather_all(blocks, tokens_in)

    small_full = full[0].reshape(4, NZ * NY, 24, 128)
    wide = small_full[0, :, :, :rows]
    n_b = layers
    n_s = n_b + layers * 6
    n_g = n_s + layers * 2
    bias_up_all = small_full[:, :, :n_b, :rows].transpose(2, 0, 1, 3).reshape(layers, -1)
    shifts_all = wide[:, n_b:n_s].transpose(1, 0, 2).reshape(layers, 6, width)
    scales_all = wide[:, n_s:n_g].transpose(1, 0, 2).reshape(layers, 2, width)
    pool_shift = wide[:, n_g].reshape(width)
    pair_all = small_full[0, :, n_g + 1, : pairing.shape[0]].reshape(-1).astype(jnp.int32)
    pool_full = full[-1][0, 0].reshape(width, width)

    weights = []
    for layer in range(layers):
        a, i, b = full[1 + 3 * layer : 4 + 3 * layer]
        a = a.reshape(4, NZ * NY * rows, 3, part + spare)
        qkv = a[..., :part].transpose(2, 1, 0, 3).reshape(3, width, width)
        proj = a[..., part:].reshape(width, width)
        up = i.reshape(4, width, -1).transpose(1, 0, 2).reshape(width, -1)
        down = b.reshape(-1, width)
        weights.append((qkv[0], qkv[1], qkv[2], proj, up, down, bias_up_all[layer],
                        shifts_all[layer], scales_all[layer]))

    labels = jnp.pad(segments[0], (HALO, HALO), constant_values=-1)
    around = lax.dynamic_slice_in_dim(labels, m * local_rows, local_rows + 2 * HALO, 0)
    mine = around[HALO : HALO + local_rows]
    same_doc = mine[:, None] == around[None, :]
    halo = jnp.stack([jnp.where(m > 0, halo[0], 0), jnp.where(m < 3, halo[1], 0)])
    keep = drop_masks.astype(F32)

    residual = tokens_in.astype(F32)
    saved_all = []
    for layer in range(layers):
        if layer:
            low = residual.astype(BF)
            halo = swap_halos(low[:HALO], low[local_rows - HALO :], 2 + layer)
        residual, saved = layer_forward(residual, halo, weights[layer], keep[layer], same_doc)
        saved_all.append(saved)

    numbers = jnp.arange(SEGS, dtype=jnp.int32)
    starts = jnp.sum((segments[0][None, :] < numbers[:, None]).astype(jnp.int32), 1)
    here = starts[:, None] == (m * local_rows + jnp.arange(local_rows, dtype=jnp.int32))[None, :]
    pick = here.astype(BF)
    shared = share_pooled(mm(pick, residual.astype(BF)).astype(BF))
    cls = shared.reshape(NZ * NY, SEGS, width)
    if inner > 1:
        cls = lax.all_gather(cls, "g", axis=1, tiled=True)
    cls = cls.reshape(-1, width)
    count = cls.shape[0]
    pooled = jnp.tanh(mm(cls, pool_full) + pool_shift)
    normed_pool, unit_back = jax.vjp(unit_rows, pooled)
    unit = normed_pool.astype(BF)
    gram = contract(unit, unit, 1, 1)
    logits = gram / TEMP
    ids = jnp.arange(count, dtype=jnp.int32)
    self_mask = ids[None, :] == ids[:, None]
    pair_mask = ids[None, :] == pair_all[:, None]
    masked = jnp.where(self_mask, -1000000000.0, logits)
    row_peak = jnp.max(masked, 1, keepdims=True)
    exponent = jnp.exp(masked - row_peak)
    totals = jnp.sum(exponent, 1, keepdims=True)
    loss_rows = row_peak[:, 0] + jnp.log(totals[:, 0]) - jnp.sum(jnp.where(pair_mask, logits, 0.0), 1)
    squares = jnp.sum(jnp.square(unit.astype(F32)), 1)
    distance = squares[:, None] + squares[None, :] - 2.0 * gram
    align_rows = jnp.sum(jnp.where(pair_mask, distance, 0.0), 1)
    unif_rows = jnp.log(jnp.sum(jnp.where(self_mask, 0.0, jnp.exp(-2.0 * distance)), 1) / (count - 1))
    grad_raw = ((exponent / totals - pair_mask.astype(F32)) / TEMP).astype(BF)
    grad_unit = contract(grad_raw, unit, 1, 0) + contract(grad_raw, unit, 0, 0)
    grad_pooled = unit_back(grad_unit)[0]
    grad_before = (grad_pooled * (1.0 - pooled * pooled)).astype(BF)
    grad_pool_b = jnp.sum(grad_before.astype(F32), 0)
    rows_pool = width // (NZ * NY * inner)
    cls_cols = lax.dynamic_slice_in_dim(cls, dp * rows_pool, rows_pool, 1)
    grad_pool_w = contract(cls_cols, grad_before, 0, 0)
    grad_pool_b = lax.dynamic_slice_in_dim(grad_pool_b, dp * rows_pool, rows_pool, 0)
    own_before = lax.dynamic_slice_in_dim(grad_before, dp * SEGS, SEGS, 0)
    grad_cls = contract(own_before, pool_full, 1, 1)
    grad_resid = lax.dot_general(
        here.astype(F32), grad_cls, (((0,), (0,)), ((), ())),
        precision=lax.Precision.HIGHEST, preferred_element_type=F32)

    def own_rows(values):
        return lax.dynamic_slice_in_dim(values, dp * SEGS, SEGS, 0)

    grads = [None] * layers
    for layer in reversed(range(layers)):
        grad_resid, grads[layer] = layer_backward(
            grad_resid, weights[layer], keep[layer], saved_all[layer], same_doc, 5 + layer)

    outs_blocks = []
    for layer in reversed(range(layers)):
        g_q, g_k, g_v, g_proj, g_up, g_down = grads[layer][:6]
        qkv = jnp.stack([g_q, g_k, g_v]).reshape(3, width, 4, part).transpose(2, 1, 0, 3)
        proj = g_proj.reshape(4, NZ * NY * rows, 3, spare)
        a = jnp.concatenate([qkv, proj], 3).reshape(2, 2, NZ, NY, rows, -1)
        i = g_up.reshape(width, 4, -1).transpose(1, 0, 2).reshape(2, 2, NZ, NY, rows, -1)
        b = g_down.reshape(2, 2, NZ, NY, -1, width)
        outs_blocks += [b, i, a]
    g_bias = jnp.stack([grads[layer][6] for layer in range(layers)])
    g_shift = jnp.stack([grads[layer][7] for layer in range(layers)])
    g_scale = jnp.stack([grads[layer][8] for layer in range(layers)])
    thin = rows // (4 * inner)

    def sliced(values):
        k = values.shape[1]
        values = values.reshape(layers, k, NZ * NY, inner, 4, thin)
        return values.transpose(4, 2, 0, 1, 3, 5).reshape(4, NZ * NY, -1)

    g_small = jnp.concatenate([
        g_bias.reshape(layers, 4, NZ * NY, rows).transpose(1, 2, 0, 3).reshape(4, NZ * NY, -1),
        sliced(g_shift), sliced(g_scale)], 2)
    n_small = g_small.shape[2]
    g_small = jnp.pad(g_small, ((0, 0), (0, 0), (0, 16 * 128 - n_small)))
    outs_blocks.append(g_small.reshape(2, 2, NZ, NY, 16, 128))
    summed = reduce_all(outs_blocks)

    def spread(values, dim):
        return values if inner == 1 else lax.psum_scatter(values, "g", scatter_dimension=dim, tiled=True)

    out_qkv, out_proj, out_up, out_down = [], [], [], []
    for layer in range(layers):
        at = 3 * (layers - 1 - layer)
        b, i, a = summed[at : at + 3]
        a = a.reshape(rows, 3, part + spare)
        out_qkv.append(spread(jnp.moveaxis(a[..., :part], 1, 0), 1))
        out_proj.append(spread(a[..., part:].reshape(rows_out, width), 0))
        out_up.append(spread(i, 0))
        out_down.append(spread(b, 0))
    flat = summed[-1].reshape(-1)
    e1 = layers * rows
    e2 = e1 + layers * 6 * inner * thin
    e3 = e2 + layers * 2 * inner * thin
    out_b_in = spread(flat[:e1].reshape(layers, rows), 1)
    out_biases = spread(flat[e1:e2].reshape(layers, 6, inner * thin), 2)
    out_gains = spread(flat[e2:e3].reshape(layers, 2, inner * thin), 2)
    return (
        own_rows(loss_rows),
        own_rows(align_rows),
        own_rows(unif_rows),
        grad_resid,
        jnp.stack(out_qkv),
        jnp.stack(out_proj),
        jnp.stack(out_up),
        jnp.stack(out_down),
        out_b_in,
        out_biases,
        out_gains,
        grad_pool_w,
        grad_pool_b,
    )


def solution(mesh):
    count = mesh.shape["dp"]
    fine = Mesh(
        mesh.devices.reshape(NZ, NY, count // (NZ * NY), 2, 2), ("z", "y", "g", "x", "c")
    )
    dp, mp = ("z", "y", "g"), ("x", "c")
    in_specs = (
        P(dp + mp, None),
        P(dp, None),
        P(dp),
        P(None, None, dp + mp, None),
        P(None, None, dp, mp),
        P(None, mp + dp, None),
        P(None, dp, mp),
        P(None, mp + dp, None),
        P(None, mp + dp),
        P(None, None, dp),
        P(None, None, dp),
        P(dp, None),
        P(dp),
    )
    out_specs = (
        P(dp),
        P(dp),
        P(dp),
        P(dp + mp, None),
        P(None, None, dp, mp),
        P(None, mp + dp, None),
        P(None, dp, mp),
        P(None, mp + dp, None),
        P(None, mp + dp),
        P(None, None, dp + mp),
        P(None, None, dp + mp),
        P(dp, None),
        P(dp),
    )
    return jax.shard_map(
        per_device, mesh=fine, in_specs=in_specs, out_specs=out_specs, check_vma=False
    )
```

```python
import jax
import jax.numpy as jnp
from jax import lax
from jax.experimental import pallas as pl
from jax.experimental.pallas import tpu as pltpu
from jax.sharding import Mesh
from jax.sharding import PartitionSpec as P

HEAD_DIM = 64
SEGS = 16
TEMP = 0.05
EPS = 1e-06
KEEP = 0.9
MESH = pl.DeviceIdType.MESH
ANY = pl.BlockSpec(memory_space=pl.ANY)
VMEM = pl.BlockSpec(memory_space=pltpu.VMEM)
BF = jnp.bfloat16
F32 = jnp.float32
NZ = 4
NY = 2


class Names:
    def __init__(self, names, refs):
        for name, ref in zip(names, refs, strict=True):
            setattr(self, name, ref)


def contract(left_side, right_side, left_dim, right_dim):
    return lax.dot_general(
        left_side,
        right_side,
        (((left_dim,), (right_dim,)), ((), ())),
        preferred_element_type=F32,
    )


def mm(a, b):
    return jnp.dot(a, b, preferred_element_type=F32)


def position():
    return tuple(lax.axis_index(name) for name in ("z", "y", "x", "c"))


def signal(sem, device):
    pl.semaphore_signal(sem, inc=1, device_id=device, device_id_type=MESH)


def remote(src, dst, send_sem, recv_sem, device):
    return pltpu.make_async_remote_copy(
        src_ref=src,
        dst_ref=dst,
        send_sem=send_sem,
        recv_sem=recv_sem,
        device_id=device,
        device_id_type=MESH,
    )


def landed(ref, sem):
    pltpu.make_async_copy(ref, ref, sem).wait()


def rows_at(start, count):
    return pl.ds(pl.multiple_of(start, 128), count)


def flat(ref):
    value = ref[...]
    return value.reshape(-1, value.shape[-1])


SMALL, QKV, PROJ, UP0, DOWN0, UP1, DOWN1 = range(7)
BLOCKS = ("small", "qkv", "proj", "up0", "down0", "up1", "down1")
SAVED = ("xw", "q", "k", "v", "p", "att", "zf", "gp", "act", "yh1", "yh2", "r1", "r2")
FWD_IN = BLOCKS + ("pool", "tok", "seg", "drop")
FWD_OUT = tuple("o_" + n for n in BLOCKS[1:]) + ("o_pool", "o_piece", "o_vec", "o_cls") + tuple("o_" + n for n in SAVED)
FWD_SCR = (
    tuple("w_" + n for n in BLOCKS) + ("w_pool", "cls_part", "cls_all") + SAVED
    + ("keep", "bias", "wo", "vec", "qv", "h", "z", "sa", "ra", "sf", "rf")
    + ("zsend", "xsend", "ysend", "recv", "own_sem", "pool_send", "pool_recv", "pool_own", "pool_core",
       "core_send", "core_recv", "halo_send", "halo_recv", "drop_sem", "out_sem", "w_sem", "misc_sem",
       "s1", "r1s", "s2", "r2s")
)


def forward_kernel(*refs):
    R = Names(FWD_IN + FWD_OUT + FWD_SCR, refs)
    z, y, x, c = position()
    up, down = z < NZ - 1, z > 0
    xdev, ydev, cdev, xcdev = {"x": 1 - x}, {"y": 1 - y}, {"c": 1 - c}, {"x": 1 - x, "c": 1 - c}
    half = R.tok.shape[0]
    ins = [getattr(R, n) for n in BLOCKS]
    lands = [getattr(R, "w_" + n) for n in BLOCKS]

    peers = [(k * NY + flip, k, flip) for k in range(NZ) for flip in range(NY) if k or flip]

    def peer(k, flip):
        return {"z": lax.rem(z + k, NZ), "y": y if flip == 0 else 1 - y}

    bar = pltpu.get_barrier_semaphore()
    for dev in (xdev, cdev, xcdev):
        signal(bar, dev)
    for _, k, flip in peers:
        signal(bar, peer(k, flip))
    pl.semaphore_wait(bar, 3 + len(peers))


    def copy(b, src, slot, device, sem):
        return remote(src, lands[b].at[slot], sem, R.recv.at[(b, *slot)], device)

    def arrived(b, slot):
        landed(lands[b].at[slot], R.recv.at[(b, *slot)])

    def x_first(b):
        return b % 2 == 0

    def sideways(b, src, slot, k):
        copy(b, src, slot, xdev, R.xsend.at[b, k]).start()
        copy(b, src, slot, ydev, R.ysend.at[b, k]).start()

    def launch(b):
        src, mine = ins[b], (x, z, y)
        pl.when(up)(lambda: copy(b, src, mine, {"z": z + 1}, R.zsend.at[b, 0]).start())
        pl.when(down)(lambda: copy(b, src, mine, {"z": z - 1}, R.zsend.at[b, 1]).start())
        sideways(b, src, mine, 0)
        pltpu.make_async_copy(src, lands[b].at[mine], R.own_sem.at[b]).start()

    def z_relay(b):
        for d in range(1, NZ):

            @pl.when(z >= d)
            def _():
                slot = (x, z - d, y)
                arrived(b, slot)
                pl.when(up)(lambda: copy(b, lands[b].at[slot], slot, {"z": z + 1}, R.zsend.at[b, 2 * d]).start())
                sideways(b, lands[b].at[slot], slot, NZ - d)

            @pl.when(z < NZ - d)
            def _():
                slot = (x, z + d, y)
                arrived(b, slot)
                pl.when(down)(lambda: copy(b, lands[b].at[slot], slot, {"z": z - 1}, R.zsend.at[b, 2 * d + 1]).start())
                sideways(b, lands[b].at[slot], slot, d)

    def xy_relay(b):
        for k in range(NZ):
            zp = lax.rem(z + k, NZ)
            sx, sy = (1 - x, zp, y), (x, zp, 1 - y)
            if x_first(b):
                arrived(b, sx)
                copy(b, lands[b].at[sx], sx, ydev, R.ysend.at[b, NZ + k]).start()
            else:
                arrived(b, sy)
                copy(b, lands[b].at[sy], sy, xdev, R.xsend.at[b, NZ + k]).start()

    def complete(b):
        for k in range(NZ):
            zp = lax.rem(z + k, NZ)
            arrived(b, (x, zp, 1 - y) if x_first(b) else (1 - x, zp, y))
            arrived(b, (1 - x, zp, 1 - y))
        pltpu.make_async_copy(ins[b], lands[b].at[x, z, y], R.own_sem.at[b]).wait()

    def sends_done(b):
        src, mine = ins[b], (x, z, y)
        for k in range(NZ):
            copy(b, src, mine, xdev, R.xsend.at[b, k]).wait_send()
            copy(b, src, mine, ydev, R.ysend.at[b, k]).wait_send()
            if x_first(b):
                copy(b, src, mine, ydev, R.ysend.at[b, NZ + k]).wait_send()
            else:
                copy(b, src, mine, xdev, R.xsend.at[b, NZ + k]).wait_send()
        for d in range(NZ):
            pl.when(up & (z >= d))(lambda: copy(b, src, mine, {"z": z + 1}, R.zsend.at[b, 2 * d]).wait_send())
            pl.when(down & (z < NZ - d))(lambda: copy(b, src, mine, {"z": z - 1}, R.zsend.at[b, 2 * d + 1]).wait_send())

    prow = R.pool.shape[0] // 2
    pool_rows = pl.ds(pl.multiple_of(c * prow, 16), prow)

    def pool_slot(zp, yp):
        return R.w_pool.at[zp, yp, pool_rows]

    def pool_copy(src, zp, yp, device, k):
        return remote(src, pool_slot(zp, yp), R.pool_send.at[k], R.pool_recv.at[zp, yp], device)

    def pool_launch():
        src = R.pool.at[pool_rows]
        pl.when(up)(lambda: pool_copy(src, z, y, {"z": z + 1}, 0).start())
        pl.when(down)(lambda: pool_copy(src, z, y, {"z": z - 1}, 1).start())
        pool_copy(src, z, y, ydev, 2 * NZ).start()
        pltpu.make_async_copy(src, pool_slot(z, y), R.pool_own).start()

    def pool_relay():
        for d in range(1, NZ):

            @pl.when(z >= d)
            def _():
                here = pool_slot(z - d, y)
                landed(here, R.pool_recv.at[z - d, y])
                pl.when(up)(lambda: pool_copy(here, z - d, y, {"z": z + 1}, 2 * d).start())
                pool_copy(here, z - d, y, ydev, 2 * NZ + NZ - d).start()

            @pl.when(z < NZ - d)
            def _():
                here = pool_slot(z + d, y)
                landed(here, R.pool_recv.at[z + d, y])
                pl.when(down)(lambda: pool_copy(here, z + d, y, {"z": z - 1}, 2 * d + 1).start())
                pool_copy(here, z + d, y, ydev, 2 * NZ + d).start()

    def pool_core():
        halves = R.w_pool.at[:, :, pool_rows]
        return remote(halves, halves, R.pool_core.at[0], R.pool_core.at[1], cdev)

    def pool_swap():
        pltpu.make_async_copy(R.pool.at[pool_rows], pool_slot(z, y), R.pool_own).wait()
        for k in range(NZ):
            zp = lax.rem(z + k, NZ)
            landed(pool_slot(zp, 1 - y), R.pool_recv.at[zp, 1 - y])
        pool_core().start()

    def pool_done():
        there = R.w_pool.at[:, :, pl.ds(pl.multiple_of((1 - c) * prow, 16), prow)]
        landed(there, R.pool_core.at[1])
        pool_core().wait_send()
        src = R.pool.at[pool_rows]
        for d in range(NZ):
            pl.when(up & (z >= d))(lambda: pool_copy(src, z, y, {"z": z + 1}, 2 * d).wait_send())
            pl.when(down & (z < NZ - d))(lambda: pool_copy(src, z, y, {"z": z - 1}, 2 * d + 1).wait_send())
            pool_copy(src, z, y, ydev, 2 * NZ + d).wait_send()


    def win(core):
        return rows_at(x * 128 + core * half, half)

    def chip(core):
        return rows_at(core * half, half)

    def swap(src, dst, n):
        return remote(src, dst, R.core_send.at[n], R.core_recv.at[n], cdev)

    def rows_swap(layer):
        here = R.xw.at[layer, win(c)]
        return swap(here, here, 4 * layer)

    def edge_copies(layer):
        src = R.xw.at[layer, rows_at(x * 128 + c * half + 128 * c, 128)]
        dst = R.xw.at[layer, rows_at(x * 512, 128)]
        return [
            remote(src, dst, R.halo_send.at[layer, i], R.halo_recv.at[layer], dev)
            for i, dev in enumerate(({"x": 1 - x, "c": c}, {"x": 1 - x, "c": 1 - c}))
        ]

    def send_rows(layer):
        rows_swap(layer).start()

        @pl.when(c == 1 - x)
        def _():
            for cp in edge_copies(layer):
                cp.start()

    def partner_rows_here(layer):
        landed(R.xw.at[layer, win(1 - c)], R.core_recv.at[4 * layer])

    def edge_here(layer):
        landed(R.xw.at[layer, rows_at((1 - x) * 512, 128)], R.halo_recv.at[layer])


    def vec(layer, k):
        return R.vec[0, 2 + 6 * layer + k : 3 + 6 * layer + k, :]

    def gain(layer, k):
        return R.vec[0, 14 + 2 * layer + k : 15 + 2 * layer + k, :]

    def spread_params():
        width = R.vec.shape[2]
        part = width // (NZ * NY)
        lane = lax.broadcasted_iota(jnp.int32, (128, width), 0)
        col = lax.broadcasted_iota(jnp.int32, (128, width), 1)
        for j in range(2):
            total = jnp.zeros((R.vec.shape[1], width), F32)
            for dp in range(NZ * NY):
                place = ((lane < part) & (col == lane + dp * part)).astype(F32).astype(BF)
                total = total + mm(R.w_small[j, dp // NY, dp % NY], place)
            R.vec[j] = total
        head = R.qv.shape[2]
        lane = lax.broadcasted_iota(jnp.int32, (width, head), 0)
        col = lax.broadcasted_iota(jnp.int32, (width, head), 1)
        low = R.vec[0].astype(BF)
        for j in range(2):
            place = (lane == col + (2 * j + c) * head).astype(F32).astype(BF)
            R.qv[j] = mm(low, place)

    def masks():
        for i in range(4):
            mine = R.seg[0:1, rows_at(x * 512 + i * 128, 128)]
            start = (3 * (x + i) + 1) // 5 * 128
            keys = R.seg[0:1, rows_at(x * 384 + start, 384)]
            column = jnp.transpose(jnp.broadcast_to(mine, (128, 128)))
            for t in range(3):
                same = column == jnp.broadcast_to(keys[:, t * 128 : t * 128 + 128], (128, 128))
                R.bias[i, :, t * 128 : t * 128 + 128] = jnp.where(same, 0.0, -1000000000.0)

    def proj_rows():
        for layer in range(2):
            for j in range(2):
                value = R.w_proj[j].astype(F32)
                rows = value.shape[2] // 2
                value = value[:, :, layer * rows : (layer + 1) * rows].reshape(-1, value.shape[3])
                R.wo[layer, j] = value.astype(BF)

    def project(layer, wrow, count, crow):
        xx = R.xw[layer, wrow]
        head = R.q.shape[3]
        for j in range(2):
            w = R.w_qkv.at[j]
            wqk = w[:, :, :, layer * 2 * head : (layer + 1) * 2 * head].reshape(-1, 2 * head)
            yqk = mm(xx, wqk)
            if crow is not None:
                bq = R.qv[j, 2 + 6 * layer : 3 + 6 * layer, :]
                R.q[layer, j, crow] = (yqk[:, :head] + bq).astype(BF) * jnp.asarray(0.125, BF)
            R.k[layer, j, wrow] = yqk[:, head:].astype(BF)
            bv = R.qv[j, 3 + 6 * layer : 4 + 6 * layer, :]
            if layer == 0:
                yv = mm(xx, w[:, :, :, 4 * head : 5 * head].reshape(-1, head))
            else:
                yv = mm(xx, w[:, :, :, 5 * head - 64 : 6 * head].reshape(-1, head + 64))[:, 64:]
            R.v[layer, j, wrow] = (yv + bv).astype(BF)

    def attend(layer):
        head = R.q.shape[3]
        lane = lax.broadcasted_iota(jnp.int32, (1, head), 1) // HEAD_DIM
        picks = [(lane == n).astype(F32) for n in range(head // HEAD_DIM)]
        count = len(picks)
        for j in range(2):

            @pl.loop(0, 4)
            def _(i):
                keys = rows_at((3 * (x + i) + 1) // 5 * 128, 384)
                mine = rows_at(i * 128, 128)
                qq = R.q[layer, j, mine]
                q3 = jnp.concatenate([qq * pick.astype(BF) for pick in picks], 0)
                scores = contract(q3, R.k[layer, j, keys], 1, 1)
                bias = R.bias[i]
                scores = scores.reshape(count, 128, 384) + bias[None]
                peak = jnp.max(scores, -1, keepdims=True)
                e = jnp.exp(scores - peak)
                p = (e * (1.0 / jnp.sum(e, -1, keepdims=True))).astype(BF).reshape(count * 128, 384)
                R.p[layer, j, i] = p
                o = mm(p, R.v[layer, j, keys])
                total = o[0:128] * picks[0]
                for n in range(1, count):
                    total = total + o[n * 128 : (n + 1) * 128] * picks[n]
                R.att[layer, j, mine] = total.astype(BF)

    def proj_part(layer, rows):
        return mm(R.att[layer, 0, rows], R.wo[layer, 0]) + mm(R.att[layer, 1, rows], R.wo[layer, 1])

    def norm(value, g, s):
        center = jnp.mean(value, 1, keepdims=True)
        spread = lax.rsqrt(jnp.mean(value * value, 1, keepdims=True) - center * center + EPS)
        hat = (value - center) * spread
        return hat * g + s, hat, spread

    def attention_out(layer):
        R.sa[layer] = proj_part(layer, chip(1 - c)).astype(BF)
        cp = swap(R.sa.at[layer], R.ra.at[layer], 4 * layer + 1)
        cp.start()
        a = proj_part(layer, chip(c))
        cp.wait_recv()
        a = a + R.ra[layer].astype(F32) + vec(layer, 2)
        out, hat, spread = norm(R.h[...] + R.keep[layer, 0].astype(F32) * a * (1.0 / KEEP), gain(layer, 0), vec(layer, 3))
        R.z[...] = out
        R.yh1[layer] = hat.astype(BF)
        R.r1[layer] = spread
        R.zf[layer, chip(c)] = out.astype(BF)
        here = R.zf.at[layer, chip(c)]
        swap(here, here, 4 * layer + 2).start()

    def ffn_up(layer, core):
        if core is None:
            landed(R.zf.at[layer, chip(1 - c)], R.core_recv.at[4 * layer + 2])
            rows = chip(1 - c)
        else:
            rows = chip(c)
        w = R.w_up0 if layer == 0 else R.w_up1
        zz = R.zf[layer, rows]
        for j in range(2):
            hid = mm(zz, flat(w.at[j])) + R.vec[j, layer : layer + 1, :]
            cdf = 0.5 + 0.5 * lax.erf(hid * 0.7071067811865476)
            R.act[layer, j, rows] = (hid * cdf).astype(BF)
            R.gp[layer, j, rows] = (cdf + hid * jnp.exp(-0.5 * hid * hid) * 0.3989422804014327).astype(BF)

    def ffn_part(layer, rows):
        w = R.w_down0 if layer == 0 else R.w_down1
        return mm(R.act[layer, 0, rows], flat(w.at[0])) + mm(R.act[layer, 1, rows], flat(w.at[1]))

    def ffn_down(layer):
        R.sf[layer] = ffn_part(layer, chip(1 - c)).astype(BF)
        cp = swap(R.sf.at[layer], R.rf.at[layer], 4 * layer + 3)
        cp.start()
        f = ffn_part(layer, chip(c))
        cp.wait_recv()
        f = f + R.rf[layer].astype(F32) + vec(layer, 4)
        out, hat, spread = norm(R.z[...] + R.keep[layer, 1].astype(F32) * f * (1.0 / KEEP), gain(layer, 1), vec(layer, 5))
        R.h[...] = out
        R.yh2[layer] = hat.astype(BF)
        R.r2[layer] = spread
        if layer == 0:
            R.xw[1, win(c)] = out.astype(BF)
            send_rows(1)


    def out_copy(k, layer):
        name = SAVED[k]
        return pltpu.make_async_copy(getattr(R, name).at[layer], getattr(R, "o_" + name).at[layer], R.out_sem.at[k, layer])

    def save(layer, *names):
        for name in names:
            out_copy(SAVED.index(name), layer).start()

    def w_copy(b):
        return pltpu.make_async_copy(lands[b], getattr(R, "o_" + BLOCKS[b]), R.w_sem.at[b])

    def misc_copies():
        return [
            pltpu.make_async_copy(R.w_pool, R.o_pool, R.misc_sem.at[0]),
            pltpu.make_async_copy(R.w_small.at[0], R.o_piece, R.misc_sem.at[1]),
            pltpu.make_async_copy(R.vec, R.o_vec, R.misc_sem.at[2]),
        ]


    def pooled():
        total = R.seg.shape[1]
        number = lax.broadcasted_iota(jnp.int32, (SEGS, total), 0)
        before = (jnp.broadcast_to(R.seg[...], (SEGS, total)) < number).astype(F32)
        starts = jnp.sum(before, 1, keepdims=True).astype(jnp.int32)
        mine = lax.broadcasted_iota(jnp.int32, (SEGS, half), 1) + (2 * x + c) * half
        pick = (mine == starts).astype(F32).astype(BF)
        row = mm(pick, R.h[...].astype(BF))
        R.cls_part[0] = row.astype(BF)
        first = [
            remote(R.cls_part.at[0], R.cls_part.at[1 + i], R.s1.at[i], R.r1s.at[i], dev)
            for i, dev in enumerate((xdev, cdev, xcdev))
        ]
        for cp in first:
            cp.start()
        for i, cp in enumerate(first):
            cp.wait_recv()
            row = row + R.cls_part[1 + i].astype(F32)
        here = R.cls_all.at[z, y]
        here[...] = row.astype(BF)
        second = [remote(here, here, R.s2.at[i], R.r2s.at[i], peer(k, flip)) for i, k, flip in peers]
        for cp in second:
            cp.start()
        for i, k, flip in peers:
            landed(R.cls_all.at[lax.rem(z + NZ - k, NZ), y if flip == 0 else 1 - y], R.r2s.at[i])
        for cp in first + second:
            cp.wait_send()
        R.o_cls[...] = R.cls_all[...]


    R.xw[0, win(c)] = R.tok[...]
    send_rows(0)
    drop = pltpu.make_async_copy(R.drop, R.keep, R.drop_sem)
    drop.start()
    launch(SMALL)
    launch(QKV)
    launch(PROJ)
    launch(UP0)
    z_relay(SMALL)
    z_relay(QKV)
    masks()
    R.h[...] = R.tok[...].astype(F32)
    partner_rows_here(0)
    edge_here(0)
    save(0, "xw")
    z_relay(PROJ)
    launch(DOWN0)
    pool_launch()
    xy_relay(SMALL)
    xy_relay(QKV)
    complete(SMALL)
    spread_params()
    z_relay(UP0)
    xy_relay(PROJ)
    launch(UP1)
    launch(DOWN1)
    z_relay(DOWN0)
    pool_relay()
    complete(QKV)
    w_copy(QKV).start()
    for core in (c, 1 - c):
        project(0, win(core), half, chip(core))
    project(0, rows_at((1 - x) * 512, 128), 128, None)
    save(0, "q", "k", "v")
    xy_relay(UP0)
    attend(0)
    save(0, "p", "att")
    complete(PROJ)
    w_copy(PROJ).start()
    proj_rows()
    z_relay(UP1)
    xy_relay(DOWN0)
    drop.wait()
    attention_out(0)
    save(0, "yh1", "r1")
    complete(UP0)
    w_copy(UP0).start()
    ffn_up(0, c)
    ffn_up(0, None)
    save(0, "zf", "gp", "act")
    z_relay(DOWN1)
    xy_relay(UP1)
    complete(DOWN0)
    w_copy(DOWN0).start()
    ffn_down(0)
    save(0, "yh2", "r2")
    project(1, win(c), half, chip(c))
    partner_rows_here(1)
    project(1, win(1 - c), half, chip(1 - c))
    edge_here(1)
    save(1, "xw")
    project(1, rows_at((1 - x) * 512, 128), 128, None)
    save(1, "q", "k", "v")
    pool_swap()
    xy_relay(DOWN1)
    attend(1)
    save(1, "p", "att")
    attention_out(1)
    save(1, "yh1", "r1")
    pool_done()
    for cp in misc_copies():
        cp.start()
    complete(UP1)
    w_copy(UP1).start()
    ffn_up(1, c)
    ffn_up(1, None)
    save(1, "zf", "gp", "act")
    complete(DOWN1)
    w_copy(DOWN1).start()
    ffn_down(1)
    save(1, "yh2", "r2")
    pooled()

    for b in range(len(BLOCKS)):
        sends_done(b)
        if b != SMALL:
            w_copy(b).wait()
    for cp in misc_copies():
        cp.wait()
    for layer in range(2):
        for k in range(len(SAVED)):
            out_copy(k, layer).wait()
        rows_swap(layer).wait_send()
        swap(R.sa.at[layer], R.ra.at[layer], 4 * layer + 1).wait_send()
        swap(R.zf.at[layer, chip(c)], R.zf.at[layer, chip(c)], 4 * layer + 2).wait_send()
        swap(R.sf.at[layer], R.rf.at[layer], 4 * layer + 3).wait_send()

        @pl.when(c == 1 - x)
        def _():
            for cp in edge_copies(layer):
                cp.wait_send()


def loss_kernel(cls, pool, vec, piece, loss, align, unif, gw, gb, gcls, u, nb, rn, dn, dpre, table, gw_all):
    z, y = lax.axis_index("z"), lax.axis_index("y")
    inner = lax.axis_size("g")
    count, width = cls.shape
    per = SEGS * inner
    pre = mm(cls[...], pool[...].reshape(width, width)) + vec[0, 18:19, :]
    value = jnp.tanh(pre)
    u[...] = value
    scale = lax.rsqrt(jnp.sum(value * value, 1, keepdims=True) + EPS)
    rn[...] = scale
    nb[...] = (value * scale).astype(BF)
    low = nb[...].astype(F32)
    squares_row = lax.dot_general(
        jnp.ones((8, width), F32), low * low, (((1,), (1,)), ((), ())),
        precision=lax.Precision.HIGHEST, preferred_element_type=F32)[0:1]
    dn[...] = jnp.zeros_like(dn)

    @pl.loop(0, count // 128)
    def _(blk):
        rows = rows_at(blk * 128, 128)
        ids = lax.broadcasted_iota(jnp.int32, (128, 1), 0) + blk * 128
        cols = lax.broadcasted_iota(jnp.int32, (1, count), 1)
        pair = jnp.zeros((128, 1), F32)
        lane = lax.broadcasted_iota(jnp.int32, (1, 128), 1)
        for o in range(NZ * NY):
            got = piece[o // NY, o % NY]
            number = got[19:20].astype(F32) * 32.0 + got[20:21].astype(F32)
            here = (ids == o * per + lane) & (lane < per)
            pair = pair + jnp.sum(jnp.where(here, number, 0.0), 1, keepdims=True)
        mine = nb[rows]
        gram = contract(mine, nb[...], 1, 1)
        logits = gram * (1.0 / TEMP)
        own = cols == ids
        twin = cols == pair.astype(jnp.int32)
        masked = jnp.where(own, -1000000000.0, logits)
        peak = jnp.max(masked, 1, keepdims=True)
        e = jnp.exp(masked - peak)
        total = jnp.sum(e, 1, keepdims=True)
        low_mine = mine.astype(F32)
        squares = jnp.sum(low_mine * low_mine, 1, keepdims=True)
        distance = squares + squares_row - 2.0 * gram
        terms = (
            peak + jnp.log(total) - jnp.sum(jnp.where(twin, logits, 0.0), 1, keepdims=True),
            jnp.sum(jnp.where(twin, distance, 0.0), 1, keepdims=True),
            jnp.log(jnp.sum(jnp.where(own, 0.0, jnp.exp(-2.0 * distance)), 1, keepdims=True) * (1.0 / (count - 1))),
        )
        for t in range(3):
            table[t, rows] = jnp.broadcast_to(terms[t], (128, 128))
        dg = ((e * (1.0 / total) - jnp.where(twin, 1.0, 0.0)) * (1.0 / TEMP)).astype(BF)
        dn[rows] += mm(dg, nb[...])
        dn[...] += contract(dg, mine, 0, 0)

    grad = dn[...]
    value = u[...]
    unit = value * rn[...]
    du = rn[...] * (grad - unit * jnp.sum(grad * unit, 1, keepdims=True))
    dpre[...] = (du * (1.0 - value * value)).astype(BF)
    dp = (z * NY + y) * inner + lax.axis_index("g")
    mine = pl.ds(pl.multiple_of(dp * SEGS, SEGS), SEGS)
    gcls[...] = contract(dpre[mine], pool[...].reshape(width, width), 1, 1)
    gb[...] = jnp.sum(dpre[...].astype(F32), 0, keepdims=True)
    gw_all[...] = contract(cls[...], dpre[...], 0, 0)
    part = gw.shape[0]
    gw[...] = gw_all[pl.ds(pl.multiple_of((z * NY + y) * part, 8), part)]
    for t, ref in enumerate((loss, align, unif)):
        ref[...] = table[t, mine][:, 0:1]


def pooled_loss(cls, pool, vec, piece):
    count, width = cls.shape
    part = width // (NZ * NY)
    one = jax.ShapeDtypeStruct((SEGS, 1), F32)
    return pl.pallas_call(
        loss_kernel,
        out_shape=[
            one, one, one,
            jax.ShapeDtypeStruct((part, width), F32),
            jax.ShapeDtypeStruct((1, width), F32),
            jax.ShapeDtypeStruct((SEGS, width), F32),
        ],
        in_specs=[VMEM] * 4,
        out_specs=[VMEM] * 6,
        scratch_shapes=[
            pltpu.VMEM((count, width), F32),
            pltpu.VMEM((count, width), BF),
            pltpu.VMEM((count, 1), F32),
            pltpu.VMEM((count, width), F32),
            pltpu.VMEM((count, width), BF),
            pltpu.VMEM((3, count, 128), F32),
            pltpu.VMEM((width, width), F32),
        ],
        compiler_params=pltpu.CompilerParams(vmem_limit_bytes=48 << 20),
        name="pooled_loss",
    )(cls, pool, vec, piece)


GRADS = ("down1", "up1", "down0", "up0", "proj", "qkv")
BWD_IN = BLOCKS[1:] + SAVED + ("vec", "seg", "drop", "gcls")
BWD_OUT = ("gx", "o_down", "o_up", "o_proj", "o_qkv", "o_small")
BWD_SCR = (
    tuple("g_" + n for n in GRADS) + tuple("px_" + n for n in GRADS) + tuple("py_" + n for n in GRADS)
    + tuple("qx_" + n for n in GRADS) + tuple("qy_" + n for n in GRADS) + tuple("zr_" + n for n in GRADS)
    + ("st_ffn", "st_proj", "st_qkv") + tuple("v_" + n for n in SAVED)
    + ("w_qkv", "w_proj", "w_up", "w_down", "keep", "wo", "dff", "daf", "send", "rz", "rh",
       "hs", "hr", "datt", "dq", "dk", "dv", "dqk", "dvp", "dwo", "dh", "dy", "small", "small_in")
    + ("w_sem", "v_sem", "keep_sem", "out_sem", "csend", "crecv", "hsend", "hrecv",
       "s1", "r1s", "s2", "r2s", "zs", "zrs", "bs", "br", "gx_sem")
)


def backward_kernel(*refs):
    R = Names(BWD_IN + BWD_OUT + BWD_SCR, refs)
    z, y, x, c = position()
    up, down = z < NZ - 1, z > 0
    xdev, ydev, cdev = {"x": 1 - x}, {"y": 1 - y}, {"c": 1 - c}
    half = R.gx.shape[0]
    head = R.q.shape[3]
    width = R.gx.shape[1]
    nblk = len(GRADS)


    def v_copy(name, layer):
        k = SAVED.index(name)
        return pltpu.make_async_copy(getattr(R, name).at[layer], getattr(R, "v_" + name), R.v_sem.at[k])

    def load(layer, *names):
        for name in names:
            v_copy(name, layer).start()

    def need(layer, *names):
        for name in names:
            v_copy(name, layer).wait()

    def qkv_copies(layer):
        src, dst = R.qkv, R.w_qkv
        low = 4 * head if layer == 0 else 5 * head - 64
        return [
            pltpu.make_async_copy(src.at[:, :, :, :, layer * 2 * head : (layer + 1) * 2 * head],
                                  dst.at[:, :, :, :, 0 : 2 * head], R.w_sem.at[0]),
            pltpu.make_async_copy(src.at[:, :, :, :, low : low + head + 64],
                                  dst.at[:, :, :, :, 2 * head : 3 * head + 64], R.w_sem.at[1]),
        ]

    def up_copy(layer):
        return pltpu.make_async_copy(R.up0 if layer == 0 else R.up1, R.w_up, R.w_sem.at[2])

    def down_copy(layer):
        return pltpu.make_async_copy(R.down0 if layer == 0 else R.down1, R.w_down, R.w_sem.at[3])

    def proj_copy():
        return pltpu.make_async_copy(R.proj, R.w_proj, R.w_sem.at[4])

    def keep_copy(layer, k):
        return pltpu.make_async_copy(R.drop.at[layer, k], R.keep.at[k], R.keep_sem.at[k])

    load(1, "yh2", "r2")
    keep_copy(1, 1).start()
    load(1, "act")
    down_copy(1).start()
    load(1, "gp")
    up_copy(1).start()
    load(1, "zf", "yh1", "r1")
    keep_copy(1, 0).start()
    load(1, "att")
    proj_copy().start()
    load(1, "p", "q", "k", "v", "xw")
    for cp in qkv_copies(1):
        cp.start()

    zp1 = z + 1 - 2 * lax.rem(z, 2)
    zp2 = lax.rem(z + 2, NZ)
    bar = pltpu.get_barrier_semaphore()
    for dev in (xdev, ydev, cdev, {"x": 1 - x, "c": 1 - c}):
        signal(bar, dev)
    for k in range(1, NZ):
        signal(bar, {"z": lax.rem(z + k, NZ)})
    pl.semaphore_wait(bar, 4 + NZ - 1)


    def g(b):
        return getattr(R, "g_" + GRADS[b])

    def split(b):
        rows = g(b).shape[3]
        return rows // 32 * 16

    def first(b):
        h = split(b)
        return (
            remote(g(b).at[1 - x, :, :, 0:h], getattr(R, "px_" + GRADS[b]), R.s1.at[b, 0], R.r1s.at[b, 0], xdev),
            remote(g(b).at[:, :, 1 - y, h:], getattr(R, "py_" + GRADS[b]), R.s1.at[b, 1], R.r1s.at[b, 1], ydev),
        )

    def second(b):
        h = split(b)
        return (
            remote(g(b).at[x, :, 1 - y, 0:h], getattr(R, "qy_" + GRADS[b]), R.s2.at[b, 0], R.r2s.at[b, 0], ydev),
            remote(g(b).at[1 - x, :, y, h:], getattr(R, "qx_" + GRADS[b]), R.s2.at[b, 1], R.r2s.at[b, 1], xdev),
        )

    def add_into(ref, other):
        ref[...] = (ref[...].astype(F32) + other.astype(F32)).astype(BF)

    def stage1(b):
        for cp in first(b):
            cp.start()

    def stage2(b):
        h = split(b)
        px, py = getattr(R, "px_" + GRADS[b]), getattr(R, "py_" + GRADS[b])
        for cp in first(b):
            cp.wait_recv()

        @pl.loop(0, NZ)
        def _(k):
            for yy in range(NY):
                add_into(g(b).at[x, k, yy, 0:h], px[k, yy])
            for xx in range(2):
                add_into(g(b).at[xx, k, y, h:], py[xx, k])

        for cp in second(b):
            cp.start()

    def z_up(b, j):
        zr = getattr(R, "zr_" + GRADS[b])
        return remote(g(b).at[x, z + j, y], zr.at[z + j], R.zs.at[b, 0, j], R.zrs.at[b, z + j], {"z": z + 1})

    def z_down(b, j):
        zr = getattr(R, "zr_" + GRADS[b])
        slot = NZ if j == 1 else z - j
        return remote(g(b).at[x, z - j, y], zr.at[slot], R.zs.at[b, 1, j], R.zrs.at[b, slot], {"z": z - 1})

    def z_landed(b, slot):
        landed(getattr(R, "zr_" + GRADS[b]).at[slot], R.zrs.at[b, slot])

    def stage3(b):
        h = split(b)
        qx, qy = getattr(R, "qx_" + GRADS[b]), getattr(R, "qy_" + GRADS[b])
        for cp in second(b):
            cp.wait_recv()

        @pl.loop(0, NZ)
        def _(k):
            add_into(g(b).at[x, k, y, 0:h], qy[k])
            add_into(g(b).at[x, k, y, h:], qx[k])

    def hops(b, far):
        zr = getattr(R, "zr_" + GRADS[b])
        for j in range(NZ - 1, 0, -1):

            @pl.when((z + j < NZ) & (jnp.logical_not(down) if far else down))
            def _():
                if not far:
                    z_landed(b, z + j)
                    add_into(g(b).at[x, z + j, y], zr[z + j])
                z_up(b, j).start()

            @pl.when((z - j >= 0) & (jnp.logical_not(up) if far else up))
            def _():
                if not far:
                    z_landed(b, z - j)
                    add_into(g(b).at[x, z - j, y], zr[z - j])
                z_down(b, j).start()

    def stage_of(b):
        return getattr(R, "st_" + (GRADS[b] if b >= 4 else "ffn"))

    def out_copy(b):
        name = GRADS[b]
        dst = R.o_proj if name == "proj" else R.o_qkv if name == "qkv" else getattr(R, "o_" + name[:-1]).at[int(name[-1])]
        return pltpu.make_async_copy(stage_of(b), dst, R.out_sem.at[b])

    def stage4(b):
        zr = getattr(R, "zr_" + GRADS[b])
        out = stage_of(b)
        if 0 < b < 4:
            out_copy(b - 1).wait()
        out[...] = g(b)[x, z, y].astype(F32)

        @pl.when(down)
        def _():
            z_landed(b, z)
            out[...] += zr[z].astype(F32)

        @pl.when(up)
        def _():
            z_landed(b, NZ)
            out[...] += zr[NZ].astype(F32)

        out_copy(b).start()

    def sends_done(b):
        for cp in first(b) + second(b):
            cp.wait_send()
        for j in range(1, NZ):
            pl.when(z + j < NZ)(lambda: z_up(b, j).wait_send())
            pl.when(z - j >= 0)(lambda: z_down(b, j).wait_send())
        if b >= 3:
            out_copy(b).wait()


    def chip(core):
        return rows_at(core * half, half)

    def win(core):
        return rows_at(x * 128 + core * half, half)

    def swap(src, dst, n):
        return remote(src, dst, R.csend.at[n], R.crecv.at[n], cdev)

    def gain(layer, k):
        return R.vec[0, 14 + 2 * layer + k : 15 + 2 * layer + k, :]

    def note(row, value):
        R.small[row : row + 1, :] = value

    def norm_back(grad, g_row, hat, spread):
        scaled = grad * g_row
        first_mean = jnp.mean(scaled, 1, keepdims=True)
        second_mean = jnp.mean(scaled * hat, 1, keepdims=True)
        return spread * (scaled - first_mean - hat * second_mean)

    def ffn_norm(layer):
        need(layer, "yh2", "r2")
        keep_copy(layer, 1).wait()
        grad, hat = R.dh[...], R.v_yh2[...].astype(F32)
        note(12 + 2 * layer + 1, jnp.sum(grad * hat, 0, keepdims=True))
        note(6 * layer + 5, jnp.sum(grad, 0, keepdims=True))
        dy = norm_back(grad, gain(layer, 1), hat, R.v_r2[...])
        R.dy[...] = dy
        df = dy * R.keep[1].astype(F32) * (1.0 / KEEP)
        note(6 * layer + 4, jnp.sum(df, 0, keepdims=True))
        R.dff[chip(c)] = df.astype(BF)
        here = R.dff.at[chip(c)]
        swap(here, here, 4 * layer).start()
        if layer == 1:
            load(0, "yh2", "r2")
            keep_copy(0, 1).start()

    def as_block(value):
        return value.astype(BF).reshape(NZ, NY, -1, value.shape[1])

    def down_grad(layer):
        here = R.dff.at[chip(c)]
        swap(here, here, 4 * layer).wait_send()
        landed(R.dff.at[chip(1 - c)], R.crecv.at[4 * layer])
        need(layer, "act")
        for j in range(2):
            (R.g_down1 if layer else R.g_down0)[j] = as_block(contract(R.v_act[j], R.dff[...], 0, 0))
        if layer == 1:
            load(0, "act")

    def up_grad(layer):
        need(layer, "gp", "zf")
        down_copy(layer).wait()
        for j in range(2):
            total = jnp.zeros((1, width), F32)
            for core in range(2):
                rows = pl.ds(core * half, half)
                dact = contract(R.dff[rows], flat(R.w_down.at[j]), 1, 1)
                dhid = (dact * R.v_gp[j, rows].astype(F32)).astype(BF)
                R.v_gp[j, rows] = dhid
                total = total + jnp.sum(dhid.astype(F32), 0, keepdims=True)
            keep_row = jnp.where(c == 0, 1.0, 0.0)
            note(16 + 4 * layer + 2 * j, total * keep_row)
            note(16 + 4 * layer + 2 * j + 1, total * (1.0 - keep_row))
            (R.g_up1 if layer else R.g_up0)[j] = as_block(contract(R.v_zf[...], R.v_gp[j], 0, 0))
        if layer == 1:
            down_copy(0).start()
            load(0, "zf")

    def mid_part(rows):
        return contract(R.v_gp[0, rows], flat(R.w_up.at[0]), 1, 1) + contract(R.v_gp[1, rows], flat(R.w_up.at[1]), 1, 1)

    def mid_exchange(layer):
        up_copy(layer).wait()
        R.send[...] = mid_part(chip(1 - c)).astype(BF)
        cp = swap(R.send, R.rz, 4 * layer + 1)
        cp.start()
        R.dy[...] += mid_part(chip(c))
        need(layer, "yh1", "r1")
        keep_copy(layer, 0).wait()
        if layer == 1:
            up_copy(0).start()
            load(0, "gp")
        cp.wait()
        grad, hat = R.dy[...] + R.rz[...].astype(F32), R.v_yh1[...].astype(F32)
        note(12 + 2 * layer, jnp.sum(grad * hat, 0, keepdims=True))
        note(6 * layer + 3, jnp.sum(grad, 0, keepdims=True))
        dy = norm_back(grad, gain(layer, 0), hat, R.v_r1[...])
        R.dy[...] = dy
        da = dy * R.keep[0].astype(F32) * (1.0 / KEEP)
        note(6 * layer + 2, jnp.sum(da, 0, keepdims=True))
        R.daf[chip(c)] = da.astype(BF)
        here = R.daf.at[chip(c)]
        swap(here, here, 4 * layer + 2).start()
        if layer == 1:
            load(0, "yh1", "r1")
            keep_copy(0, 0).start()

    def proj_grad(layer):
        if layer == 1:
            proj_copy().wait()
        for j in range(2):
            value = R.w_proj[j].astype(F32)
            rows = value.shape[2] // 2
            value = value[:, :, layer * rows : (layer + 1) * rows].reshape(-1, value.shape[3])
            R.wo[j] = value.astype(BF)
        here = R.daf.at[chip(c)]
        swap(here, here, 4 * layer + 2).wait_send()
        landed(R.daf.at[chip(1 - c)], R.crecv.at[4 * layer + 2])
        need(layer, "att")
        for j in range(2):
            for core in range(2):
                rows = pl.ds(core * half, half)
                R.datt[j, rows] = contract(R.daf[rows], R.wo[j], 1, 1).astype(BF)
            grad = contract(R.v_att[j], R.daf[...], 0, 0)
            if layer == 1:
                R.dwo[j] = grad.astype(BF)
            else:
                both = [v.reshape(NZ * NY, -1, width) for v in (grad, R.dwo[j].astype(F32))]
                R.g_proj[j] = as_block(jnp.concatenate(both, 1).reshape(-1, width))
        if layer == 1:
            load(0, "att")

    def attend_back(layer):
        need(layer, "p", "q", "k", "v")
        lane = lax.broadcasted_iota(jnp.int32, (1, head), 1) // HEAD_DIM
        picks = [(lane == n).astype(F32) for n in range(head // HEAD_DIM)]
        count = len(picks)
        for j in range(2):
            R.dk[...] = jnp.zeros_like(R.dk)
            R.dv[...] = jnp.zeros_like(R.dv)
            R.dq[...] = jnp.zeros_like(R.dq)

            @pl.loop(0, 4)
            def _(i):
                keys = rows_at((3 * (x + i) + 1) // 5 * 128, 384)
                mine = rows_at(i * 128, 128)
                kk = R.v_k[j, keys]
                qq, dd = R.v_q[j, mine], R.datt[j, mine]
                q3 = jnp.concatenate([qq * pick.astype(BF) for pick in picks], 0)
                d3 = jnp.concatenate([dd * pick.astype(BF) for pick in picks], 0)
                p3 = R.v_p[j, i]
                dp = contract(d3, R.v_v[j, keys], 1, 1)
                pf = p3.astype(F32)
                ds = (pf * (dp - jnp.sum(pf * dp, 1, keepdims=True))).astype(BF)
                R.dv[keys] += contract(p3, d3, 0, 0)
                R.dk[keys] += contract(ds, q3, 0, 0)
                dq = mm(ds, kk)
                total = dq[0:128] * picks[0]
                for n in range(1, count):
                    total = total + dq[n * 128 : (n + 1) * 128] * picks[n]
                R.dq[rows_at(x * 128 + i * 128, 128)] = total * 0.125

            dq, dk, dv = R.dq[...].astype(BF), R.dk[...].astype(BF), R.dv[...].astype(BF)
            dq, dk, dv = dq.astype(F32), dk.astype(F32), dv.astype(F32)
            R.dqk[j] = jnp.concatenate([dq, dk], 1).astype(BF)
            gap = jnp.zeros((dv.shape[0], 64), F32)
            R.dvp[j] = jnp.concatenate([dv, gap] if layer == 0 else [gap, dv], 1).astype(BF)
            own = jnp.where(c == 0, 1.0, 0.0)
            for row, part in ((0, dq), (1, dv)):
                line = jnp.sum(part, 0, keepdims=True)
                pair = [line * own, line * (1.0 - own)]
                zero = jnp.zeros((1, 2 * head), F32)
                if j == 0:
                    note(6 * layer + row, jnp.concatenate(pair + [zero], 1))
                else:
                    R.small[6 * layer + row : 6 * layer + row + 1, :] += jnp.concatenate([zero] + pair, 1)
        if layer == 1:
            load(0, "p", "q", "k", "v")

    def qkv_grad(layer):
        need(layer, "xw")
        for j in range(2):
            R.g_qkv[j, :, :, :, layer * 2 * head : (layer + 1) * 2 * head] = as_block(contract(R.v_xw[...], R.dqk[j], 0, 0))
            gv = as_block(contract(R.v_xw[...], R.dvp[j], 0, 0))
            if layer == 1:
                R.g_qkv[j, :, :, :, 5 * head - 64 :] = gv
            else:
                R.g_qkv[j, :, :, :, 4 * head : 4 * head + 128] = gv[..., 0:128]
                R.g_qkv[j, :, :, :, 4 * head + 128 : 5 * head + 64] += gv[..., 128:]
        if layer == 1:
            load(0, "xw")

    def in_part(rows):
        total = None
        for j in range(2):
            w = R.w_qkv.at[j]
            wqk = w[:, :, :, 0 : 2 * head].reshape(width, 2 * head)
            wv = w[:, :, :, 2 * head :].reshape(width, head + 64)
            term = contract(R.dqk[j, rows], wqk, 1, 1) + contract(R.dvp[j, rows], wv, 1, 1)
            total = term if total is None else total + term
        return total

    def halo_copy(layer):
        return remote(R.hs, R.hr.at[layer, c], R.hsend.at[layer], R.hrecv.at[layer, c], {"x": 1 - x, "c": x})

    def in_exchange(layer):
        for cp in qkv_copies(layer):
            cp.wait()
        R.hs[...] = in_part(rows_at((1 - x) * 512, 128)).astype(BF)
        halo_copy(layer).start()
        R.send[...] = in_part(win(1 - c)).astype(BF)
        cp = swap(R.send, R.rh, 4 * layer + 3)
        cp.start()
        R.dh[...] = R.dy[...] + in_part(win(c))
        if layer == 1:
            for again in qkv_copies(0):
                again.start()
        cp.wait()
        R.dh[...] += R.rh[...].astype(F32)

        @pl.when(c == 1 - x)
        def _():
            edge = rows_at(128 * c, 128)
            for core in range(2):
                landed(R.hr.at[layer, core], R.hrecv.at[layer, core])
                R.dh[edge] += R.hr[layer, core].astype(F32)

        halo_copy(layer).wait_send()


    def small_copy(k):
        dev = (cdev, xdev, ydev, {"z": zp1}, {"z": zp2})[k]
        return remote(R.small, R.small_in.at[k], R.bs.at[k], R.br.at[k], dev)

    def small_sum(k):
        small_copy(k).wait()
        R.small[...] += R.small_in[k]


    total = R.seg.shape[1]
    number = lax.broadcasted_iota(jnp.int32, (SEGS, total), 0)
    before = (jnp.broadcast_to(R.seg[...], (SEGS, total)) < number).astype(F32)
    starts = jnp.sum(before, 1, keepdims=True).astype(jnp.int32)
    mine = lax.broadcasted_iota(jnp.int32, (SEGS, half), 1) + (2 * x + c) * half
    pick = (mine == starts).astype(F32)
    R.dh[...] = lax.dot_general(
        pick, R.gcls[...], (((0,), (0,)), ((), ())), precision=lax.Precision.HIGHEST, preferred_element_type=F32)

    ffn_norm(1)
    down_grad(1)
    stage1(0)
    up_grad(1)
    stage1(1)
    mid_exchange(1)
    proj_grad(1)
    attend_back(1)
    stage2(0)
    qkv_grad(1)
    in_exchange(1)
    ffn_norm(0)
    down_grad(0)
    stage1(2)
    stage2(1)
    up_grad(0)
    stage1(3)
    stage3(0)
    hops(0, True)
    mid_exchange(0)
    proj_grad(0)
    stage1(4)
    attend_back(0)
    qkv_grad(0)
    stage1(5)
    hops(0, False)
    stage3(1)
    hops(1, True)
    stage2(2)
    in_exchange(0)
    gx_copy = pltpu.make_async_copy(R.dh, R.gx, R.gx_sem)
    gx_copy.start()
    small_copy(0).start()
    hops(1, False)
    stage4(0)
    small_sum(0)
    small_copy(1).start()
    stage2(3)
    stage3(2)
    hops(2, True)
    small_sum(1)
    small_copy(2).start()
    stage4(1)
    hops(2, False)
    stage2(4)
    stage3(3)
    hops(3, True)
    small_sum(2)
    small_copy(3).start()
    stage4(2)
    hops(3, False)
    stage2(5)
    stage3(4)
    hops(4, True)
    small_sum(3)
    small_copy(4).start()
    stage4(3)
    hops(4, False)
    stage3(5)
    hops(5, True)
    small_sum(4)
    R.o_small[...] = R.small[...]
    stage4(4)
    hops(5, False)
    stage4(5)
    gx_copy.wait()
    for b in range(nblk):
        sends_done(b)


def saved_shapes(half, width):
    head = width // 4
    return {
        "xw": ((640, width), BF),
        "q": ((2, 512, head), BF),
        "k": ((2, 640, head), BF),
        "v": ((2, 640, head), BF),
        "p": ((2, 4, 384, 384), BF),
        "att": ((2, 512, head), BF),
        "zf": ((512, width), BF),
        "gp": ((2, 512, width), BF),
        "act": ((2, 512, width), BF),
        "yh1": ((half, width), BF),
        "yh2": ((half, width), BF),
        "r1": ((half, 1), F32),
        "r2": ((half, 1), F32),
    }


def run_forward(blocks, pool, tok, seg, drop):
    half, width = tok.shape
    saved = saved_shapes(half, width)
    head = width // 4
    dma = pltpu.SemaphoreType.DMA
    land = [(2, NZ, NY, *b.shape) for b in blocks]
    nb = len(blocks)
    shape = jax.ShapeDtypeStruct
    outs = [shape(s, BF) for s in land[1:]]
    outs += [
        shape((NZ, NY, *pool.shape), BF),
        shape((NZ, NY, *blocks[0].shape), BF),
        shape((2, 32, width), F32),
        shape((NZ, NY, SEGS, width), BF),
    ]
    outs += [shape((2, *s), t) for s, t in saved.values()]
    out_specs = [VMEM if n == "o_cls" else ANY for n in FWD_OUT]
    scratch = [pltpu.VMEM(s, BF) for s in land]
    scratch += [
        pltpu.VMEM((NZ, NY, *pool.shape), BF),
        pltpu.VMEM((4, SEGS, width), BF),
        pltpu.VMEM((NZ, NY, SEGS, width), BF),
    ]
    scratch += [pltpu.VMEM((2, *s), t) for s, t in saved.values()]
    scratch += [
        pltpu.VMEM(drop.shape, drop.dtype),
        pltpu.VMEM((4, 128, 384), F32),
        pltpu.VMEM((2, 2, head, width), BF),
        pltpu.VMEM((2, 32, width), F32),
        pltpu.VMEM((2, 32, head), F32),
        pltpu.VMEM((half, width), F32),
        pltpu.VMEM((half, width), F32),
    ]
    scratch += [pltpu.VMEM((2, half, width), BF)] * 4
    scratch += [
        dma((nb, 2 * NZ)), dma((nb, 2 * NZ)), dma((nb, 2 * NZ)), dma((nb, 2, NZ, NY)), dma((nb,)),
        dma((3 * NZ,)), dma((NZ, NY)), dma, dma((2,)),
        dma((8,)), dma((8,)), dma((2, 2)), dma((2,)), dma, dma((len(SAVED), 2)), dma((nb,)), dma((3,)),
        dma((3,)), dma((3,)), dma((NZ * NY,)), dma((NZ * NY,)),
    ]
    return pl.pallas_call(
        forward_kernel,
        out_shape=outs,
        in_specs=[ANY] * (nb + 1) + [VMEM, VMEM, ANY],
        out_specs=out_specs,
        scratch_shapes=scratch,
        compiler_params=pltpu.CompilerParams(collective_id=1, has_side_effects=True, vmem_limit_bytes=60 << 20),
        name="forward",
    )(*blocks, pool, tok, seg, drop)


def run_backward(weights, saved, vec, seg, drop, gcls):
    half, width = drop.shape[2:]
    head = width // 4
    dma = pltpu.SemaphoreType.DMA
    by_name = dict(zip(BLOCKS[1:], weights))
    blocks = [by_name[n].shape[3:] for n in GRADS]
    nb = len(GRADS)
    shape = jax.ShapeDtypeStruct
    thin, wide = by_name["up0"].shape[3:]
    outs = [
        shape((half, width), F32),
        shape((2, thin, wide), F32),
        shape((2, thin, wide), F32),
        shape(by_name["proj"].shape[3:], F32),
        shape(by_name["qkv"].shape[3:], F32),
        shape((24, width), F32),
    ]

    def per_block(shape_of, kind=BF):
        return [pltpu.VMEM(shape_of(r, w, r // 32 * 16), kind) for r, w in blocks]

    scratch = per_block(lambda r, w, h: (2, NZ, NY, r, w))
    scratch += per_block(lambda r, w, h: (NZ, NY, h, w))
    scratch += per_block(lambda r, w, h: (2, NZ, r - h, w))
    scratch += per_block(lambda r, w, h: (NZ, r - h, w))
    scratch += per_block(lambda r, w, h: (NZ, h, w))
    scratch += per_block(lambda r, w, h: (NZ + 1, r, w))
    scratch += [pltpu.VMEM(blocks[k], F32) for k in (0, 4, 5)]
    scratch += [pltpu.VMEM(s, t) for s, t in saved_shapes(half, width).values()]
    rows = by_name["qkv"].shape[3]
    scratch += [
        pltpu.VMEM((2, NZ, NY, rows, 3 * head + 64), BF),
        pltpu.VMEM(by_name["proj"].shape, BF),
        pltpu.VMEM(by_name["up0"].shape, BF),
        pltpu.VMEM(by_name["down0"].shape, BF),
        pltpu.VMEM((2, half, width), drop.dtype),
        pltpu.VMEM((2, head, width), BF),
        pltpu.VMEM((512, width), BF),
        pltpu.VMEM((512, width), BF),
        pltpu.VMEM((half, width), BF),
        pltpu.VMEM((half, width), BF),
        pltpu.VMEM((half, width), BF),
        pltpu.VMEM((128, width), BF),
        pltpu.VMEM((2, 2, 128, width), BF),
        pltpu.VMEM((2, 512, head), BF),
        pltpu.VMEM((640, head), F32),
        pltpu.VMEM((640, head), F32),
        pltpu.VMEM((640, head), F32),
        pltpu.VMEM((2, 640, 2 * head), BF),
        pltpu.VMEM((2, 640, head + 64), BF),
        pltpu.VMEM((2, head, width), BF),
        pltpu.VMEM((half, width), F32),
        pltpu.VMEM((half, width), F32),
        pltpu.VMEM((24, width), F32),
        pltpu.VMEM((5, 24, width), F32),
    ]
    scratch += [
        dma((5,)), dma((len(SAVED),)), dma((2,)), dma((nb,)), dma((8,)), dma((8,)), dma((2,)), dma((2, 2)),
        dma((nb, 2)), dma((nb, 2)), dma((nb, 2)), dma((nb, 2)), dma((nb, 2, NZ)), dma((nb, NZ + 1)),
        dma((5,)), dma((5,)), dma,
    ]
    return pl.pallas_call(
        backward_kernel,
        out_shape=outs,
        in_specs=[ANY] * (len(weights) + len(saved)) + [VMEM, VMEM, ANY, VMEM],
        out_specs=[ANY, ANY, ANY, ANY, ANY, VMEM],
        scratch_shapes=scratch,
        compiler_params=pltpu.CompilerParams(collective_id=2, has_side_effects=True, vmem_limit_bytes=63 << 20),
        name="backward",
    )(*weights, *saved, vec, seg, drop, gcls)


def per_device(tokens_in, segments, pairing, drop_masks, w_qkv, w_out, w_in, w_back, b_in, biases,
               gains, pool_w, pool_b):
    inner = lax.axis_size("g")
    layers = w_qkv.shape[0]
    width = tokens_in.shape[1]
    z, y, x, c = position()
    m = 2 * x + c
    dp = (z * NY + y) * inner + lax.axis_index("g")

    def group(arr, dim):
        return arr if inner == 1 else lax.all_gather(arr, "g", axis=dim, tiled=True)

    w_qkv, w_out, w_in, w_back = group(w_qkv, 2), group(w_out, 1), group(w_in, 1), group(w_back, 1)
    b_in, biases, gains = group(b_in, 1), group(biases, 2), group(gains, 2)
    pool_w, pool_b, pairing = group(pool_w, 0), group(pool_b, 0), group(pairing, 0)
    rows = w_in.shape[1]

    def wide(values):
        values = values.reshape(-1, values.shape[-1])
        return jnp.pad(values, ((0, 0), (0, 128 - values.shape[1])))

    small = jnp.concatenate([
        wide(b_in), wide(biases), wide(gains), wide(pool_b),
        wide((pairing // 32).astype(BF)), wide((pairing % 32).astype(BF))], 0)
    small = jnp.pad(small, ((0, 32 - small.shape[0]), (0, 0)))
    qkv = jnp.concatenate([w_qkv[0, 0], w_qkv[0, 1], w_qkv[1, 0], w_qkv[1, 1], w_qkv[0, 2], w_qkv[1, 2]], 1)
    proj = w_out.reshape(-1, width)
    blocks = [small, qkv, proj, w_in[0], w_back[0], w_in[1], w_back[1]]
    res = run_forward(blocks, pool_w, tokens_in, segments, drop_masks)
    named = dict(zip(FWD_OUT, res))
    cls = named["o_cls"].reshape(NZ * NY, SEGS, width)
    if inner > 1:
        cls = lax.all_gather(cls, "g", axis=1, tiled=True)
    cls = cls.reshape(-1, width)
    loss, align, unif, grad_pool_w, grad_pool_b, gcls = pooled_loss(cls, named["o_pool"], named["o_vec"], named["o_piece"])
    weights = [named["o_" + n] for n in BLOCKS[1:]]
    saved = [named["o_" + n] for n in SAVED]
    grad_x, down, up, proj, qkv, sums = run_backward(weights, saved, named["o_vec"], segments, drop_masks, gcls)

    def spread(values, dim):
        return values if inner == 1 else lax.psum_scatter(values, "g", scatter_dimension=dim, tiled=True)

    part = w_qkv.shape[3]
    pieces = [qkv[:, k * part : (k + 1) * part] for k in range(6)]
    out_qkv = jnp.stack([jnp.stack([pieces[0], pieces[1], pieces[4]]), jnp.stack([pieces[2], pieces[3], pieces[5]])])
    if inner > 1:
        sums = lax.psum(sums, "g")
    thin = rows // (4 * inner)
    here = lax.dynamic_slice_in_dim(sums[:16], dp * 4 * thin + m * thin, thin, 1)
    up_sums = sums[16:24].reshape(layers, 4 * width)
    n_up = rows // inner
    out_b_in = lax.dynamic_slice_in_dim(up_sums, m * width + dp * n_up, n_up, 1)
    n_pool = pool_w.shape[0] // inner
    g = lax.axis_index("g")
    if inner > 1:
        grad_pool_w = lax.dynamic_slice_in_dim(grad_pool_w, g * n_pool, n_pool, 0)
    grad_pool_b = lax.dynamic_slice_in_dim(grad_pool_b[0], dp * n_pool, n_pool, 0)
    return (
        loss[:, 0],
        align[:, 0],
        unif[:, 0],
        grad_x,
        spread(out_qkv, 2),
        spread(proj.reshape(layers, -1, width), 1),
        spread(up, 1),
        spread(down, 1),
        out_b_in,
        here[:12].reshape(layers, 6, thin),
        here[12:].reshape(layers, 2, thin),
        grad_pool_w,
        grad_pool_b,
    )


def solution(mesh):
    count = mesh.shape["dp"]
    fine = Mesh(
        mesh.devices.reshape(NZ, NY, count // (NZ * NY), 2, 2), ("z", "y", "g", "x", "c")
    )
    dp, mp = ("z", "y", "g"), ("x", "c")
    in_specs = (
        P(dp + mp, None),
        P(dp, None),
        P(dp),
        P(None, None, dp + mp, None),
        P(None, None, dp, mp),
        P(None, mp + dp, None),
        P(None, dp, mp),
        P(None, mp + dp, None),
        P(None, mp + dp),
        P(None, None, dp),
        P(None, None, dp),
        P(dp, None),
        P(dp),
    )
    out_specs = (
        P(dp),
        P(dp),
        P(dp),
        P(dp + mp, None),
        P(None, None, dp, mp),
        P(None, mp + dp, None),
        P(None, dp, mp),
        P(None, mp + dp, None),
        P(None, mp + dp),
        P(None, None, dp + mp),
        P(None, None, dp + mp),
        P(dp, None),
        P(dp),
    )
    return jax.shard_map(
        per_device, mesh=fine, in_specs=in_specs, out_specs=out_specs, check_vma=False
    )
```

```python
import jax
import jax.numpy as jnp
from jax import lax
from jax.experimental import pallas as pl
from jax.experimental.pallas import tpu as pltpu
from jax.sharding import Mesh
from jax.sharding import PartitionSpec as P

HEAD_DIM = 64
SEGS = 16
TEMP = 0.05
EPS = 1e-06
KEEP = 0.9
MESH = pl.DeviceIdType.MESH
ANY = pl.BlockSpec(memory_space=pl.ANY)
VMEM = pl.BlockSpec(memory_space=pltpu.VMEM)
BF = jnp.bfloat16
F32 = jnp.float32
NZ = 4
NY = 2


class Names:
    def __init__(self, names, refs):
        for name, ref in zip(names, refs, strict=True):
            setattr(self, name, ref)


def contract(left_side, right_side, left_dim, right_dim):
    return lax.dot_general(
        left_side,
        right_side,
        (((left_dim,), (right_dim,)), ((), ())),
        preferred_element_type=F32,
    )


def mm(a, b):
    return jnp.dot(a, b, preferred_element_type=F32)


def position():
    return tuple(lax.axis_index(name) for name in ("z", "y", "x", "c"))


def signal(sem, device):
    pl.semaphore_signal(sem, inc=1, device_id=device, device_id_type=MESH)


def remote(src, dst, send_sem, recv_sem, device):
    return pltpu.make_async_remote_copy(
        src_ref=src,
        dst_ref=dst,
        send_sem=send_sem,
        recv_sem=recv_sem,
        device_id=device,
        device_id_type=MESH,
    )


def landed(ref, sem):
    pltpu.make_async_copy(ref, ref, sem).wait()


def rows_at(start, count):
    return pl.ds(pl.multiple_of(start, 128), count)


def flat(ref):
    value = ref[...]
    return value.reshape(-1, value.shape[-1])


SMALL, QKV, PROJ, UP0, DOWN0, UP1, DOWN1 = range(7)
BLOCKS = ("small", "qkv", "proj", "up0", "down0", "up1", "down1")
SAVED = ("xw", "q", "k", "v", "p", "att", "zf", "gp", "act", "yh1", "yh2", "r1", "r2", "kp")
FWD_IN = BLOCKS + ("pool", "tok", "seg", "drop")
FWD_OUT = tuple("o_" + n for n in BLOCKS[1:]) + ("o_pool", "o_piece", "o_vec", "o_cls") + tuple("o_" + n for n in SAVED)
FWD_SCR = (
    tuple("w_" + n for n in BLOCKS) + ("w_pool", "cls_part", "cls_all") + SAVED
    + ("keep", "bias", "wo", "vec", "qv", "h", "z", "sa", "ra", "sf", "rf")
    + ("zsend", "xsend", "ysend", "recv", "own_sem", "pool_send", "pool_recv", "pool_own", "pool_core",
       "core_send", "core_recv", "halo_send", "halo_recv", "drop_sem", "out_sem", "w_sem", "misc_sem",
       "s1", "r1s", "s2", "r2s")
)


FORWARD_ORDER = (
    "L.P", "L.D1", "L.S", "L.U1", "R0.P", "masks", "L.U0", "Z1.S", "L.Q", "Z2.S", "Z1.D1", "R0.S", "Z3.S",
    "R0.U1", "R0.U0", "Z2.D1", "Z1.P", "Z1.U0", "E.P", "R2.S", "R0.Q", "R1.S", "L.D0", "R0.D1", "Z1.Q",
    "Z3.D1", "E.U0", "E.U1", "Z2.Q", "R0.D0", "F1.U0", "Z2.U0", "F1.P", "Z3.Q", "R3.S", "pool_launch",
    "F1.U1", "Z3.U0", "F2.U0", "R1.Q", "F2.P", "E.D0", "R1.D1", "pool_relay1", "Z2.P", "C.S", "F3.U0", "F3.P",
    "R2.Q", "pool_relay2", "pool_relay3", "Z3.P", "R2.D1", "spread", "R3.Q", "F1.D0", "F2.D0", "Z1.D0",
    "pool_swap", "C.Q", "Z1.U1", "proj0a", "proj0b", "proj0c", "Z2.D0", "att0a", "C.P", "att0b", "prow",
    "Z3.D0", "ao0a", "Z2.U1", "C.U0", "R3.D1", "ao0b", "F3.D0", "Z3.U1", "up0a", "up0b", "C.D0", "dn0a",
    "F2.U1", "dn0b", "C.D1", "proj1a", "proj1b", "pool_done", "F3.U1", "proj1c", "att1a", "C.U1", "att1b",
    "ao1a", "ao1b", "up1a", "up1b", "dn1a", "dn1b", "pooled",
)


def forward_kernel(*refs):
    R = Names(FWD_IN + FWD_OUT + FWD_SCR, refs)
    z, y, x, c = position()
    up, down = z < NZ - 1, z > 0
    xdev, ydev, cdev, xcdev = {"x": 1 - x}, {"y": 1 - y}, {"c": 1 - c}, {"x": 1 - x, "c": 1 - c}
    half = R.tok.shape[0]
    ins = [getattr(R, n) for n in BLOCKS]
    lands = [getattr(R, "w_" + n) for n in BLOCKS]

    peers = [(k * NY + flip, k, flip) for k in range(NZ) for flip in range(NY) if k or flip]

    def peer(k, flip):
        return {"z": lax.rem(z + k, NZ), "y": y if flip == 0 else 1 - y}

    bar = pltpu.get_barrier_semaphore()
    for dev in (xdev, cdev, xcdev):
        signal(bar, dev)
    for _, k, flip in peers:
        signal(bar, peer(k, flip))
    pl.semaphore_wait(bar, 3 + len(peers))


    def copy(b, src, slot, device, sem):
        return remote(src, lands[b].at[slot], sem, R.recv.at[(b, *slot)], device)

    def arrived(b, slot):
        landed(lands[b].at[slot], R.recv.at[(b, *slot)])

    def by_z(b):
        return b in (PROJ, UP0, DOWN0, UP1)

    def over_y(b):
        return b in (SMALL, UP0, UP1, DOWN1)

    def sideways(b, src, slot, k):
        copy(b, src, slot, xdev, R.xsend.at[b, k]).start()
        copy(b, src, slot, ydev, R.ysend.at[b, k]).start()

    def launch(b):
        src, mine = ins[b], (x, z, y)
        pl.when(up)(lambda: copy(b, src, mine, {"z": z + 1}, R.zsend.at[b, 0]).start())
        pl.when(down)(lambda: copy(b, src, mine, {"z": z - 1}, R.zsend.at[b, 1]).start())
        sideways(b, src, mine, 0)
        pltpu.make_async_copy(src, lands[b].at[mine], R.own_sem.at[b]).start()

    def z_relay(b, d):
        @pl.when(z >= d)
        def _():
            slot = (x, z - d, y)
            arrived(b, slot)
            pl.when(up)(lambda: copy(b, lands[b].at[slot], slot, {"z": z + 1}, R.zsend.at[b, 2 * d]).start())
            sideways(b, lands[b].at[slot], slot, NZ - d)

        @pl.when(z < NZ - d)
        def _():
            slot = (x, z + d, y)
            arrived(b, slot)
            pl.when(down)(lambda: copy(b, lands[b].at[slot], slot, {"z": z - 1}, R.zsend.at[b, 2 * d + 1]).start())
            sideways(b, lands[b].at[slot], slot, d)

    def xy_relay(b, k):
        zp = lax.rem(z + k, NZ)
        sx, sy = (1 - x, zp, y), (x, zp, 1 - y)
        if over_y(b):
            arrived(b, sx)
            copy(b, lands[b].at[sx], sx, ydev, R.ysend.at[b, NZ + k]).start()
        else:
            arrived(b, sy)
            copy(b, lands[b].at[sy], sy, xdev, R.xsend.at[b, NZ + k]).start()

    def corner_launch(b):
        slot = (1 - x, z, 1 - y)
        arrived(b, slot)
        pl.when(up)(lambda: copy(b, lands[b].at[slot], slot, {"z": z + 1}, R.zsend.at[b, 2 * NZ]).start())
        pl.when(down)(lambda: copy(b, lands[b].at[slot], slot, {"z": z - 1}, R.zsend.at[b, 2 * NZ + 1]).start())

    def corner_relay(b, d):
        @pl.when(z >= d)
        def _():
            slot = (1 - x, z - d, 1 - y)
            arrived(b, slot)
            pl.when(up)(lambda: copy(b, lands[b].at[slot], slot, {"z": z + 1}, R.zsend.at[b, 2 * NZ + 2 * d]).start())

        @pl.when(z < NZ - d)
        def _():
            slot = (1 - x, z + d, 1 - y)
            arrived(b, slot)
            pl.when(down)(lambda: copy(b, lands[b].at[slot], slot, {"z": z - 1}, R.zsend.at[b, 2 * NZ + 2 * d + 1]).start())

    def complete(b):
        relays = 1 if by_z(b) else NZ
        for k in range(NZ):
            zp = lax.rem(z + k, NZ)
            if k >= relays or not over_y(b):
                arrived(b, (1 - x, zp, y))
            if k >= relays or over_y(b):
                arrived(b, (x, zp, 1 - y))
            if not by_z(b):
                arrived(b, (1 - x, zp, 1 - y))
        pltpu.make_async_copy(ins[b], lands[b].at[x, z, y], R.own_sem.at[b]).wait()
        if b != SMALL:
            w_copy(b).start()

    def sends_done(b):
        src, mine = ins[b], (x, z, y)
        for k in range(NZ):
            copy(b, src, mine, xdev, R.xsend.at[b, k]).wait_send()
            copy(b, src, mine, ydev, R.ysend.at[b, k]).wait_send()
        for k in range(1 if by_z(b) else NZ):
            if over_y(b):
                copy(b, src, mine, ydev, R.ysend.at[b, NZ + k]).wait_send()
            else:
                copy(b, src, mine, xdev, R.xsend.at[b, NZ + k]).wait_send()
        for d in range(NZ):
            for base in (0, 2 * NZ) if by_z(b) else (0,):
                pl.when(up & (z >= d))(lambda: copy(b, src, mine, {"z": z + 1}, R.zsend.at[b, base + 2 * d]).wait_send())
                pl.when(down & (z < NZ - d))(lambda: copy(b, src, mine, {"z": z - 1}, R.zsend.at[b, base + 2 * d + 1]).wait_send())

    prow = R.pool.shape[0] // 2
    pool_rows = pl.ds(pl.multiple_of(c * prow, 16), prow)

    def pool_slot(zp, yp):
        return R.w_pool.at[zp, yp, pool_rows]

    def pool_copy(src, zp, yp, device, k):
        return remote(src, pool_slot(zp, yp), R.pool_send.at[k], R.pool_recv.at[zp, yp], device)

    def pool_launch():
        src = R.pool.at[pool_rows]
        pl.when(up)(lambda: pool_copy(src, z, y, {"z": z + 1}, 0).start())
        pl.when(down)(lambda: pool_copy(src, z, y, {"z": z - 1}, 1).start())
        pool_copy(src, z, y, ydev, 2 * NZ).start()
        pltpu.make_async_copy(src, pool_slot(z, y), R.pool_own).start()

    def pool_relay(d):
        @pl.when(z >= d)
        def _():
            here = pool_slot(z - d, y)
            landed(here, R.pool_recv.at[z - d, y])
            pl.when(up)(lambda: pool_copy(here, z - d, y, {"z": z + 1}, 2 * d).start())
            pool_copy(here, z - d, y, ydev, 2 * NZ + NZ - d).start()

        @pl.when(z < NZ - d)
        def _():
            here = pool_slot(z + d, y)
            landed(here, R.pool_recv.at[z + d, y])
            pl.when(down)(lambda: pool_copy(here, z + d, y, {"z": z - 1}, 2 * d + 1).start())
            pool_copy(here, z + d, y, ydev, 2 * NZ + d).start()

    def pool_core():
        halves = R.w_pool.at[:, :, pool_rows]
        return remote(halves, halves, R.pool_core.at[0], R.pool_core.at[1], cdev)

    def pool_swap():
        pltpu.make_async_copy(R.pool.at[pool_rows], pool_slot(z, y), R.pool_own).wait()
        for k in range(NZ):
            zp = lax.rem(z + k, NZ)
            landed(pool_slot(zp, 1 - y), R.pool_recv.at[zp, 1 - y])
        pool_core().start()

    def pool_done():
        there = R.w_pool.at[:, :, pl.ds(pl.multiple_of((1 - c) * prow, 16), prow)]
        landed(there, R.pool_core.at[1])
        pool_core().wait_send()
        src = R.pool.at[pool_rows]
        for d in range(NZ):
            pl.when(up & (z >= d))(lambda: pool_copy(src, z, y, {"z": z + 1}, 2 * d).wait_send())
            pl.when(down & (z < NZ - d))(lambda: pool_copy(src, z, y, {"z": z - 1}, 2 * d + 1).wait_send())
            pool_copy(src, z, y, ydev, 2 * NZ + d).wait_send()
        for cp in misc_copies():
            cp.start()


    def win(core):
        return rows_at(x * 128 + core * half, half)

    def chip(core):
        return rows_at(core * half, half)

    def swap(src, dst, n):
        return remote(src, dst, R.core_send.at[n], R.core_recv.at[n], cdev)

    def rows_swap(layer):
        here = R.xw.at[layer, win(c)]
        return swap(here, here, 4 * layer)

    def edge_copies(layer):
        src = R.xw.at[layer, rows_at(x * 128 + c * half + 128 * c, 128)]
        dst = R.xw.at[layer, rows_at(x * 512, 128)]
        return [
            remote(src, dst, R.halo_send.at[layer, i], R.halo_recv.at[layer], dev)
            for i, dev in enumerate(({"x": 1 - x, "c": c}, {"x": 1 - x, "c": 1 - c}))
        ]

    def send_rows(layer):
        rows_swap(layer).start()

        @pl.when(c == 1 - x)
        def _():
            for cp in edge_copies(layer):
                cp.start()

    def partner_rows_here(layer):
        landed(R.xw.at[layer, win(1 - c)], R.core_recv.at[4 * layer])

    def edge_here(layer):
        landed(R.xw.at[layer, rows_at((1 - x) * 512, 128)], R.halo_recv.at[layer])


    def vec(layer, k):
        return R.vec[0, 2 + 6 * layer + k : 3 + 6 * layer + k, :]

    def gain(layer, k):
        return R.vec[0, 14 + 2 * layer + k : 15 + 2 * layer + k, :]

    def spread_params():
        width = R.vec.shape[2]
        part = width // (NZ * NY)
        lane = lax.broadcasted_iota(jnp.int32, (128, width), 0)
        col = lax.broadcasted_iota(jnp.int32, (128, width), 1)
        for j in range(2):
            total = jnp.zeros((R.vec.shape[1], width), F32)
            for dp in range(NZ * NY):
                place = ((lane < part) & (col == lane + dp * part)).astype(F32).astype(BF)
                total = total + mm(R.w_small[j, dp // NY, dp % NY], place)
            R.vec[j] = total
        head = R.qv.shape[2]
        lane = lax.broadcasted_iota(jnp.int32, (width, head), 0)
        col = lax.broadcasted_iota(jnp.int32, (width, head), 1)
        low = R.vec[0].astype(BF)
        for j in range(2):
            place = (lane == col + (2 * j + c) * head).astype(F32).astype(BF)
            R.qv[j] = mm(low, place)

    def masks():
        for i in range(4):
            mine = R.seg[0:1, rows_at(x * 512 + i * 128, 128)]
            start = (3 * (x + i) + 1) // 5 * 128
            keys = R.seg[0:1, rows_at(x * 384 + start, 384)]
            column = jnp.transpose(jnp.broadcast_to(mine, (128, 128)))
            for t in range(3):
                same = column == jnp.broadcast_to(keys[:, t * 128 : t * 128 + 128], (128, 128))
                R.bias[i, :, t * 128 : t * 128 + 128] = jnp.where(same, 0.0, -1000000000.0)

    def proj_rows():
        for layer in range(2):
            for j in range(2):
                value = R.w_proj[j].astype(F32)
                rows = value.shape[2] // 2
                value = value[:, :, layer * rows : (layer + 1) * rows].reshape(-1, value.shape[3])
                R.wo[layer, j] = value.astype(BF)

    def project(layer, wrow, count, crow):
        xx = R.xw[layer, wrow]
        head = R.q.shape[3]
        for j in range(2):
            w = R.w_qkv.at[j]
            wqk = w[:, :, :, layer * 2 * head : (layer + 1) * 2 * head].reshape(-1, 2 * head)
            yqk = mm(xx, wqk)
            if crow is not None:
                bq = R.qv[j, 2 + 6 * layer : 3 + 6 * layer, :]
                R.q[layer, j, crow] = (yqk[:, :head] + bq).astype(BF) * jnp.asarray(0.125, BF)
            R.k[layer, j, wrow] = yqk[:, head:].astype(BF)
            bv = R.qv[j, 3 + 6 * layer : 4 + 6 * layer, :]
            if layer == 0:
                yv = mm(xx, w[:, :, :, 4 * head : 5 * head].reshape(-1, head))
            else:
                yv = mm(xx, w[:, :, :, 5 * head - 64 : 6 * head].reshape(-1, head + 64))[:, 64:]
            R.v[layer, j, wrow] = (yv + bv).astype(BF)

    def attend(layer, j):
        head = R.q.shape[3]
        lane = lax.broadcasted_iota(jnp.int32, (1, head), 1) // HEAD_DIM
        picks = [(lane == n).astype(F32) for n in range(head // HEAD_DIM)]
        count = len(picks)

        @pl.loop(0, 4)
        def _(i):
            keys = rows_at((3 * (x + i) + 1) // 5 * 128, 384)
            mine = rows_at(i * 128, 128)
            qq = R.q[layer, j, mine]
            q3 = jnp.concatenate([qq * pick.astype(BF) for pick in picks], 0)
            scores = contract(q3, R.k[layer, j, keys], 1, 1)
            bias = R.bias[i]
            scores = scores.reshape(count, 128, 384) + bias[None]
            peak = jnp.max(scores, -1, keepdims=True)
            e = jnp.exp(scores - peak)
            p = (e * (1.0 / jnp.sum(e, -1, keepdims=True))).astype(BF).reshape(count * 128, 384)
            R.p[layer, j, i] = p
            o = mm(p, R.v[layer, j, keys])
            total = o[0:128] * picks[0]
            for n in range(1, count):
                total = total + o[n * 128 : (n + 1) * 128] * picks[n]
            R.att[layer, j, mine] = total.astype(BF)

        if j == 1:
            save(layer, "p", "att")

    def proj_part(layer, rows):
        return mm(R.att[layer, 0, rows], R.wo[layer, 0]) + mm(R.att[layer, 1, rows], R.wo[layer, 1])

    def norm(value, g, s):
        center = jnp.mean(value, 1, keepdims=True)
        spread = lax.rsqrt(jnp.mean(value * value, 1, keepdims=True) - center * center + EPS)
        hat = (value - center) * spread
        return hat * g + s, hat, spread

    def attention_give(layer):
        R.sa[layer] = proj_part(layer, chip(1 - c)).astype(BF)
        swap(R.sa.at[layer], R.ra.at[layer], 4 * layer + 1).start()

    def attention_out(layer):
        if layer == 0:
            drop.wait()
            for n in range(2):
                for k in range(2):
                    R.kp[n, k] = R.keep[n, k].astype(F32).astype(BF)
                save(n, "kp")
        a = proj_part(layer, chip(c))
        swap(R.sa.at[layer], R.ra.at[layer], 4 * layer + 1).wait_recv()
        a = a + R.ra[layer].astype(F32) + vec(layer, 2)
        out, hat, spread = norm(R.h[...] + R.kp[layer, 0].astype(F32) * a * (1.0 / KEEP), gain(layer, 0), vec(layer, 3))
        R.z[...] = out
        R.yh1[layer] = hat.astype(BF)
        R.r1[layer] = spread
        R.zf[layer, chip(c)] = out.astype(BF)
        here = R.zf.at[layer, chip(c)]
        swap(here, here, 4 * layer + 2).start()
        save(layer, "yh1", "r1")

    def ffn_up(layer, own):
        if not own:
            landed(R.zf.at[layer, chip(1 - c)], R.core_recv.at[4 * layer + 2])
        rows = chip(c if own else 1 - c)
        w = R.w_up0 if layer == 0 else R.w_up1
        zz = R.zf[layer, rows]
        for j in range(2):
            hid = mm(zz, flat(w.at[j])) + R.vec[j, layer : layer + 1, :]
            cdf = 0.5 + 0.5 * lax.erf(hid * 0.7071067811865476)
            R.act[layer, j, rows] = (hid * cdf).astype(BF)
            R.gp[layer, j, rows] = (cdf + hid * jnp.exp(-0.5 * hid * hid) * 0.3989422804014327).astype(BF)
        if not own:
            save(layer, "zf", "gp", "act")

    def ffn_part(layer, rows):
        w = R.w_down0 if layer == 0 else R.w_down1
        return mm(R.act[layer, 0, rows], flat(w.at[0])) + mm(R.act[layer, 1, rows], flat(w.at[1]))

    def ffn_give(layer):
        R.sf[layer] = ffn_part(layer, chip(1 - c)).astype(BF)
        swap(R.sf.at[layer], R.rf.at[layer], 4 * layer + 3).start()

    def ffn_down(layer):
        f = ffn_part(layer, chip(c))
        swap(R.sf.at[layer], R.rf.at[layer], 4 * layer + 3).wait_recv()
        f = f + R.rf[layer].astype(F32) + vec(layer, 4)
        out, hat, spread = norm(R.z[...] + R.kp[layer, 1].astype(F32) * f * (1.0 / KEEP), gain(layer, 1), vec(layer, 5))
        R.h[...] = out
        R.yh2[layer] = hat.astype(BF)
        R.r2[layer] = spread
        if layer == 0:
            R.xw[1, win(c)] = out.astype(BF)
            send_rows(1)
        save(layer, "yh2", "r2")

    def project_part(layer, part):
        if part == 0:
            project(layer, win(c), half, chip(c))
        elif part == 1:
            partner_rows_here(layer)
            project(layer, win(1 - c), half, chip(1 - c))
        else:
            edge_here(layer)
            project(layer, rows_at((1 - x) * 512, 128), 128, None)
            save(layer, "xw", "q", "k", "v")


    def out_copy(k, layer):
        name = SAVED[k]
        return pltpu.make_async_copy(getattr(R, name).at[layer], getattr(R, "o_" + name).at[layer], R.out_sem.at[k, layer])

    def save(layer, *names):
        for name in names:
            out_copy(SAVED.index(name), layer).start()

    def w_copy(b):
        return pltpu.make_async_copy(lands[b], getattr(R, "o_" + BLOCKS[b]), R.w_sem.at[b])

    def misc_copies():
        return [
            pltpu.make_async_copy(R.w_pool, R.o_pool, R.misc_sem.at[0]),
            pltpu.make_async_copy(R.w_small.at[0], R.o_piece, R.misc_sem.at[1]),
            pltpu.make_async_copy(R.vec, R.o_vec, R.misc_sem.at[2]),
        ]


    def pooled():
        total = R.seg.shape[1]
        number = lax.broadcasted_iota(jnp.int32, (SEGS, total), 0)
        before = (jnp.broadcast_to(R.seg[...], (SEGS, total)) < number).astype(F32)
        starts = jnp.sum(before, 1, keepdims=True).astype(jnp.int32)
        mine = lax.broadcasted_iota(jnp.int32, (SEGS, half), 1) + (2 * x + c) * half
        pick = (mine == starts).astype(F32).astype(BF)
        row = mm(pick, R.h[...].astype(BF))
        R.cls_part[0] = row.astype(BF)
        first = [
            remote(R.cls_part.at[0], R.cls_part.at[1 + i], R.s1.at[i], R.r1s.at[i], dev)
            for i, dev in enumerate((xdev, cdev, xcdev))
        ]
        for cp in first:
            cp.start()
        for i, cp in enumerate(first):
            cp.wait_recv()
            row = row + R.cls_part[1 + i].astype(F32)
        here = R.cls_all.at[z, y]
        here[...] = row.astype(BF)
        second = [remote(here, here, R.s2.at[i], R.r2s.at[i], peer(k, flip)) for i, k, flip in peers]
        for cp in second:
            cp.start()
        for i, k, flip in peers:
            landed(R.cls_all.at[lax.rem(z + NZ - k, NZ), y if flip == 0 else 1 - y], R.r2s.at[i])
        for cp in first + second:
            cp.wait_send()
        R.o_cls[...] = R.cls_all[...]


    R.xw[0, win(c)] = R.tok[...]
    send_rows(0)
    drop = pltpu.make_async_copy(R.drop, R.keep, R.drop_sem)
    drop.start()
    R.h[...] = R.tok[...].astype(F32)
    short = {"S": SMALL, "Q": QKV, "P": PROJ, "U0": UP0, "D0": DOWN0, "U1": UP1, "D1": DOWN1}
    single = {"masks": masks, "spread": spread_params, "prow": proj_rows, "pooled": pooled,
              "pool_launch": pool_launch, "pool_swap": pool_swap, "pool_done": pool_done}
    staged = {
        "proja": lambda n: project_part(n, 0), "projb": lambda n: project_part(n, 1),
        "projc": lambda n: project_part(n, 2), "atta": lambda n: attend(n, 0), "attb": lambda n: attend(n, 1),
        "aoa": attention_give, "aob": attention_out, "upa": lambda n: ffn_up(n, True),
        "upb": lambda n: ffn_up(n, False), "dna": ffn_give, "dnb": ffn_down,
    }
    moves = {"L": launch, "E": corner_launch, "C": complete}
    hops = {"Z": z_relay, "R": xy_relay, "F": corner_relay}
    for step in FORWARD_ORDER:
        if "." in step:
            kind, block = step.split(".")
            if kind in moves:
                moves[kind](short[block])
            else:
                hops[kind[0]](short[block], int(kind[1]))
        elif step.startswith("pool_relay"):
            pool_relay(int(step[-1]))
        elif step in single:
            single[step]()
        else:
            name = "".join(ch for ch in step if not ch.isdigit())
            staged[name](int("".join(ch for ch in step if ch.isdigit())))

    for b in range(len(BLOCKS)):
        sends_done(b)
        if b != SMALL:
            w_copy(b).wait()
    for cp in misc_copies():
        cp.wait()
    for layer in range(2):
        for k in range(len(SAVED)):
            out_copy(k, layer).wait()
        rows_swap(layer).wait_send()
        swap(R.sa.at[layer], R.ra.at[layer], 4 * layer + 1).wait_send()
        swap(R.zf.at[layer, chip(c)], R.zf.at[layer, chip(c)], 4 * layer + 2).wait_send()
        swap(R.sf.at[layer], R.rf.at[layer], 4 * layer + 3).wait_send()

        @pl.when(c == 1 - x)
        def _():
            for cp in edge_copies(layer):
                cp.wait_send()


def loss_kernel(cls, pool, vec, piece, loss, align, unif, gw, gb, gcls, u, nb, rn, dn, dpre, table, gw_all):
    z, y = lax.axis_index("z"), lax.axis_index("y")
    inner = lax.axis_size("g")
    count, width = cls.shape
    per = SEGS * inner
    pre = mm(cls[...], pool[...].reshape(width, width)) + vec[0, 18:19, :]
    value = jnp.tanh(pre)
    u[...] = value
    scale = lax.rsqrt(jnp.sum(value * value, 1, keepdims=True) + EPS)
    rn[...] = scale
    nb[...] = (value * scale).astype(BF)
    low = nb[...].astype(F32)
    squares_row = lax.dot_general(
        jnp.ones((8, width), F32), low * low, (((1,), (1,)), ((), ())),
        precision=lax.Precision.HIGHEST, preferred_element_type=F32)[0:1]
    dn[...] = jnp.zeros_like(dn)

    @pl.loop(0, count // 128)
    def _(blk):
        rows = rows_at(blk * 128, 128)
        ids = lax.broadcasted_iota(jnp.int32, (128, 1), 0) + blk * 128
        cols = lax.broadcasted_iota(jnp.int32, (1, count), 1)
        pair = jnp.zeros((128, 1), F32)
        lane = lax.broadcasted_iota(jnp.int32, (1, 128), 1)
        for o in range(NZ * NY):
            got = piece[o // NY, o % NY]
            number = got[19:20].astype(F32) * 32.0 + got[20:21].astype(F32)
            here = (ids == o * per + lane) & (lane < per)
            pair = pair + jnp.sum(jnp.where(here, number, 0.0), 1, keepdims=True)
        mine = nb[rows]
        gram = contract(mine, nb[...], 1, 1)
        logits = gram * (1.0 / TEMP)
        own = cols == ids
        twin = cols == pair.astype(jnp.int32)
        masked = jnp.where(own, -1000000000.0, logits)
        peak = jnp.max(masked, 1, keepdims=True)
        e = jnp.exp(masked - peak)
        total = jnp.sum(e, 1, keepdims=True)
        low_mine = mine.astype(F32)
        squares = jnp.sum(low_mine * low_mine, 1, keepdims=True)
        distance = squares + squares_row - 2.0 * gram
        terms = (
            peak + jnp.log(total) - jnp.sum(jnp.where(twin, logits, 0.0), 1, keepdims=True),
            jnp.sum(jnp.where(twin, distance, 0.0), 1, keepdims=True),
            jnp.log(jnp.sum(jnp.where(own, 0.0, jnp.exp(-2.0 * distance)), 1, keepdims=True) * (1.0 / (count - 1))),
        )
        for t in range(3):
            table[t, rows] = jnp.broadcast_to(terms[t], (128, 128))
        dg = ((e * (1.0 / total) - jnp.where(twin, 1.0, 0.0)) * (1.0 / TEMP)).astype(BF)
        dn[rows] += mm(dg, nb[...])
        dn[...] += contract(dg, mine, 0, 0)

    grad = dn[...]
    value = u[...]
    unit = value * rn[...]
    du = rn[...] * (grad - unit * jnp.sum(grad * unit, 1, keepdims=True))
    dpre[...] = (du * (1.0 - value * value)).astype(BF)
    dp = (z * NY + y) * inner + lax.axis_index("g")
    mine = pl.ds(pl.multiple_of(dp * SEGS, SEGS), SEGS)
    gcls[...] = contract(dpre[mine], pool[...].reshape(width, width), 1, 1)
    gb[...] = jnp.sum(dpre[...].astype(F32), 0, keepdims=True)
    gw_all[...] = contract(cls[...], dpre[...], 0, 0)
    part = gw.shape[0]
    gw[...] = gw_all[pl.ds(pl.multiple_of((z * NY + y) * part, 8), part)]
    for t, ref in enumerate((loss, align, unif)):
        ref[...] = table[t, mine][:, 0:1]


def pooled_loss(cls, pool, vec, piece):
    count, width = cls.shape
    part = width // (NZ * NY)
    one = jax.ShapeDtypeStruct((SEGS, 1), F32)
    return pl.pallas_call(
        loss_kernel,
        out_shape=[
            one, one, one,
            jax.ShapeDtypeStruct((part, width), F32),
            jax.ShapeDtypeStruct((1, width), F32),
            jax.ShapeDtypeStruct((SEGS, width), F32),
        ],
        in_specs=[VMEM] * 4,
        out_specs=[VMEM] * 6,
        scratch_shapes=[
            pltpu.VMEM((count, width), F32),
            pltpu.VMEM((count, width), BF),
            pltpu.VMEM((count, 1), F32),
            pltpu.VMEM((count, width), F32),
            pltpu.VMEM((count, width), BF),
            pltpu.VMEM((3, count, 128), F32),
            pltpu.VMEM((width, width), F32),
        ],
        compiler_params=pltpu.CompilerParams(vmem_limit_bytes=48 << 20),
        name="pooled_loss",
    )(cls, pool, vec, piece)


GRADS = ("down1", "up1", "qk1", "down0", "up0", "proj", "last")
CORNER = {"down1": "x", "up1": "y", "qk1": "x"}
BWD_IN = BLOCKS[1:] + SAVED + ("vec", "seg", "gcls")
BWD_OUT = ("gx", "o_down", "o_up", "o_proj", "o_qk1", "o_last", "o_small")
BWD_SCR = (
    tuple("g_" + n for n in GRADS) + tuple("zr_" + n for n in GRADS)
    + tuple("px_" + n for n in GRADS) + tuple("py_" + n for n in GRADS)
    + tuple(t + n for n in GRADS for t in (("pd_", "zd_") if n in CORNER else ("qx_", "qy_")))
    + ("st_ffn", "st_proj", "st_qk1", "st_last") + tuple("v_" + n for n in SAVED)
    + ("w_qkv", "w_proj", "w_up", "w_down", "wo", "dff", "daf", "send", "rz", "rh",
       "hs", "hr", "datt", "dq", "dk", "dv", "dqk", "dvp", "dwo", "dh", "dy", "small", "small_in")
    + ("w_sem", "v_sem", "out_sem", "csend", "crecv", "hsend", "hrecv",
       "s1", "rx", "ry", "rd", "s2", "r2s", "zs", "zrs", "bs", "br", "gx_sem")
)
BACKWARD_ORDER = (
    "fn1", "fw1", "dga1", "dgb1", "down1.E0", "dha1", "dhb1", "mida1", "midb1", "midc1", "uga1", "pr1",
    "down1.E1d", "ugb1", "aw1", "pd1", "up1.E0", "aba1", "abb1", "inh1", "qga1", "up1.E1d", "pr0", "up1.E1u",
    "ina1", "pg1", "qgb1", "qk1.E0", "inb1", "inc1", "fn0", "down1.E1u", "free1", "up1.E2", "fw0", "dha0",
    "dhb0", "mida0", "up1.E3", "midb0", "uga0", "ugb0", "up0.S1", "qk1.E1u", "up1.E4", "midc0", "down1.E2",
    "aw0", "dga0", "qk1.E1d", "pg0", "dgb0", "down0.S1", "qk1.E2", "down1.E3", "up0.S2", "pd0", "up1.E5u",
    "aba0", "up1.E5d", "abb0", "sm0", "down1.E4", "down0.S2", "qga0", "qgb0", "down1.E5d", "proj.S1",
    "up1.E6", "qk1.E3", "last.S1", "down1.E5u", "up0.S3", "up0.E5d", "sw0", "up0.E5u", "qk1.E4", "down0.S3",
    "down1.E6", "proj.S2", "qk1.E5u", "sm1", "qk1.E5d", "last.S2", "down0.E5d", "down0.E5u", "proj.S3",
    "inh0", "ina0", "sw1", "qk1.E6", "last.S3", "inb0", "sm2", "last.E5u", "last.E5d", "proj.E5u", "sw2",
    "sm3", "proj.E5d", "sw3", "sm4", "up0.E6", "last.E6", "inc0", "proj.E6", "down0.E6", "sw4",
)


def backward_kernel(*refs):
    R = Names(BWD_IN + BWD_OUT + BWD_SCR, refs)
    z, y, x, c = position()
    up, down = z < NZ - 1, z > 0
    xdev, ydev, cdev = {"x": 1 - x}, {"y": 1 - y}, {"c": 1 - c}
    half = R.gx.shape[0]
    head = R.q.shape[3]
    width = R.gx.shape[1]


    def v_copy(name, layer):
        k = SAVED.index(name)
        return pltpu.make_async_copy(getattr(R, name).at[layer], getattr(R, "v_" + name), R.v_sem.at[k])

    def load(layer, *names):
        for name in names:
            v_copy(name, layer).start()

    def need(layer, *names):
        for name in names:
            v_copy(name, layer).wait()

    def qkv_copies(layer):
        src, dst = R.qkv, R.w_qkv
        low = 4 * head if layer == 0 else 5 * head - 64
        return [
            pltpu.make_async_copy(src.at[:, :, :, :, layer * 2 * head : (layer + 1) * 2 * head],
                                  dst.at[:, :, :, :, 0 : 2 * head], R.w_sem.at[0]),
            pltpu.make_async_copy(src.at[:, :, :, :, low : low + head + 64],
                                  dst.at[:, :, :, :, 2 * head : 3 * head + 64], R.w_sem.at[1]),
        ]

    def up_copy(layer):
        return pltpu.make_async_copy(R.up0 if layer == 0 else R.up1, R.w_up, R.w_sem.at[2])

    def down_copy(layer):
        return pltpu.make_async_copy(R.down0 if layer == 0 else R.down1, R.w_down, R.w_sem.at[3])

    def proj_copy():
        return pltpu.make_async_copy(R.proj, R.w_proj, R.w_sem.at[4])

    load(1, "yh2", "r2", "kp", "act")
    down_copy(1).start()
    load(1, "gp", "zf")
    up_copy(1).start()
    load(1, "yh1", "r1", "att")
    proj_copy().start()
    load(1, "p", "q", "k", "v", "xw")
    for cp in qkv_copies(1):
        cp.start()

    zp1 = z + 1 - 2 * lax.rem(z, 2)
    zp2 = lax.rem(z + 2, NZ)
    bar = pltpu.get_barrier_semaphore()
    for dev in (xdev, ydev, cdev, {"x": 1 - x, "c": 1 - c}):
        signal(bar, dev)
    for k in range(1, NZ):
        signal(bar, {"z": lax.rem(z + k, NZ)})
    pl.semaphore_wait(bar, 4 + NZ - 1)


    def part(prefix, b):
        return getattr(R, prefix + b)

    def add_into(ref, *others):
        total = ref[...].astype(F32)
        for other in others:
            total = total + other.astype(F32)
        ref[...] = total.astype(BF)

    def column(kind):
        return (x, y) if kind == 0 else (1 - x, 1 - y)

    def z_up(b, kind, j):
        n, (cx, cy) = GRADS.index(b), column(kind)
        return remote(part("g_", b).at[cx, z + j, cy], part(("zr_", "zd_")[kind], b).at[z + j],
                      R.zs.at[n, kind, 0, j], R.zrs.at[n, kind, z + j], {"z": z + 1})

    def z_down(b, kind, j):
        n, (cx, cy) = GRADS.index(b), column(kind)
        slot = NZ if j == 1 else z - j
        return remote(part("g_", b).at[cx, z - j, cy], part(("zr_", "zd_")[kind], b).at[slot],
                      R.zs.at[n, kind, 1, j], R.zrs.at[n, kind, slot], {"z": z - 1})

    def z_landed(b, kind, slot):
        ref = part(("zr_", "zd_")[kind], b).at[slot]
        landed(ref, R.zrs.at[GRADS.index(b), kind, slot])
        return ref[...]

    def z_ends(b, kind):
        @pl.when(z == 0)
        def _():
            for j in range(NZ - 1, 0, -1):
                z_up(b, kind, j).start()

        @pl.when(z == NZ - 1)
        def _():
            for j in range(NZ - 1, 0, -1):
                z_down(b, kind, j).start()

    def z_pass(b, kind, upward):
        cx, cy = column(kind)
        for j in range(NZ - 2, 0, -1):
            if upward:

                @pl.when(down & (z + j < NZ))
                def _():
                    add_into(part("g_", b).at[cx, z + j, cy], z_landed(b, kind, z + j))
                    z_up(b, kind, j).start()

            else:

                @pl.when(up & (z - j >= 0))
                def _():
                    add_into(part("g_", b).at[cx, z - j, cy], z_landed(b, kind, z - j))
                    z_down(b, kind, j).start()

    def z_close(b, kind):
        cx, cy = column(kind)
        here = part("g_", b).at[cx, z, cy]
        pl.when(down)(lambda: add_into(here, z_landed(b, kind, z)))
        pl.when(up)(lambda: add_into(here, z_landed(b, kind, NZ)))

    def wide(b):
        n = GRADS.index(b)
        if CORNER[b] == "x":
            return remote(part("g_", b).at[1 - x, :, y], part("px_", b), R.s1.at[n, 0], R.rx.at[n, 0], xdev)
        return remote(part("g_", b).at[x, :, 1 - y], part("py_", b), R.s1.at[n, 0], R.ry.at[n, 0], ydev)

    def narrow(b, k):
        n, zk = GRADS.index(b), lax.rem(z + k, NZ)
        if CORNER[b] == "x":
            return remote(part("g_", b).at[x, zk, 1 - y], part("py_", b).at[zk], R.s1.at[n, 1 + k], R.ry.at[n, zk], ydev)
        return remote(part("g_", b).at[1 - x, zk, y], part("px_", b).at[zk], R.s1.at[n, 1 + k], R.rx.at[n, zk], xdev)

    def corner_share(b):
        n = GRADS.index(b)
        return remote(part("g_", b).at[1 - x, z, 1 - y], part("pd_", b), R.s1.at[n, 1 + NZ], R.rd.at[n],
                      xdev if CORNER[b] == "x" else ydev)

    def corner_first(b):
        wide(b).start()
        for k in range(1, NZ):
            narrow(b, k).start()
        z_ends(b, 1)

    def corner_out(b):
        z_close(b, 1)
        corner_share(b).start()

    def corner_in(b):
        corner_share(b).wait_recv()
        here = part("g_", b).at[x, z, 1 - y] if CORNER[b] == "x" else part("g_", b).at[1 - x, z, y]
        add_into(here, part("pd_", b)[...])
        narrow(b, 0).start()

    def corner_join(b):
        n = GRADS.index(b)
        px, py = part("px_", b), part("py_", b)
        wide(b).wait_recv()
        for k in range(NZ):
            if CORNER[b] == "x":
                landed(py.at[k], R.ry.at[n, k])
            else:
                landed(px.at[k], R.rx.at[n, k])

        @pl.loop(0, NZ)
        def _(k):
            add_into(part("g_", b).at[x, k, y], px[k], py[k])

        z_ends(b, 0)

    def split(b):
        return part("g_", b).shape[3] // 32 * 16

    def first(b):
        n, h, g = GRADS.index(b), split(b), part("g_", b)
        return (
            remote(g.at[1 - x, :, :, 0:h], part("px_", b), R.s1.at[n, 0], R.rx.at[n, 0], xdev),
            remote(g.at[:, :, 1 - y, h:], part("py_", b), R.s1.at[n, 1], R.ry.at[n, 0], ydev),
        )

    def second(b):
        n, h, g = GRADS.index(b), split(b), part("g_", b)
        return (
            remote(g.at[x, :, 1 - y, 0:h], part("qy_", b), R.s2.at[n, 0], R.r2s.at[n, 0], ydev),
            remote(g.at[1 - x, :, y, h:], part("qx_", b), R.s2.at[n, 1], R.r2s.at[n, 1], xdev),
        )

    def plane_first(b):
        for cp in first(b):
            cp.start()

    def plane_second(b):
        h, g = split(b), part("g_", b)
        px, py = part("px_", b), part("py_", b)
        for cp in first(b):
            cp.wait_recv()

        @pl.loop(0, NZ)
        def _(k):
            for yy in range(NY):
                add_into(g.at[x, k, yy, 0:h], px[k, yy])
            for xx in range(2):
                add_into(g.at[xx, k, y, h:], py[xx, k])

        for cp in second(b):
            cp.start()

    def plane_join(b):
        h, g = split(b), part("g_", b)
        qx, qy = part("qx_", b), part("qy_", b)
        for cp in second(b):
            cp.wait_recv()

        @pl.loop(0, NZ)
        def _(k):
            add_into(g.at[x, k, y, 0:h], qy[k])
            add_into(g.at[x, k, y, h:], qx[k])

        z_ends(b, 0)

    def stage_of(b):
        return R.st_ffn if b[:-1] in ("down", "up") else part("st_", b)

    def out_copy(b):
        dst = part("o_", b[:-1]).at[int(b[-1])] if b[:-1] in ("down", "up") else part("o_", b)
        return pltpu.make_async_copy(stage_of(b), dst, R.out_sem.at[GRADS.index(b)])

    ffn_done = []

    def finish(b):
        out = stage_of(b)
        if b[:-1] in ("down", "up"):
            if ffn_done:
                out_copy(ffn_done[-1]).wait()
            ffn_done.append(b)
        out[...] = part("g_", b)[x, z, y].astype(F32)

        @pl.when(down)
        def _():
            out[...] += z_landed(b, 0, z).astype(F32)

        @pl.when(up)
        def _():
            out[...] += z_landed(b, 0, NZ).astype(F32)

        out_copy(b).start()

    def sends_done(b):
        if b in CORNER:
            copies = [wide(b), corner_share(b)] + [narrow(b, k) for k in range(NZ)]
        else:
            copies = first(b) + second(b)
        for cp in copies:
            cp.wait_send()
        for kind in (0, 1) if b in CORNER else (0,):
            for j in range(1, NZ):
                pl.when(z + j < NZ)(lambda: z_up(b, kind, j).wait_send())
                pl.when(z - j >= 0)(lambda: z_down(b, kind, j).wait_send())
        if not (b[:-1] in ("down", "up") and b != ffn_done[-1]):
            out_copy(b).wait()


    def chip(core):
        return rows_at(core * half, half)

    def win(core):
        return rows_at(x * 128 + core * half, half)

    def swap(src, dst, n):
        return remote(src, dst, R.csend.at[n], R.crecv.at[n], cdev)

    def gain(layer, k):
        return R.vec[0, 14 + 2 * layer + k : 15 + 2 * layer + k, :]

    def note(row, value):
        R.small[row : row + 1, :] = value

    def norm_back(grad, g_row, hat, spread):
        scaled = grad * g_row
        first_mean = jnp.mean(scaled, 1, keepdims=True)
        second_mean = jnp.mean(scaled * hat, 1, keepdims=True)
        return spread * (scaled - first_mean - hat * second_mean)

    def ffn_norm(layer):
        need(layer, "yh2", "r2", "kp")
        grad, hat = R.dh[...], R.v_yh2[...].astype(F32)
        note(12 + 2 * layer + 1, jnp.sum(grad * hat, 0, keepdims=True))
        note(6 * layer + 5, jnp.sum(grad, 0, keepdims=True))
        dy = norm_back(grad, gain(layer, 1), hat, R.v_r2[...])
        R.dy[...] = dy
        df = dy * R.v_kp[1].astype(F32) * (1.0 / KEEP)
        note(6 * layer + 4, jnp.sum(df, 0, keepdims=True))
        R.dff[chip(c)] = df.astype(BF)
        here = R.dff.at[chip(c)]
        swap(here, here, 4 * layer).start()
        if layer == 1:
            load(0, "yh2", "r2")

    def ffn_wait(layer):
        here = R.dff.at[chip(c)]
        swap(here, here, 4 * layer).wait_send()
        landed(R.dff.at[chip(1 - c)], R.crecv.at[4 * layer])

    def as_block(value):
        return value.astype(BF).reshape(NZ, NY, -1, value.shape[1])

    def down_grad(layer, j):
        if j == 0:
            need(layer, "act")
        (R.g_down1 if layer else R.g_down0)[j] = as_block(contract(R.v_act[j], R.dff[...], 0, 0))
        if layer == 1 and j == 1:
            load(0, "act")

    def units_back(layer, j):
        if j == 0:
            need(layer, "gp")
            down_copy(layer).wait()
        total = jnp.zeros((1, width), F32)
        for core in range(2):
            rows = pl.ds(core * half, half)
            dact = contract(R.dff[rows], flat(R.w_down.at[j]), 1, 1)
            dhid = (dact * R.v_gp[j, rows].astype(F32)).astype(BF)
            R.v_gp[j, rows] = dhid
            total = total + jnp.sum(dhid.astype(F32), 0, keepdims=True)
        keep_row = jnp.where(c == 0, 1.0, 0.0)
        note(16 + 4 * layer + 2 * j, total * keep_row)
        note(16 + 4 * layer + 2 * j + 1, total * (1.0 - keep_row))
        if layer == 1 and j == 1:
            down_copy(0).start()

    def up_grad(layer, j):
        if j == 0:
            need(layer, "zf")
        (R.g_up1 if layer else R.g_up0)[j] = as_block(contract(R.v_zf[...], R.v_gp[j], 0, 0))
        if layer == 1 and j == 1:
            load(0, "zf")

    def mid_part(rows):
        return contract(R.v_gp[0, rows], flat(R.w_up.at[0]), 1, 1) + contract(R.v_gp[1, rows], flat(R.w_up.at[1]), 1, 1)

    def mid_give(layer):
        up_copy(layer).wait()
        R.send[...] = mid_part(chip(1 - c)).astype(BF)
        swap(R.send, R.rz, 4 * layer + 1).start()

    def mid_own(layer):
        R.dy[...] += mid_part(chip(c))

    def mid_norm(layer):
        need(layer, "yh1", "r1")
        swap(R.send, R.rz, 4 * layer + 1).wait()
        grad, hat = R.dy[...] + R.rz[...].astype(F32), R.v_yh1[...].astype(F32)
        note(12 + 2 * layer, jnp.sum(grad * hat, 0, keepdims=True))
        note(6 * layer + 3, jnp.sum(grad, 0, keepdims=True))
        dy = norm_back(grad, gain(layer, 0), hat, R.v_r1[...])
        R.dy[...] = dy
        da = dy * R.v_kp[0].astype(F32) * (1.0 / KEEP)
        note(6 * layer + 2, jnp.sum(da, 0, keepdims=True))
        R.daf[chip(c)] = da.astype(BF)
        here = R.daf.at[chip(c)]
        swap(here, here, 4 * layer + 2).start()
        if layer == 1:
            load(0, "yh1", "r1", "kp")

    def free_ffn(layer):
        up_copy(0).start()
        load(0, "gp")

    def proj_rows_back(layer):
        if layer == 1:
            proj_copy().wait()
        for j in range(2):
            value = R.w_proj[j].astype(F32)
            rows = value.shape[2] // 2
            value = value[:, :, layer * rows : (layer + 1) * rows].reshape(-1, value.shape[3])
            R.wo[j] = value.astype(BF)

    def proj_wait(layer):
        here = R.daf.at[chip(c)]
        swap(here, here, 4 * layer + 2).wait_send()
        landed(R.daf.at[chip(1 - c)], R.crecv.at[4 * layer + 2])

    def proj_back(layer):
        for j in range(2):
            for core in range(2):
                rows = pl.ds(core * half, half)
                R.datt[j, rows] = contract(R.daf[rows], R.wo[j], 1, 1).astype(BF)

    def proj_grad(layer):
        need(layer, "att")
        for j in range(2):
            grad = contract(R.v_att[j], R.daf[...], 0, 0)
            if layer == 1:
                R.dwo[j] = grad.astype(BF)
            else:
                both = [v.reshape(NZ * NY, -1, width) for v in (grad, R.dwo[j].astype(F32))]
                R.g_proj[j] = as_block(jnp.concatenate(both, 1).reshape(-1, width))
        if layer == 1:
            load(0, "att")

    def attend_back(layer, j):
        if j == 0:
            need(layer, "p", "q", "k", "v")
        lane = lax.broadcasted_iota(jnp.int32, (1, head), 1) // HEAD_DIM
        picks = [(lane == n).astype(F32) for n in range(head // HEAD_DIM)]
        count = len(picks)
        R.dk[...] = jnp.zeros_like(R.dk)
        R.dv[...] = jnp.zeros_like(R.dv)
        R.dq[...] = jnp.zeros_like(R.dq)

        @pl.loop(0, 4)
        def _(i):
            keys = rows_at((3 * (x + i) + 1) // 5 * 128, 384)
            mine = rows_at(i * 128, 128)
            kk = R.v_k[j, keys]
            qq, dd = R.v_q[j, mine], R.datt[j, mine]
            q3 = jnp.concatenate([qq * pick.astype(BF) for pick in picks], 0)
            d3 = jnp.concatenate([dd * pick.astype(BF) for pick in picks], 0)
            p3 = R.v_p[j, i]
            dp = contract(d3, R.v_v[j, keys], 1, 1)
            pf = p3.astype(F32)
            ds = (pf * (dp - jnp.sum(pf * dp, 1, keepdims=True))).astype(BF)
            R.dv[keys] += contract(p3, d3, 0, 0)
            R.dk[keys] += contract(ds, q3, 0, 0)
            dq = mm(ds, kk)
            total = dq[0:128] * picks[0]
            for n in range(1, count):
                total = total + dq[n * 128 : (n + 1) * 128] * picks[n]
            R.dq[rows_at(x * 128 + i * 128, 128)] = total * 0.125

        dq, dk, dv = (v[...].astype(BF).astype(F32) for v in (R.dq, R.dk, R.dv))
        R.dqk[j] = jnp.concatenate([dq, dk], 1).astype(BF)
        gap = jnp.zeros((dv.shape[0], 64), F32)
        R.dvp[j] = jnp.concatenate([dv, gap] if layer == 0 else [gap, dv], 1).astype(BF)
        own = jnp.where(c == 0, 1.0, 0.0)
        for row, value in ((0, dq), (1, dv)):
            line = jnp.sum(value, 0, keepdims=True)
            pair = [line * own, line * (1.0 - own)]
            zero = jnp.zeros((1, 2 * head), F32)
            if j == 0:
                note(6 * layer + row, jnp.concatenate(pair + [zero], 1))
            else:
                R.small[6 * layer + row : 6 * layer + row + 1, :] += jnp.concatenate([zero] + pair, 1)
        if layer == 1 and j == 1:
            load(0, "p", "q", "k", "v")

    def qkv_grad(layer, j):
        if j == 0:
            need(layer, "xw")
        gqk = as_block(contract(R.v_xw[...], R.dqk[j], 0, 0))
        gv = as_block(contract(R.v_xw[...], R.dvp[j], 0, 0))
        if layer == 1:
            R.g_qk1[j] = gqk
            R.g_last[j, :, :, :, 3 * head - 64 :] = gv
        else:
            R.g_last[j, :, :, :, 0 : 2 * head] = gqk
            R.g_last[j, :, :, :, 2 * head : 2 * head + 128] = gv[..., 0:128]
            R.g_last[j, :, :, :, 2 * head + 128 : 3 * head + 64] += gv[..., 128:]
        if layer == 1 and j == 1:
            load(0, "xw")

    def in_part(rows):
        total = None
        for j in range(2):
            w = R.w_qkv.at[j]
            wqk = w[:, :, :, 0 : 2 * head].reshape(width, 2 * head)
            wv = w[:, :, :, 2 * head :].reshape(width, head + 64)
            term = contract(R.dqk[j, rows], wqk, 1, 1) + contract(R.dvp[j, rows], wv, 1, 1)
            total = term if total is None else total + term
        return total

    def halo_copy(layer):
        return remote(R.hs, R.hr.at[layer, c], R.hsend.at[layer], R.hrecv.at[layer, c], {"x": 1 - x, "c": x})

    def in_halo(layer):
        for cp in qkv_copies(layer):
            cp.wait()
        R.hs[...] = in_part(rows_at((1 - x) * 512, 128)).astype(BF)
        halo_copy(layer).start()

    def in_give(layer):
        R.send[...] = in_part(win(1 - c)).astype(BF)
        swap(R.send, R.rh, 4 * layer + 3).start()

    def in_own(layer):
        R.dh[...] = R.dy[...] + in_part(win(c))
        if layer == 1:
            for again in qkv_copies(0):
                again.start()

    def in_sum(layer):
        swap(R.send, R.rh, 4 * layer + 3).wait()
        R.dh[...] += R.rh[...].astype(F32)

        @pl.when(c == 1 - x)
        def _():
            edge = rows_at(128 * c, 128)
            for core in range(2):
                landed(R.hr.at[layer, core], R.hrecv.at[layer, core])
                R.dh[edge] += R.hr[layer, core].astype(F32)

        halo_copy(layer).wait_send()
        if layer == 0:
            gx_copy.start()


    def small_copy(k):
        dev = (cdev, xdev, ydev, {"z": zp1}, {"z": zp2})[k]
        return remote(R.small, R.small_in.at[k], R.bs.at[k], R.br.at[k], dev)

    def small_sum(k):
        small_copy(k).wait()
        R.small[...] += R.small_in[k]


    total = R.seg.shape[1]
    number = lax.broadcasted_iota(jnp.int32, (SEGS, total), 0)
    before = (jnp.broadcast_to(R.seg[...], (SEGS, total)) < number).astype(F32)
    starts = jnp.sum(before, 1, keepdims=True).astype(jnp.int32)
    mine = lax.broadcasted_iota(jnp.int32, (SEGS, half), 1) + (2 * x + c) * half
    pick = (mine == starts).astype(F32)
    R.dh[...] = lax.dot_general(
        pick, R.gcls[...], (((0,), (0,)), ((), ())), precision=lax.Precision.HIGHEST, preferred_element_type=F32)

    gx_copy = pltpu.make_async_copy(R.dh, R.gx, R.gx_sem)
    layered = {
        "fn": ffn_norm, "fw": ffn_wait, "dga": lambda n: down_grad(n, 0), "dgb": lambda n: down_grad(n, 1),
        "dha": lambda n: units_back(n, 0), "dhb": lambda n: units_back(n, 1),
        "uga": lambda n: up_grad(n, 0), "ugb": lambda n: up_grad(n, 1),
        "mida": mid_give, "midb": mid_own, "midc": mid_norm, "free": free_ffn,
        "pr": proj_rows_back, "aw": proj_wait, "pd": proj_back, "pg": proj_grad,
        "aba": lambda n: attend_back(n, 0), "abb": lambda n: attend_back(n, 1),
        "qga": lambda n: qkv_grad(n, 0), "qgb": lambda n: qkv_grad(n, 1),
        "inh": in_halo, "ina": in_give, "inb": in_own, "inc": in_sum,
        "sm": lambda k: small_copy(k).start(), "sw": small_sum,
    }
    sums = {
        "E0": corner_first, "E1u": lambda b: z_pass(b, 1, True), "E1d": lambda b: z_pass(b, 1, False),
        "E2": corner_out, "E3": corner_in, "E4": corner_join,
        "S1": plane_first, "S2": plane_second, "S3": plane_join,
        "E5u": lambda b: z_pass(b, 0, True), "E5d": lambda b: z_pass(b, 0, False), "E6": finish,
    }
    for step in BACKWARD_ORDER:
        if "." in step:
            block, kind = step.split(".")
            sums[kind](block)
        else:
            layered[step[:-1]](int(step[-1]))
    R.o_small[...] = R.small[...]
    gx_copy.wait()
    for b in GRADS:
        sends_done(b)


def saved_shapes(half, width):
    head = width // 4
    return {
        "xw": ((640, width), BF),
        "q": ((2, 512, head), BF),
        "k": ((2, 640, head), BF),
        "v": ((2, 640, head), BF),
        "p": ((2, 4, 384, 384), BF),
        "att": ((2, 512, head), BF),
        "zf": ((512, width), BF),
        "gp": ((2, 512, width), BF),
        "act": ((2, 512, width), BF),
        "yh1": ((half, width), BF),
        "yh2": ((half, width), BF),
        "r1": ((half, 1), F32),
        "r2": ((half, 1), F32),
        "kp": ((2, half, width), BF),
    }


def run_forward(blocks, pool, tok, seg, drop):
    half, width = tok.shape
    saved = saved_shapes(half, width)
    head = width // 4
    dma = pltpu.SemaphoreType.DMA
    land = [(2, NZ, NY, *b.shape) for b in blocks]
    nb = len(blocks)
    shape = jax.ShapeDtypeStruct
    outs = [shape(s, BF) for s in land[1:]]
    outs += [
        shape((NZ, NY, *pool.shape), BF),
        shape((NZ, NY, *blocks[0].shape), BF),
        shape((2, 32, width), F32),
        shape((NZ, NY, SEGS, width), BF),
    ]
    outs += [shape((2, *s), t) for s, t in saved.values()]
    out_specs = [VMEM if n == "o_cls" else ANY for n in FWD_OUT]
    scratch = [pltpu.VMEM(s, BF) for s in land]
    scratch += [
        pltpu.VMEM((NZ, NY, *pool.shape), BF),
        pltpu.VMEM((4, SEGS, width), BF),
        pltpu.VMEM((NZ, NY, SEGS, width), BF),
    ]
    scratch += [pltpu.VMEM((2, *s), t) for s, t in saved.values()]
    scratch += [
        pltpu.VMEM(drop.shape, drop.dtype),
        pltpu.VMEM((4, 128, 384), F32),
        pltpu.VMEM((2, 2, head, width), BF),
        pltpu.VMEM((2, 32, width), F32),
        pltpu.VMEM((2, 32, head), F32),
        pltpu.VMEM((half, width), F32),
        pltpu.VMEM((half, width), F32),
    ]
    scratch += [pltpu.VMEM((2, half, width), BF)] * 4
    scratch += [
        dma((nb, 4 * NZ)), dma((nb, 2 * NZ)), dma((nb, 2 * NZ)), dma((nb, 2, NZ, NY)), dma((nb,)),
        dma((3 * NZ,)), dma((NZ, NY)), dma, dma((2,)),
        dma((8,)), dma((8,)), dma((2, 2)), dma((2,)), dma, dma((len(SAVED), 2)), dma((nb,)), dma((3,)),
        dma((3,)), dma((3,)), dma((NZ * NY,)), dma((NZ * NY,)),
    ]
    return pl.pallas_call(
        forward_kernel,
        out_shape=outs,
        in_specs=[ANY] * (nb + 1) + [VMEM, VMEM, ANY],
        out_specs=out_specs,
        scratch_shapes=scratch,
        compiler_params=pltpu.CompilerParams(collective_id=1, has_side_effects=True, vmem_limit_bytes=60 << 20),
        name="forward",
    )(*blocks, pool, tok, seg, drop)


def run_backward(weights, saved, vec, seg, gcls):
    width = vec.shape[2]
    half = saved[SAVED.index("yh1")].shape[1]
    head = width // 4
    dma = pltpu.SemaphoreType.DMA
    by_name = dict(zip(BLOCKS[1:], weights))
    rows, wide = by_name["up0"].shape[3:]
    thin = by_name["proj"].shape[3]
    cut = {n: (rows, wide) for n in GRADS}
    cut["proj"] = (thin, width)
    cut["qk1"] = (rows, 2 * head)
    cut["last"] = (rows, 4 * head)
    nb = len(GRADS)
    shape = jax.ShapeDtypeStruct
    outs = [
        shape((half, width), F32),
        shape((2, rows, wide), F32),
        shape((2, rows, wide), F32),
        shape(cut["proj"], F32),
        shape(cut["qk1"], F32),
        shape(cut["last"], F32),
        shape((24, width), F32),
    ]

    def low(*dims):
        return pltpu.VMEM(dims, BF)

    def full(*dims):
        return pltpu.VMEM(dims, F32)

    scratch = [low(2, NZ, NY, *cut[n]) for n in GRADS]
    scratch += [low(NZ + 1, *cut[n]) for n in GRADS]
    split = {n: cut[n][0] // 32 * 16 for n in GRADS}
    for n in GRADS:
        r, w = cut[n]
        scratch.append(low(NZ, r, w) if n in CORNER else low(NZ, NY, split[n], w))
    for n in GRADS:
        r, w = cut[n]
        scratch.append(low(NZ, r, w) if n in CORNER else low(2, NZ, r - split[n], w))
    for n in GRADS:
        r, w = cut[n]
        if n in CORNER:
            scratch += [low(r, w), low(NZ + 1, r, w)]
        else:
            scratch += [low(NZ, r - split[n], w), low(NZ, split[n], w)]
    scratch += [full(rows, wide), full(*cut["proj"]), full(*cut["qk1"]), full(*cut["last"])]
    scratch += [pltpu.VMEM(s, t) for s, t in saved_shapes(half, width).values()]
    scratch += [
        low(2, NZ, NY, rows, 3 * head + 64),
        low(*by_name["proj"].shape),
        low(*by_name["up0"].shape),
        low(*by_name["down0"].shape),
        low(2, head, width),
        low(512, width),
        low(512, width),
        low(half, width),
        low(half, width),
        low(half, width),
        low(128, width),
        low(2, 2, 128, width),
        low(2, 512, head),
        full(640, head),
        full(640, head),
        full(640, head),
        low(2, 640, 2 * head),
        low(2, 640, head + 64),
        low(2, head, width),
        full(half, width),
        full(half, width),
        full(24, width),
        full(5, 24, width),
    ]
    scratch += [
        dma((5,)), dma((len(SAVED),)), dma((nb,)), dma((8,)), dma((8,)), dma((2,)), dma((2, 2)),
        dma((nb, NZ + 2)), dma((nb, NZ)), dma((nb, NZ)), dma((nb,)), dma((nb, 2)), dma((nb, 2)),
        dma((nb, 2, 2, NZ)), dma((nb, 2, NZ + 1)), dma((5,)), dma((5,)), dma,
    ]
    return pl.pallas_call(
        backward_kernel,
        out_shape=outs,
        in_specs=[ANY] * (len(weights) + len(saved)) + [VMEM] * 3,
        out_specs=[ANY] * 6 + [VMEM],
        scratch_shapes=scratch,
        compiler_params=pltpu.CompilerParams(collective_id=2, has_side_effects=True, vmem_limit_bytes=63 << 20),
        name="backward",
    )(*weights, *saved, vec, seg, gcls)


def per_device(tokens_in, segments, pairing, drop_masks, w_qkv, w_out, w_in, w_back, b_in, biases,
               gains, pool_w, pool_b):
    inner = lax.axis_size("g")
    layers = w_qkv.shape[0]
    width = tokens_in.shape[1]
    z, y, x, c = position()
    m = 2 * x + c
    dp = (z * NY + y) * inner + lax.axis_index("g")

    def group(arr, dim):
        return arr if inner == 1 else lax.all_gather(arr, "g", axis=dim, tiled=True)

    w_qkv, w_out, w_in, w_back = group(w_qkv, 2), group(w_out, 1), group(w_in, 1), group(w_back, 1)
    b_in, biases, gains = group(b_in, 1), group(biases, 2), group(gains, 2)
    pool_w, pool_b, pairing = group(pool_w, 0), group(pool_b, 0), group(pairing, 0)
    rows = w_in.shape[1]

    def wide(values):
        values = values.reshape(-1, values.shape[-1])
        return jnp.pad(values, ((0, 0), (0, 128 - values.shape[1])))

    small = jnp.concatenate([
        wide(b_in), wide(biases), wide(gains), wide(pool_b),
        wide((pairing // 32).astype(BF)), wide((pairing % 32).astype(BF))], 0)
    small = jnp.pad(small, ((0, 32 - small.shape[0]), (0, 0)))
    qkv = jnp.concatenate([w_qkv[0, 0], w_qkv[0, 1], w_qkv[1, 0], w_qkv[1, 1], w_qkv[0, 2], w_qkv[1, 2]], 1)
    proj = w_out.reshape(-1, width)
    blocks = [small, qkv, proj, w_in[0], w_back[0], w_in[1], w_back[1]]
    res = run_forward(blocks, pool_w, tokens_in, segments, drop_masks)
    named = dict(zip(FWD_OUT, res))
    cls = named["o_cls"].reshape(NZ * NY, SEGS, width)
    if inner > 1:
        cls = lax.all_gather(cls, "g", axis=1, tiled=True)
    cls = cls.reshape(-1, width)
    loss, align, unif, grad_pool_w, grad_pool_b, gcls = pooled_loss(cls, named["o_pool"], named["o_vec"], named["o_piece"])
    weights = [named["o_" + n] for n in BLOCKS[1:]]
    saved = [named["o_" + n] for n in SAVED]
    grad_x, down, up, proj, qk1, last, sums = run_backward(weights, saved, named["o_vec"], segments, gcls)

    def spread(values, dim):
        return values if inner == 1 else lax.psum_scatter(values, "g", scatter_dimension=dim, tiled=True)

    part = w_qkv.shape[3]
    low = [last[:, k * part : (k + 1) * part] for k in range(4)]
    out_qkv = jnp.stack([jnp.stack(low[:3]), jnp.stack([qk1[:, :part], qk1[:, part:], low[3]])])
    if inner > 1:
        sums = lax.psum(sums, "g")
    thin = rows // (4 * inner)
    here = lax.dynamic_slice_in_dim(sums[:16], dp * 4 * thin + m * thin, thin, 1)
    up_sums = sums[16:24].reshape(layers, 4 * width)
    n_up = rows // inner
    out_b_in = lax.dynamic_slice_in_dim(up_sums, m * width + dp * n_up, n_up, 1)
    n_pool = pool_w.shape[0] // inner
    g = lax.axis_index("g")
    if inner > 1:
        grad_pool_w = lax.dynamic_slice_in_dim(grad_pool_w, g * n_pool, n_pool, 0)
    grad_pool_b = lax.dynamic_slice_in_dim(grad_pool_b[0], dp * n_pool, n_pool, 0)
    return (
        loss[:, 0],
        align[:, 0],
        unif[:, 0],
        grad_x,
        spread(out_qkv, 2),
        spread(proj.reshape(layers, -1, width), 1),
        spread(up, 1),
        spread(down, 1),
        out_b_in,
        here[:12].reshape(layers, 6, thin),
        here[12:].reshape(layers, 2, thin),
        grad_pool_w,
        grad_pool_b,
    )


def solution(mesh):
    count = mesh.shape["dp"]
    fine = Mesh(
        mesh.devices.reshape(NZ, NY, count // (NZ * NY), 2, 2), ("z", "y", "g", "x", "c")
    )
    dp, mp = ("z", "y", "g"), ("x", "c")
    in_specs = (
        P(dp + mp, None),
        P(dp, None),
        P(dp),
        P(None, None, dp + mp, None),
        P(None, None, dp, mp),
        P(None, mp + dp, None),
        P(None, dp, mp),
        P(None, mp + dp, None),
        P(None, mp + dp),
        P(None, None, dp),
        P(None, None, dp),
        P(dp, None),
        P(dp),
    )
    out_specs = (
        P(dp),
        P(dp),
        P(dp),
        P(dp + mp, None),
        P(None, None, dp, mp),
        P(None, mp + dp, None),
        P(None, dp, mp),
        P(None, mp + dp, None),
        P(None, mp + dp),
        P(None, None, dp + mp),
        P(None, None, dp + mp),
        P(dp, None),
        P(dp),
    )
    return jax.shard_map(
        per_device, mesh=fine, in_specs=in_specs, out_specs=out_specs, check_vma=False
    )
```

```python
import functools
from typing import NamedTuple

import jax
import jax.numpy as jnp
from jax import lax
from jax.experimental import pallas as pl
from jax.experimental.pallas import tpu as pltpu
from jax.sharding import Mesh
from jax.sharding import PartitionSpec as P

HEAD_DIM = 64
SEGS = 16
TEMP = 0.05
EPS = 1e-06
KEEP = 0.9
MESH = pl.DeviceIdType.MESH
ANY = pl.BlockSpec(memory_space=pl.ANY)
VMEM = pl.BlockSpec(memory_space=pltpu.VMEM)
BF = jnp.bfloat16
F32 = jnp.float32
NZ = 4
NY = 2


class Names:
    def __init__(self, names, refs):
        for name, ref in zip(names, refs, strict=True):
            setattr(self, name, ref)


def contract(left_side, right_side, left_dim, right_dim):
    return lax.dot_general(
        left_side,
        right_side,
        (((left_dim,), (right_dim,)), ((), ())),
        preferred_element_type=F32,
    )


def mm(a, b):
    return jnp.dot(a, b, preferred_element_type=F32)


def position():
    return tuple(lax.axis_index(name) for name in ("z", "y", "x", "c"))


def signal(sem, device):
    pl.semaphore_signal(sem, inc=1, device_id=device, device_id_type=MESH)


def remote(src, dst, send_sem, recv_sem, device):
    return pltpu.make_async_remote_copy(
        src_ref=src,
        dst_ref=dst,
        send_sem=send_sem,
        recv_sem=recv_sem,
        device_id=device,
        device_id_type=MESH,
    )


def landed(ref, sem):
    pltpu.make_async_copy(ref, ref, sem).wait()


def rows_at(start, count):
    return pl.ds(pl.multiple_of(start, 128), count)


def flat(ref):
    value = ref[...]
    return value.reshape(-1, value.shape[-1])


class ForwardArgs(NamedTuple):
    wqkv: object
    wout: object
    up: object
    down: object
    b_in: object
    biases: object
    gains: object
    pool_b: object
    pairing: object
    pool: object
    tok: object
    seg: object
    drop: object


class ForwardScratch(NamedTuple):
    keep: object
    bias: object
    wo: object
    vec: object
    qv: object
    h: object
    z: object
    sa: object
    ra: object
    sf: object
    rf: object
    zsend: object
    xsend: object
    ysend: object
    recv: object
    own_sem: object
    pool_send: object
    pool_recv: object
    pool_own: object
    pool_core: object
    core_send: object
    core_recv: object
    halo_send: object
    halo_recv: object
    drop_sem: object
    out_sem: object
    w_sem: object
    misc_sem: object
    s1: object
    r1s: object
    s2: object
    r2s: object
    wide: object
    sm: object
    sq: object
    sp: object
    cls: object


SMALL, QKV, PROJ, UP0, DOWN0, UP1, DOWN1 = range(7)
BLOCKS = ("small", "qkv", "proj", "up0", "down0", "up1", "down1")
SAVED = ("xw", "q", "k", "v", "p", "att", "zf", "gp", "act", "yh1", "yh2", "r1", "r2", "kp")
FWD_IN = ForwardArgs._fields
LOSS_OUT = ("loss", "align", "unif", "gw", "gb", "gcls")
LOSS_SCR = ("u", "nb", "rn", "dn", "dpre", "table", "gw_all")


def forward_out(whole):
    after = LOSS_OUT if whole else ("o_pool", "o_piece", "o_cls")
    return tuple("o_" + n for n in BLOCKS[1:]) + ("o_vec",) + after + tuple("o_" + n for n in SAVED)


FWD_SCR = (
    tuple("w_" + n for n in BLOCKS) + ("w_pool", "cls_part", "cls_all") + SAVED
    + ForwardScratch._fields
)


FORWARD_ORDER = (
    2, 6, 0, 5, 43, 73, 3, 14, 1, 15, 32, 35, 16, 46, 44, 33, 20, 23, 51, 37, 39, 36, 4, 47, 17, 34, 52, 54,
    18, 45, 58, 24, 55, 19, 38, 67, 64, 25, 59, 40, 56, 53, 48, 68, 21, 7, 60, 57, 41, 69, 70, 22, 49, 74, 42,
    61, 62, 26, 71, 8, 29, 77, 78, 79, 27, 80, 9, 81, 75, 28, 82, 30, 10, 50, 83, 63, 31, 84, 85, 11, 86, 65,
    87, 13, 88, 89, 72, 66, 90, 91, 12, 92, 93, 94, 95, 96, 97, 98, 76,
)


def forward_kernel(whole, *refs):
    R = Names(FWD_IN + forward_out(whole) + FWD_SCR + (LOSS_SCR if whole else ()), refs)
    z, y, x, c = position()
    up, down = z < NZ - 1, z > 0
    xdev, ydev, cdev, xcdev = {"x": 1 - x}, {"y": 1 - y}, {"c": 1 - c}, {"x": 1 - x, "c": 1 - c}
    half = R.tok.shape[0]
    ins = [R.sm, R.sq, R.sp, R.up.at[0], R.down.at[0], R.up.at[1], R.down.at[1]]
    lands = [getattr(R, "w_" + n) for n in BLOCKS]

    peers = [(k * NY + flip, k, flip) for k in range(NZ) for flip in range(NY) if k or flip]

    def peer(k, flip):
        return {"z": lax.rem(z + k, NZ), "y": y if flip == 0 else 1 - y}

    R.wide[...] = jnp.zeros_like(R.wide)
    n = R.b_in.shape[1]
    row = 0
    for value in (R.b_in[...], R.biases[0], R.biases[1], R.gains[0], R.gains[1], R.pool_b[...]):
        R.wide[row : row + value.shape[0], 0:n] = value.astype(F32)
        row += value.shape[0]
    pair = R.pairing[...]
    R.wide[row : row + 1, 0 : pair.shape[1]] = (pair // 32).astype(F32)
    R.wide[row + 1 : row + 2, 0 : pair.shape[1]] = lax.rem(pair, 32).astype(F32)
    R.sm[...] = R.wide[...].astype(BF)
    parts = [R.wqkv[layer, k].astype(F32) for layer, k in ((0, 0), (0, 1), (1, 0), (1, 1), (0, 2), (1, 2))]
    R.sq[...] = jnp.concatenate(parts, 1).astype(BF)
    R.sp[...] = jnp.concatenate([R.wout[0].astype(F32), R.wout[1].astype(F32)], 0).astype(BF)

    bar = pltpu.get_barrier_semaphore()
    for dev in (xdev, cdev, xcdev):
        signal(bar, dev)
    for _, k, flip in peers:
        signal(bar, peer(k, flip))
    pl.semaphore_wait(bar, 3 + len(peers))


    def copy(b, src, slot, device, sem):
        return remote(src, lands[b].at[slot], sem, R.recv.at[(b, *slot)], device)

    def arrived(b, slot):
        landed(lands[b].at[slot], R.recv.at[(b, *slot)])

    def by_z(b):
        return b in (PROJ, UP0, DOWN0, UP1)

    def over_y(b):
        return b in (SMALL, UP0, UP1, DOWN1)

    def sideways(b, src, slot, k):
        copy(b, src, slot, xdev, R.xsend.at[b, k]).start()
        copy(b, src, slot, ydev, R.ysend.at[b, k]).start()

    def launch(b):
        src, mine = ins[b], (x, z, y)
        pl.when(up)(lambda: copy(b, src, mine, {"z": z + 1}, R.zsend.at[b, 0]).start())
        pl.when(down)(lambda: copy(b, src, mine, {"z": z - 1}, R.zsend.at[b, 1]).start())
        sideways(b, src, mine, 0)
        pltpu.make_async_copy(src, lands[b].at[mine], R.own_sem.at[b]).start()

    def z_relay(b, d):
        @pl.when(z >= d)
        def _():
            slot = (x, z - d, y)
            arrived(b, slot)
            pl.when(up)(lambda: copy(b, lands[b].at[slot], slot, {"z": z + 1}, R.zsend.at[b, 2 * d]).start())
            sideways(b, lands[b].at[slot], slot, NZ - d)

        @pl.when(z < NZ - d)
        def _():
            slot = (x, z + d, y)
            arrived(b, slot)
            pl.when(down)(lambda: copy(b, lands[b].at[slot], slot, {"z": z - 1}, R.zsend.at[b, 2 * d + 1]).start())
            sideways(b, lands[b].at[slot], slot, d)

    def xy_relay(b, k):
        zp = lax.rem(z + k, NZ)
        sx, sy = (1 - x, zp, y), (x, zp, 1 - y)
        if over_y(b):
            arrived(b, sx)
            copy(b, lands[b].at[sx], sx, ydev, R.ysend.at[b, NZ + k]).start()
        else:
            arrived(b, sy)
            copy(b, lands[b].at[sy], sy, xdev, R.xsend.at[b, NZ + k]).start()

    def corner_launch(b):
        slot = (1 - x, z, 1 - y)
        arrived(b, slot)
        pl.when(up)(lambda: copy(b, lands[b].at[slot], slot, {"z": z + 1}, R.zsend.at[b, 2 * NZ]).start())
        pl.when(down)(lambda: copy(b, lands[b].at[slot], slot, {"z": z - 1}, R.zsend.at[b, 2 * NZ + 1]).start())

    def corner_relay(b, d):
        @pl.when(z >= d)
        def _():
            slot = (1 - x, z - d, 1 - y)
            arrived(b, slot)
            pl.when(up)(lambda: copy(b, lands[b].at[slot], slot, {"z": z + 1}, R.zsend.at[b, 2 * NZ + 2 * d]).start())

        @pl.when(z < NZ - d)
        def _():
            slot = (1 - x, z + d, 1 - y)
            arrived(b, slot)
            pl.when(down)(lambda: copy(b, lands[b].at[slot], slot, {"z": z - 1}, R.zsend.at[b, 2 * NZ + 2 * d + 1]).start())

    def complete(b):
        relays = 1 if by_z(b) else NZ
        for k in range(NZ):
            zp = lax.rem(z + k, NZ)
            if k >= relays or not over_y(b):
                arrived(b, (1 - x, zp, y))
            if k >= relays or over_y(b):
                arrived(b, (x, zp, 1 - y))
            if not by_z(b):
                arrived(b, (1 - x, zp, 1 - y))
        pltpu.make_async_copy(ins[b], lands[b].at[x, z, y], R.own_sem.at[b]).wait()
        if b != SMALL:
            w_copy(b).start()

    def sends_done(b):
        src, mine = ins[b], (x, z, y)
        for k in range(NZ):
            copy(b, src, mine, xdev, R.xsend.at[b, k]).wait_send()
            copy(b, src, mine, ydev, R.ysend.at[b, k]).wait_send()
        for k in range(1 if by_z(b) else NZ):
            if over_y(b):
                copy(b, src, mine, ydev, R.ysend.at[b, NZ + k]).wait_send()
            else:
                copy(b, src, mine, xdev, R.xsend.at[b, NZ + k]).wait_send()
        for d in range(NZ):
            for base in (0, 2 * NZ) if by_z(b) else (0,):
                pl.when(up & (z >= d))(lambda: copy(b, src, mine, {"z": z + 1}, R.zsend.at[b, base + 2 * d]).wait_send())
                pl.when(down & (z < NZ - d))(lambda: copy(b, src, mine, {"z": z - 1}, R.zsend.at[b, base + 2 * d + 1]).wait_send())

    prow = R.pool.shape[0] // 2
    pool_rows = pl.ds(pl.multiple_of(c * prow, 16), prow)

    def pool_slot(zp, yp):
        return R.w_pool.at[zp, yp, pool_rows]

    def pool_copy(src, zp, yp, device, k):
        return remote(src, pool_slot(zp, yp), R.pool_send.at[k], R.pool_recv.at[zp, yp], device)

    def pool_launch():
        src = R.pool.at[pool_rows]
        pl.when(up)(lambda: pool_copy(src, z, y, {"z": z + 1}, 0).start())
        pl.when(down)(lambda: pool_copy(src, z, y, {"z": z - 1}, 1).start())
        pool_copy(src, z, y, ydev, 2 * NZ).start()
        pltpu.make_async_copy(src, pool_slot(z, y), R.pool_own).start()

    def pool_relay(d):
        @pl.when(z >= d)
        def _():
            here = pool_slot(z - d, y)
            landed(here, R.pool_recv.at[z - d, y])
            pl.when(up)(lambda: pool_copy(here, z - d, y, {"z": z + 1}, 2 * d).start())
            pool_copy(here, z - d, y, ydev, 2 * NZ + NZ - d).start()

        @pl.when(z < NZ - d)
        def _():
            here = pool_slot(z + d, y)
            landed(here, R.pool_recv.at[z + d, y])
            pl.when(down)(lambda: pool_copy(here, z + d, y, {"z": z - 1}, 2 * d + 1).start())
            pool_copy(here, z + d, y, ydev, 2 * NZ + d).start()

    def pool_core():
        halves = R.w_pool.at[:, :, pool_rows]
        return remote(halves, halves, R.pool_core.at[0], R.pool_core.at[1], cdev)

    def pool_swap():
        pltpu.make_async_copy(R.pool.at[pool_rows], pool_slot(z, y), R.pool_own).wait()
        for k in range(NZ):
            zp = lax.rem(z + k, NZ)
            landed(pool_slot(zp, 1 - y), R.pool_recv.at[zp, 1 - y])
        pool_core().start()

    def pool_done():
        there = R.w_pool.at[:, :, pl.ds(pl.multiple_of((1 - c) * prow, 16), prow)]
        landed(there, R.pool_core.at[1])
        pool_core().wait_send()
        src = R.pool.at[pool_rows]
        for d in range(NZ):
            pl.when(up & (z >= d))(lambda: pool_copy(src, z, y, {"z": z + 1}, 2 * d).wait_send())
            pl.when(down & (z < NZ - d))(lambda: pool_copy(src, z, y, {"z": z - 1}, 2 * d + 1).wait_send())
            pool_copy(src, z, y, ydev, 2 * NZ + d).wait_send()
        for cp in misc_copies():
            cp.start()


    def win(core):
        return rows_at(x * 128 + core * half, half)

    def chip(core):
        return rows_at(core * half, half)

    def swap(src, dst, n):
        return remote(src, dst, R.core_send.at[n], R.core_recv.at[n], cdev)

    def rows_swap(layer):
        here = R.xw.at[layer, win(c)]
        return swap(here, here, 4 * layer)

    def edge_copies(layer):
        src = R.xw.at[layer, rows_at(x * 128 + c * half + 128 * c, 128)]
        dst = R.xw.at[layer, rows_at(x * 512, 128)]
        return [
            remote(src, dst, R.halo_send.at[layer, i], R.halo_recv.at[layer], dev)
            for i, dev in enumerate(({"x": 1 - x, "c": c}, {"x": 1 - x, "c": 1 - c}))
        ]

    def send_rows(layer):
        rows_swap(layer).start()

        @pl.when(c == 1 - x)
        def _():
            for cp in edge_copies(layer):
                cp.start()

    def partner_rows_here(layer):
        landed(R.xw.at[layer, win(1 - c)], R.core_recv.at[4 * layer])

    def edge_here(layer):
        landed(R.xw.at[layer, rows_at((1 - x) * 512, 128)], R.halo_recv.at[layer])


    def vec(layer, k):
        return R.vec[0, 2 + 6 * layer + k : 3 + 6 * layer + k, :]

    def gain(layer, k):
        return R.vec[0, 14 + 2 * layer + k : 15 + 2 * layer + k, :]

    def spread_params():
        width = R.vec.shape[2]
        part = width // (NZ * NY)
        lane = lax.broadcasted_iota(jnp.int32, (128, width), 0)
        col = lax.broadcasted_iota(jnp.int32, (128, width), 1)
        for j in range(2):
            total = jnp.zeros((R.vec.shape[1], width), F32)
            for dp in range(NZ * NY):
                place = ((lane < part) & (col == lane + dp * part)).astype(F32).astype(BF)
                total = total + mm(R.w_small[j, dp // NY, dp % NY], place)
            R.vec[j] = total
        head = R.qv.shape[2]
        lane = lax.broadcasted_iota(jnp.int32, (width, head), 0)
        col = lax.broadcasted_iota(jnp.int32, (width, head), 1)
        low = R.vec[0].astype(BF)
        for j in range(2):
            place = (lane == col + (2 * j + c) * head).astype(F32).astype(BF)
            R.qv[j] = mm(low, place)

    def masks():
        for i in range(4):
            mine = R.seg[0:1, rows_at(x * 512 + i * 128, 128)]
            start = (3 * (x + i) + 1) // 5 * 128
            keys = R.seg[0:1, rows_at(x * 384 + start, 384)]
            column = jnp.transpose(jnp.broadcast_to(mine, (128, 128)))
            for t in range(3):
                same = column == jnp.broadcast_to(keys[:, t * 128 : t * 128 + 128], (128, 128))
                R.bias[i, :, t * 128 : t * 128 + 128] = jnp.where(same, 0.0, -1000000000.0)

    def proj_rows():
        for layer in range(2):
            for j in range(2):
                value = R.w_proj[j].astype(F32)
                rows = value.shape[2] // 2
                value = value[:, :, layer * rows : (layer + 1) * rows].reshape(-1, value.shape[3])
                R.wo[layer, j] = value.astype(BF)

    def project(layer, wrow, count, crow):
        xx = R.xw[layer, wrow]
        head = R.q.shape[3]
        for j in range(2):
            w = R.w_qkv.at[j]
            wqk = w[:, :, :, layer * 2 * head : (layer + 1) * 2 * head].reshape(-1, 2 * head)
            yqk = mm(xx, wqk)
            if crow is not None:
                bq = R.qv[j, 2 + 6 * layer : 3 + 6 * layer, :]
                R.q[layer, j, crow] = (yqk[:, :head] + bq).astype(BF) * jnp.asarray(0.125, BF)
            R.k[layer, j, wrow] = yqk[:, head:].astype(BF)
            bv = R.qv[j, 3 + 6 * layer : 4 + 6 * layer, :]
            if layer == 0:
                yv = mm(xx, w[:, :, :, 4 * head : 5 * head].reshape(-1, head))
            else:
                yv = mm(xx, w[:, :, :, 5 * head - 64 : 6 * head].reshape(-1, head + 64))[:, 64:]
            R.v[layer, j, wrow] = (yv + bv).astype(BF)

    def attend(layer, j):
        head = R.q.shape[3]
        lane = lax.broadcasted_iota(jnp.int32, (1, head), 1) // HEAD_DIM
        picks = [(lane == n).astype(F32) for n in range(head // HEAD_DIM)]
        count = len(picks)

        @pl.loop(0, 4)
        def _(i):
            keys = rows_at((3 * (x + i) + 1) // 5 * 128, 384)
            mine = rows_at(i * 128, 128)
            qq = R.q[layer, j, mine]
            q3 = jnp.concatenate([qq * pick.astype(BF) for pick in picks], 0)
            scores = contract(q3, R.k[layer, j, keys], 1, 1)
            bias = R.bias[i]
            scores = scores.reshape(count, 128, 384) + bias[None]
            peak = jnp.max(scores, -1, keepdims=True)
            e = jnp.exp(scores - peak)
            p = (e * (1.0 / jnp.sum(e, -1, keepdims=True))).astype(BF).reshape(count * 128, 384)
            R.p[layer, j, i] = p
            o = mm(p, R.v[layer, j, keys])
            total = o[0:128] * picks[0]
            for n in range(1, count):
                total = total + o[n * 128 : (n + 1) * 128] * picks[n]
            R.att[layer, j, mine] = total.astype(BF)

        if j == 1:
            save(layer, "p", "att")

    def proj_part(layer, rows):
        return mm(R.att[layer, 0, rows], R.wo[layer, 0]) + mm(R.att[layer, 1, rows], R.wo[layer, 1])

    def norm(value, g, s):
        center = jnp.mean(value, 1, keepdims=True)
        spread = lax.rsqrt(jnp.mean(value * value, 1, keepdims=True) - center * center + EPS)
        hat = (value - center) * spread
        return hat * g + s, hat, spread

    def attention_give(layer):
        R.sa[layer] = proj_part(layer, chip(1 - c)).astype(BF)
        swap(R.sa.at[layer], R.ra.at[layer], 4 * layer + 1).start()

    def attention_out(layer):
        if layer == 0:
            drop.wait()
            for n in range(2):
                for k in range(2):
                    R.kp[n, k] = R.keep[n, k].astype(F32).astype(BF)
                save(n, "kp")
        a = proj_part(layer, chip(c))
        swap(R.sa.at[layer], R.ra.at[layer], 4 * layer + 1).wait_recv()
        a = a + R.ra[layer].astype(F32) + vec(layer, 2)
        out, hat, spread = norm(R.h[...] + R.kp[layer, 0].astype(F32) * a * (1.0 / KEEP), gain(layer, 0), vec(layer, 3))
        R.z[...] = out
        R.yh1[layer] = hat.astype(BF)
        R.r1[layer] = spread
        R.zf[layer, chip(c)] = out.astype(BF)
        here = R.zf.at[layer, chip(c)]
        swap(here, here, 4 * layer + 2).start()
        save(layer, "yh1", "r1")

    def ffn_up(layer, own):
        if not own:
            landed(R.zf.at[layer, chip(1 - c)], R.core_recv.at[4 * layer + 2])
        rows = chip(c if own else 1 - c)
        w = R.w_up0 if layer == 0 else R.w_up1
        zz = R.zf[layer, rows]
        for j in range(2):
            hid = mm(zz, flat(w.at[j])) + R.vec[j, layer : layer + 1, :]
            cdf = 0.5 + 0.5 * lax.erf(hid * 0.7071067811865476)
            R.act[layer, j, rows] = (hid * cdf).astype(BF)
            R.gp[layer, j, rows] = (cdf + hid * jnp.exp(-0.5 * hid * hid) * 0.3989422804014327).astype(BF)
        if not own:
            save(layer, "zf", "gp", "act")

    def ffn_part(layer, rows):
        w = R.w_down0 if layer == 0 else R.w_down1
        return mm(R.act[layer, 0, rows], flat(w.at[0])) + mm(R.act[layer, 1, rows], flat(w.at[1]))

    def ffn_give(layer):
        R.sf[layer] = ffn_part(layer, chip(1 - c)).astype(BF)
        swap(R.sf.at[layer], R.rf.at[layer], 4 * layer + 3).start()

    def ffn_down(layer):
        f = ffn_part(layer, chip(c))
        swap(R.sf.at[layer], R.rf.at[layer], 4 * layer + 3).wait_recv()
        f = f + R.rf[layer].astype(F32) + vec(layer, 4)
        out, hat, spread = norm(R.z[...] + R.kp[layer, 1].astype(F32) * f * (1.0 / KEEP), gain(layer, 1), vec(layer, 5))
        R.h[...] = out
        R.yh2[layer] = hat.astype(BF)
        R.r2[layer] = spread
        if layer == 0:
            R.xw[1, win(c)] = out.astype(BF)
            send_rows(1)
        save(layer, "yh2", "r2")

    def project_part(layer, part):
        if part == 0:
            project(layer, win(c), half, chip(c))
        elif part == 1:
            partner_rows_here(layer)
            project(layer, win(1 - c), half, chip(1 - c))
        else:
            edge_here(layer)
            project(layer, rows_at((1 - x) * 512, 128), 128, None)
            save(layer, "xw", "q", "k", "v")


    def out_copy(k, layer):
        name = SAVED[k]
        return pltpu.make_async_copy(getattr(R, name).at[layer], getattr(R, "o_" + name).at[layer], R.out_sem.at[k, layer])

    def save(layer, *names):
        for name in names:
            out_copy(SAVED.index(name), layer).start()

    def w_copy(b):
        return pltpu.make_async_copy(lands[b], getattr(R, "o_" + BLOCKS[b]), R.w_sem.at[b])

    def misc_copies():
        copies = [pltpu.make_async_copy(R.vec, R.o_vec, R.misc_sem.at[0])]
        if not whole:
            copies.append(pltpu.make_async_copy(R.w_pool, R.o_pool, R.misc_sem.at[1]))
            copies.append(pltpu.make_async_copy(R.w_small.at[0], R.o_piece, R.misc_sem.at[2]))
        return copies


    def pooled():
        total = R.seg.shape[1]
        number = lax.broadcasted_iota(jnp.int32, (SEGS, total), 0)
        before = (jnp.broadcast_to(R.seg[...], (SEGS, total)) < number).astype(F32)
        starts = jnp.sum(before, 1, keepdims=True).astype(jnp.int32)
        mine = lax.broadcasted_iota(jnp.int32, (SEGS, half), 1) + (2 * x + c) * half
        pick = (mine == starts).astype(F32).astype(BF)
        row = mm(pick, R.h[...].astype(BF))
        R.cls_part[0] = row.astype(BF)
        first = [
            remote(R.cls_part.at[0], R.cls_part.at[1 + i], R.s1.at[i], R.r1s.at[i], dev)
            for i, dev in enumerate((xdev, cdev, xcdev))
        ]
        for cp in first:
            cp.start()
        for i, cp in enumerate(first):
            cp.wait_recv()
            row = row + R.cls_part[1 + i].astype(F32)
        here = R.cls_all.at[z, y]
        here[...] = row.astype(BF)
        second = [remote(here, here, R.s2.at[i], R.r2s.at[i], peer(k, flip)) for i, k, flip in peers]
        for cp in second:
            cp.start()
        for i, k, flip in peers:
            landed(R.cls_all.at[lax.rem(z + NZ - k, NZ), y if flip == 0 else 1 - y], R.r2s.at[i])
        if whole:
            R.cls[...] = R.cls_all[...].reshape(R.cls.shape)
            work_out_loss(R.cls, R.w_pool, R.vec, R.w_small.at[0], *[getattr(R, n) for n in LOSS_OUT + LOSS_SCR])
        else:
            R.o_cls[...] = R.cls_all[...]
        for cp in first + second:
            cp.wait_send()


    R.xw[0, win(c)] = R.tok[...]
    send_rows(0)
    drop = pltpu.make_async_copy(R.drop, R.keep, R.drop_sem)
    drop.start()
    R.h[...] = R.tok[...].astype(F32)
    def act(fn, *args):
        actions.append(functools.partial(fn, *args))

    actions = []
    every = range(len(BLOCKS))
    along = [b for b in every if by_z(b)]
    for b in every:
        act(launch, b)
    for b in every:
        act(complete, b)
    for b in every:
        for d in range(1, NZ):
            act(z_relay, b, d)
    for b in every:
        for k in range(1 if by_z(b) else NZ):
            act(xy_relay, b, k)
    for b in along:
        act(corner_launch, b)
    for b in along:
        for d in range(1, NZ):
            act(corner_relay, b, d)
    act(pool_launch)
    for d in range(1, NZ):
        act(pool_relay, d)
    for fn in (pool_swap, pool_done, masks, spread_params, proj_rows, pooled):
        act(fn)
    for layer in range(2):
        for k in range(3):
            act(project_part, layer, k)
        for j in range(2):
            act(attend, layer, j)
        act(attention_give, layer)
        act(attention_out, layer)
        act(ffn_up, layer, True)
        act(ffn_up, layer, False)
        act(ffn_give, layer)
        act(ffn_down, layer)
    for step in FORWARD_ORDER:
        actions[step]()

    for b in range(len(BLOCKS)):
        sends_done(b)
        if b != SMALL:
            w_copy(b).wait()
    for cp in misc_copies():
        cp.wait()
    for layer in range(2):
        for k in range(len(SAVED)):
            out_copy(k, layer).wait()
        rows_swap(layer).wait_send()
        swap(R.sa.at[layer], R.ra.at[layer], 4 * layer + 1).wait_send()
        swap(R.zf.at[layer, chip(c)], R.zf.at[layer, chip(c)], 4 * layer + 2).wait_send()
        swap(R.sf.at[layer], R.rf.at[layer], 4 * layer + 3).wait_send()

        @pl.when(c == 1 - x)
        def _():
            for cp in edge_copies(layer):
                cp.wait_send()


def work_out_loss(cls, pool, vec, piece, loss, align, unif, gw, gb, gcls, u, nb, rn, dn, dpre, table, gw_all):
    z, y = lax.axis_index("z"), lax.axis_index("y")
    inner = lax.axis_size("g")
    count, width = cls.shape
    per = SEGS * inner
    pre = mm(cls[...], pool[...].reshape(width, width)) + vec[0, 18:19, :]
    value = jnp.tanh(pre)
    u[...] = value
    scale = lax.rsqrt(jnp.sum(value * value, 1, keepdims=True) + EPS)
    rn[...] = scale
    nb[...] = (value * scale).astype(BF)
    low = nb[...].astype(F32)
    squares_row = lax.dot_general(
        jnp.ones((8, width), F32), low * low, (((1,), (1,)), ((), ())),
        precision=lax.Precision.HIGHEST, preferred_element_type=F32)[0:1]
    dn[...] = jnp.zeros_like(dn)

    @pl.loop(0, count // 128)
    def _(blk):
        rows = rows_at(blk * 128, 128)
        ids = lax.broadcasted_iota(jnp.int32, (128, 1), 0) + blk * 128
        cols = lax.broadcasted_iota(jnp.int32, (1, count), 1)
        pair = jnp.zeros((128, 1), F32)
        lane = lax.broadcasted_iota(jnp.int32, (1, 128), 1)
        for o in range(NZ * NY):
            got = piece[o // NY, o % NY]
            number = got[19:20].astype(F32) * 32.0 + got[20:21].astype(F32)
            here = (ids == o * per + lane) & (lane < per)
            pair = pair + jnp.sum(jnp.where(here, number, 0.0), 1, keepdims=True)
        mine = nb[rows]
        gram = contract(mine, nb[...], 1, 1)
        logits = gram * (1.0 / TEMP)
        own = cols == ids
        twin = cols == pair.astype(jnp.int32)
        masked = jnp.where(own, -1000000000.0, logits)
        peak = jnp.max(masked, 1, keepdims=True)
        e = jnp.exp(masked - peak)
        total = jnp.sum(e, 1, keepdims=True)
        low_mine = mine.astype(F32)
        squares = jnp.sum(low_mine * low_mine, 1, keepdims=True)
        distance = squares + squares_row - 2.0 * gram
        terms = (
            peak + jnp.log(total) - jnp.sum(jnp.where(twin, logits, 0.0), 1, keepdims=True),
            jnp.sum(jnp.where(twin, distance, 0.0), 1, keepdims=True),
            jnp.log(jnp.sum(jnp.where(own, 0.0, jnp.exp(-2.0 * distance)), 1, keepdims=True) * (1.0 / (count - 1))),
        )
        for t in range(3):
            table[t, rows] = jnp.broadcast_to(terms[t], (128, 128))
        dg = ((e * (1.0 / total) - jnp.where(twin, 1.0, 0.0)) * (1.0 / TEMP)).astype(BF)
        dn[rows] += mm(dg, nb[...])
        dn[...] += contract(dg, mine, 0, 0)

    grad = dn[...]
    value = u[...]
    unit = value * rn[...]
    du = rn[...] * (grad - unit * jnp.sum(grad * unit, 1, keepdims=True))
    dpre[...] = (du * (1.0 - value * value)).astype(BF)
    dp = (z * NY + y) * inner + lax.axis_index("g")
    mine = pl.ds(pl.multiple_of(dp * SEGS, SEGS), SEGS)
    gcls[...] = contract(dpre[mine], pool[...].reshape(width, width), 1, 1)
    thin = gb.shape[1]
    columns = jnp.sum(dpre[...].astype(F32), 0, keepdims=True)
    gb[...] = pltpu.roll(jnp.broadcast_to(columns, (8, width)), lax.rem(width - dp * thin, width), 1)[0:1, 0:thin]
    gw_all[...] = contract(cls[...], dpre[...], 0, 0)
    part = gw.shape[0]
    gw[...] = gw_all[pl.ds(pl.multiple_of((z * NY + y) * part, 8), part)]
    for t, ref in enumerate((loss, align, unif)):
        lines = [jnp.transpose(table[t, n * 128 : (n + 1) * 128])[0:8] for n in range(count // 128)]
        line = jnp.concatenate(lines, 1)
        ref[...] = pltpu.roll(line, lax.rem(count - dp * SEGS, count), 1)[0:1, 0:SEGS]


def loss_shapes(count, width):
    one = jax.ShapeDtypeStruct((1, SEGS), F32)
    outs = [
        one, one, one,
        jax.ShapeDtypeStruct((width // (NZ * NY), width), F32),
        jax.ShapeDtypeStruct((1, width * SEGS // count), F32),
        jax.ShapeDtypeStruct((SEGS, width), F32),
    ]
    scratch = [
        pltpu.VMEM((count, width), F32),
        pltpu.VMEM((count, width), BF),
        pltpu.VMEM((count, 1), F32),
        pltpu.VMEM((count, width), F32),
        pltpu.VMEM((count, width), BF),
        pltpu.VMEM((3, count, 128), F32),
        pltpu.VMEM((width, width), F32),
    ]
    return outs, scratch


def pooled_loss(cls, pool, vec, piece):
    outs, scratch = loss_shapes(*cls.shape)
    return pl.pallas_call(
        work_out_loss,
        out_shape=outs,
        in_specs=[VMEM] * 4,
        out_specs=[VMEM] * 6,
        scratch_shapes=scratch,
        compiler_params=pltpu.CompilerParams(vmem_limit_bytes=48 << 20),
        name="pooled_loss",
    )(cls, pool, vec, piece)


class BackwardScratch(NamedTuple):
    w_qkv: object
    w_proj: object
    w_up: object
    w_down: object
    wo: object
    dff: object
    daf: object
    send: object
    rz: object
    rh: object
    hs: object
    hr: object
    datt: object
    dq: object
    dk: object
    dv: object
    dqk: object
    dvp: object
    dwo: object
    dh: object
    dy: object
    small: object
    small_in: object
    w_sem: object
    v_sem: object
    out_sem: object
    csend: object
    crecv: object
    hsend: object
    hrecv: object
    s1: object
    rx: object
    ry: object
    rd: object
    s2: object
    r2s: object
    zs: object
    zrs: object
    bs: object
    br: object
    gx_sem: object


GRADS = ("down1", "up1", "qk1", "down0", "up0", "proj", "last")
CORNER = {"down1": "x", "up1": "y", "down0": "x"}
BWD_IN = BLOCKS[1:] + SAVED + ("vec", "seg", "gcls")
BWD_OUT = ("gx", "o_down", "o_up", "o_proj", "o_qkv", "o_small")
BWD_SCR = (
    tuple("g_" + n for n in GRADS) + tuple("zr_" + n for n in GRADS)
    + tuple("px_" + n for n in GRADS) + tuple("py_" + n for n in GRADS)
    + tuple(t + n for n in GRADS for t in (("pd_", "zd_") if n in CORNER else ("qx_", "qy_")))
    + ("st_ffn", "st_proj", "st_qkv") + tuple("v_" + n for n in SAVED)
    + BackwardScratch._fields
)
BACKWARD_ORDER = (
    23, 34, 24, 25, 26, 57, 27, 28, 31, 32, 33, 35, 29, 30, 62, 36, 38, 39, 42, 40, 58, 41, 43, 67, 44, 45, 0,
    11, 63, 37, 1, 2, 59, 3, 71, 46, 4, 68, 5, 8, 64, 60, 6, 9, 10, 12, 7, 76, 69, 13, 15, 72, 65, 16, 73, 17,
    77, 74, 18, 84, 14, 78, 47, 52, 48, 85, 80, 86, 81, 66, 19, 20, 75, 53, 49, 82, 54, 50, 70, 79, 21, 22,
    55, 87, 51, 61, 83, 56,
)


def backward_kernel(*refs):
    R = Names(BWD_IN + BWD_OUT + BWD_SCR, refs)
    z, y, x, c = position()
    up, down = z < NZ - 1, z > 0
    xdev, ydev, cdev = {"x": 1 - x}, {"y": 1 - y}, {"c": 1 - c}
    half = R.gx.shape[0]
    head = R.q.shape[3]
    width = R.gx.shape[1]


    def v_copy(name, layer):
        k = SAVED.index(name)
        return pltpu.make_async_copy(getattr(R, name).at[layer], getattr(R, "v_" + name), R.v_sem.at[k])

    def load(layer, *names):
        for name in names:
            v_copy(name, layer).start()

    def need(layer, *names):
        for name in names:
            v_copy(name, layer).wait()

    def qkv_copies(layer):
        src, dst = R.qkv, R.w_qkv
        low = 4 * head if layer == 0 else 5 * head - 64
        return [
            pltpu.make_async_copy(src.at[:, :, :, :, layer * 2 * head : (layer + 1) * 2 * head],
                                  dst.at[:, :, :, :, 0 : 2 * head], R.w_sem.at[0]),
            pltpu.make_async_copy(src.at[:, :, :, :, low : low + head + 64],
                                  dst.at[:, :, :, :, 2 * head : 3 * head + 64], R.w_sem.at[1]),
        ]

    def up_copy(layer):
        return pltpu.make_async_copy(R.up0 if layer == 0 else R.up1, R.w_up, R.w_sem.at[2])

    def down_copy(layer):
        return pltpu.make_async_copy(R.down0 if layer == 0 else R.down1, R.w_down, R.w_sem.at[3])

    def proj_copy():
        return pltpu.make_async_copy(R.proj, R.w_proj, R.w_sem.at[4])

    load(1, "yh2", "r2", "kp", "act")
    down_copy(1).start()
    load(1, "gp", "zf")
    up_copy(1).start()
    load(1, "yh1", "r1", "att")
    proj_copy().start()
    load(1, "p", "q", "k", "v", "xw")
    for cp in qkv_copies(1):
        cp.start()

    zp1 = z + 1 - 2 * lax.rem(z, 2)
    zp2 = lax.rem(z + 2, NZ)
    bar = pltpu.get_barrier_semaphore()
    for dev in (xdev, ydev, cdev, {"x": 1 - x, "c": 1 - c}):
        signal(bar, dev)
    for k in range(1, NZ):
        signal(bar, {"z": lax.rem(z + k, NZ)})
    pl.semaphore_wait(bar, 4 + NZ - 1)


    def part(prefix, b):
        return getattr(R, prefix + b)

    def add_into(ref, *others):
        total = ref[...].astype(F32)
        for other in others:
            total = total + other.astype(F32)
        ref[...] = total.astype(BF)

    def column(kind):
        return (x, y) if kind == 0 else (1 - x, 1 - y)

    def z_copy(b, kind, k):
        n, (cx, cy), zt = GRADS.index(b), column(kind), lax.rem(z + k, NZ)
        return remote(part("g_", b).at[cx, zt, cy], part(("zr_", "zd_")[kind], b).at[k - 1],
                      R.zs.at[n, kind, k - 1], R.zrs.at[n, kind, k - 1], {"z": zt})

    def z_start(b, kind):
        for k in range(1, NZ):
            z_copy(b, kind, k).start()

    def z_landed(b, kind):
        ref = part(("zr_", "zd_")[kind], b)
        for k in range(NZ - 1):
            landed(ref.at[k], R.zrs.at[GRADS.index(b), kind, k])
        return [ref[k] for k in range(NZ - 1)]

    def wide(b):
        n = GRADS.index(b)
        if CORNER[b] == "x":
            return remote(part("g_", b).at[1 - x, :, y], part("px_", b), R.s1.at[n, 0], R.rx.at[n, 0], xdev)
        return remote(part("g_", b).at[x, :, 1 - y], part("py_", b), R.s1.at[n, 0], R.ry.at[n, 0], ydev)

    def narrow(b, k):
        n, zk = GRADS.index(b), lax.rem(z + k, NZ)
        if CORNER[b] == "x":
            return remote(part("g_", b).at[x, zk, 1 - y], part("py_", b).at[zk], R.s1.at[n, 1 + k], R.ry.at[n, zk], ydev)
        return remote(part("g_", b).at[1 - x, zk, y], part("px_", b).at[zk], R.s1.at[n, 1 + k], R.rx.at[n, zk], xdev)

    def corner_share(b):
        n = GRADS.index(b)
        return remote(part("g_", b).at[1 - x, z, 1 - y], part("pd_", b), R.s1.at[n, 1 + NZ], R.rd.at[n],
                      xdev if CORNER[b] == "x" else ydev)

    def corner_first(b):
        wide(b).start()
        for k in range(1, NZ):
            narrow(b, k).start()
        z_start(b, 1)

    def corner_out(b):
        add_into(part("g_", b).at[1 - x, z, 1 - y], *z_landed(b, 1))
        corner_share(b).start()

    def corner_in(b):
        corner_share(b).wait_recv()
        here = part("g_", b).at[x, z, 1 - y] if CORNER[b] == "x" else part("g_", b).at[1 - x, z, y]
        add_into(here, part("pd_", b)[...])
        narrow(b, 0).start()

    def corner_join(b):
        n = GRADS.index(b)
        px, py = part("px_", b), part("py_", b)
        wide(b).wait_recv()
        for k in range(NZ):
            if CORNER[b] == "x":
                landed(py.at[k], R.ry.at[n, k])
            else:
                landed(px.at[k], R.rx.at[n, k])

        @pl.loop(0, NZ)
        def _(k):
            add_into(part("g_", b).at[x, k, y], px[k], py[k])

        z_start(b, 0)

    def split(b):
        return part("g_", b).shape[3] // 48 * 16

    def first(b):
        n, h, g = GRADS.index(b), split(b), part("g_", b)
        return (
            remote(g.at[1 - x, :, :, 0:h], part("px_", b), R.s1.at[n, 0], R.rx.at[n, 0], xdev),
            remote(g.at[:, :, 1 - y, h:], part("py_", b), R.s1.at[n, 1], R.ry.at[n, 0], ydev),
        )

    def second(b):
        n, h, g = GRADS.index(b), split(b), part("g_", b)
        return (
            remote(g.at[x, :, 1 - y, 0:h], part("qy_", b), R.s2.at[n, 0], R.r2s.at[n, 0], ydev),
            remote(g.at[1 - x, :, y, h:], part("qx_", b), R.s2.at[n, 1], R.r2s.at[n, 1], xdev),
        )

    def plane_first(b):
        for cp in first(b):
            cp.start()

    def plane_second(b):
        h, g = split(b), part("g_", b)
        px, py = part("px_", b), part("py_", b)
        for cp in first(b):
            cp.wait_recv()

        @pl.loop(0, NZ)
        def _(k):
            for yy in range(NY):
                add_into(g.at[x, k, yy, 0:h], px[k, yy])
            for xx in range(2):
                add_into(g.at[xx, k, y, h:], py[xx, k])

        for cp in second(b):
            cp.start()

    def plane_join(b):
        h, g = split(b), part("g_", b)
        qx, qy = part("qx_", b), part("qy_", b)
        for cp in second(b):
            cp.wait_recv()

        @pl.loop(0, NZ)
        def _(k):
            add_into(g.at[x, k, y, 0:h], qy[k])
            add_into(g.at[x, k, y, h:], qx[k])

        z_start(b, 0)

    def out_copies(b):
        sem = R.out_sem.at[GRADS.index(b)]
        if b[:-1] in ("down", "up"):
            return [pltpu.make_async_copy(R.st_ffn, part("o_", b[:-1]).at[int(b[-1])], sem.at[0])]
        if b == "proj":
            rows = R.o_proj.shape[1]
            return [pltpu.make_async_copy(R.st_proj.at[n * rows : (n + 1) * rows], R.o_proj.at[n], sem.at[n]) for n in range(2)]
        places = ((1, 0), (1, 1)) if b == "qk1" else ((0, 0), (0, 1), (0, 2), (1, 2))
        return [pltpu.make_async_copy(R.st_qkv.at[p], R.o_qkv.at[p], sem.at[k]) for k, p in enumerate(places)]

    ffn_done = []

    def finish(b):
        if b[:-1] in ("down", "up"):
            if ffn_done:
                for cp in out_copies(ffn_done[-1]):
                    cp.wait()
            ffn_done.append(b)
        total = part("g_", b)[x, z, y].astype(F32)
        for other in z_landed(b, 0):
            total = total + other.astype(F32)
        if b[:-1] in ("down", "up"):
            R.st_ffn[...] = total
        elif b == "proj":
            R.st_proj[...] = total
        else:
            places = ((1, 0), (1, 1)) if b == "qk1" else ((0, 0), (0, 1), (0, 2), (1, 2))
            for k, p in enumerate(places):
                R.st_qkv[p] = total[:, k * head : (k + 1) * head]
        for cp in out_copies(b):
            cp.start()

    def sends_done(b):
        if b in CORNER:
            copies = [wide(b), corner_share(b)] + [narrow(b, k) for k in range(NZ)]
        else:
            copies = first(b) + second(b)
        for cp in copies:
            cp.wait_send()
        for kind in (0, 1) if b in CORNER else (0,):
            for k in range(1, NZ):
                z_copy(b, kind, k).wait_send()
        if not (b[:-1] in ("down", "up") and b != ffn_done[-1]):
            for cp in out_copies(b):
                cp.wait()


    def chip(core):
        return rows_at(core * half, half)

    def win(core):
        return rows_at(x * 128 + core * half, half)

    def swap(src, dst, n):
        return remote(src, dst, R.csend.at[n], R.crecv.at[n], cdev)

    def gain(layer, k):
        return R.vec[0, 14 + 2 * layer + k : 15 + 2 * layer + k, :]

    def note(row, value):
        R.small[row : row + 1, :] = value

    def norm_back(grad, g_row, hat, spread):
        scaled = grad * g_row
        first_mean = jnp.mean(scaled, 1, keepdims=True)
        second_mean = jnp.mean(scaled * hat, 1, keepdims=True)
        return spread * (scaled - first_mean - hat * second_mean)

    def ffn_norm(layer):
        need(layer, "yh2", "r2", "kp")
        grad, hat = R.dh[...], R.v_yh2[...].astype(F32)
        note(12 + 2 * layer + 1, jnp.sum(grad * hat, 0, keepdims=True))
        note(6 * layer + 5, jnp.sum(grad, 0, keepdims=True))
        dy = norm_back(grad, gain(layer, 1), hat, R.v_r2[...])
        R.dy[...] = dy
        df = dy * R.v_kp[1].astype(F32) * (1.0 / KEEP)
        note(6 * layer + 4, jnp.sum(df, 0, keepdims=True))
        R.dff[chip(c)] = df.astype(BF)
        here = R.dff.at[chip(c)]
        swap(here, here, 4 * layer).start()
        if layer == 1:
            load(0, "yh2", "r2")

    def ffn_wait(layer):
        here = R.dff.at[chip(c)]
        swap(here, here, 4 * layer).wait_send()
        landed(R.dff.at[chip(1 - c)], R.crecv.at[4 * layer])

    def as_block(value):
        return value.astype(BF).reshape(NZ, NY, -1, value.shape[1])

    def down_grad(layer, j):
        if j == 0:
            need(layer, "act")
        (R.g_down1 if layer else R.g_down0)[j] = as_block(contract(R.v_act[j], R.dff[...], 0, 0))
        if layer == 1 and j == 1:
            load(0, "act")

    def units_back(layer, j):
        if j == 0:
            need(layer, "gp")
            down_copy(layer).wait()
        total = jnp.zeros((1, width), F32)
        for core in range(2):
            rows = pl.ds(core * half, half)
            dact = contract(R.dff[rows], flat(R.w_down.at[j]), 1, 1)
            dhid = (dact * R.v_gp[j, rows].astype(F32)).astype(BF)
            R.v_gp[j, rows] = dhid
            total = total + jnp.sum(dhid.astype(F32), 0, keepdims=True)
        keep_row = jnp.where(c == 0, 1.0, 0.0)
        note(16 + 4 * layer + 2 * j, total * keep_row)
        note(16 + 4 * layer + 2 * j + 1, total * (1.0 - keep_row))
        if layer == 1 and j == 1:
            down_copy(0).start()

    def up_grad(layer, j):
        if j == 0:
            need(layer, "zf")
        (R.g_up1 if layer else R.g_up0)[j] = as_block(contract(R.v_zf[...], R.v_gp[j], 0, 0))
        if layer == 1 and j == 1:
            load(0, "zf")

    def mid_part(rows):
        return contract(R.v_gp[0, rows], flat(R.w_up.at[0]), 1, 1) + contract(R.v_gp[1, rows], flat(R.w_up.at[1]), 1, 1)

    def mid_give(layer):
        up_copy(layer).wait()
        R.send[...] = mid_part(chip(1 - c)).astype(BF)
        swap(R.send, R.rz, 4 * layer + 1).start()

    def mid_own(layer):
        R.dy[...] += mid_part(chip(c))

    def mid_norm(layer):
        need(layer, "yh1", "r1")
        swap(R.send, R.rz, 4 * layer + 1).wait()
        grad, hat = R.dy[...] + R.rz[...].astype(F32), R.v_yh1[...].astype(F32)
        note(12 + 2 * layer, jnp.sum(grad * hat, 0, keepdims=True))
        note(6 * layer + 3, jnp.sum(grad, 0, keepdims=True))
        dy = norm_back(grad, gain(layer, 0), hat, R.v_r1[...])
        R.dy[...] = dy
        da = dy * R.v_kp[0].astype(F32) * (1.0 / KEEP)
        note(6 * layer + 2, jnp.sum(da, 0, keepdims=True))
        R.daf[chip(c)] = da.astype(BF)
        here = R.daf.at[chip(c)]
        swap(here, here, 4 * layer + 2).start()
        if layer == 1:
            load(0, "yh1", "r1", "kp")

    def free_ffn(layer):
        up_copy(0).start()
        load(0, "gp")

    def proj_rows_back(layer):
        if layer == 1:
            proj_copy().wait()
        for j in range(2):
            value = R.w_proj[j].astype(F32)
            rows = value.shape[2] // 2
            value = value[:, :, layer * rows : (layer + 1) * rows].reshape(-1, value.shape[3])
            R.wo[j] = value.astype(BF)

    def proj_wait(layer):
        here = R.daf.at[chip(c)]
        swap(here, here, 4 * layer + 2).wait_send()
        landed(R.daf.at[chip(1 - c)], R.crecv.at[4 * layer + 2])

    def proj_back(layer):
        for j in range(2):
            for core in range(2):
                rows = pl.ds(core * half, half)
                R.datt[j, rows] = contract(R.daf[rows], R.wo[j], 1, 1).astype(BF)

    def proj_grad(layer):
        need(layer, "att")
        for j in range(2):
            grad = contract(R.v_att[j], R.daf[...], 0, 0)
            if layer == 1:
                R.dwo[j] = grad.astype(BF)
            else:
                both = [v.reshape(NZ * NY, -1, width) for v in (grad, R.dwo[j].astype(F32))]
                R.g_proj[j] = as_block(jnp.concatenate(both, 1).reshape(-1, width))
        if layer == 1:
            load(0, "att")

    def attend_back(layer, j):
        if j == 0:
            need(layer, "p", "q", "k", "v")
        lane = lax.broadcasted_iota(jnp.int32, (1, head), 1) // HEAD_DIM
        picks = [(lane == n).astype(F32) for n in range(head // HEAD_DIM)]
        count = len(picks)
        R.dk[...] = jnp.zeros_like(R.dk)
        R.dv[...] = jnp.zeros_like(R.dv)
        R.dq[...] = jnp.zeros_like(R.dq)

        @pl.loop(0, 4)
        def _(i):
            keys = rows_at((3 * (x + i) + 1) // 5 * 128, 384)
            mine = rows_at(i * 128, 128)
            kk = R.v_k[j, keys]
            qq, dd = R.v_q[j, mine], R.datt[j, mine]
            q3 = jnp.concatenate([qq * pick.astype(BF) for pick in picks], 0)
            d3 = jnp.concatenate([dd * pick.astype(BF) for pick in picks], 0)
            p3 = R.v_p[j, i]
            dp = contract(d3, R.v_v[j, keys], 1, 1)
            pf = p3.astype(F32)
            ds = (pf * (dp - jnp.sum(pf * dp, 1, keepdims=True))).astype(BF)
            R.dv[keys] += contract(p3, d3, 0, 0)
            R.dk[keys] += contract(ds, q3, 0, 0)
            dq = mm(ds, kk)
            total = dq[0:128] * picks[0]
            for n in range(1, count):
                total = total + dq[n * 128 : (n + 1) * 128] * picks[n]
            R.dq[rows_at(x * 128 + i * 128, 128)] = total * 0.125

        dq, dk, dv = (v[...].astype(BF).astype(F32) for v in (R.dq, R.dk, R.dv))
        R.dqk[j] = jnp.concatenate([dq, dk], 1).astype(BF)
        gap = jnp.zeros((dv.shape[0], 64), F32)
        R.dvp[j] = jnp.concatenate([dv, gap] if layer == 0 else [gap, dv], 1).astype(BF)
        own = jnp.where(c == 0, 1.0, 0.0)
        for row, value in ((0, dq), (1, dv)):
            line = jnp.sum(value, 0, keepdims=True)
            pair = [line * own, line * (1.0 - own)]
            zero = jnp.zeros((1, 2 * head), F32)
            if j == 0:
                note(6 * layer + row, jnp.concatenate(pair + [zero], 1))
            else:
                R.small[6 * layer + row : 6 * layer + row + 1, :] += jnp.concatenate([zero] + pair, 1)
        if layer == 1 and j == 1:
            load(0, "p", "q", "k", "v")

    def qkv_grad(layer, j):
        if j == 0:
            need(layer, "xw")
        gqk = as_block(contract(R.v_xw[...], R.dqk[j], 0, 0))
        gv = as_block(contract(R.v_xw[...], R.dvp[j], 0, 0))
        if layer == 1:
            R.g_qk1[j] = gqk
            R.g_last[j, :, :, :, 3 * head - 64 :] = gv
        else:
            R.g_last[j, :, :, :, 0 : 2 * head] = gqk
            R.g_last[j, :, :, :, 2 * head : 2 * head + 128] = gv[..., 0:128]
            R.g_last[j, :, :, :, 2 * head + 128 : 3 * head + 64] += gv[..., 128:]
        if layer == 1 and j == 1:
            load(0, "xw")

    def in_part(rows):
        total = None
        for j in range(2):
            w = R.w_qkv.at[j]
            wqk = w[:, :, :, 0 : 2 * head].reshape(width, 2 * head)
            wv = w[:, :, :, 2 * head :].reshape(width, head + 64)
            term = contract(R.dqk[j, rows], wqk, 1, 1) + contract(R.dvp[j, rows], wv, 1, 1)
            total = term if total is None else total + term
        return total

    def halo_copy(layer):
        return remote(R.hs, R.hr.at[layer, c], R.hsend.at[layer], R.hrecv.at[layer, c], {"x": 1 - x, "c": x})

    def in_halo(layer):
        for cp in qkv_copies(layer):
            cp.wait()
        R.hs[...] = in_part(rows_at((1 - x) * 512, 128)).astype(BF)
        halo_copy(layer).start()

    def in_give(layer):
        R.send[...] = in_part(win(1 - c)).astype(BF)
        swap(R.send, R.rh, 4 * layer + 3).start()

    def in_own(layer):
        R.dh[...] = R.dy[...] + in_part(win(c))
        if layer == 1:
            for again in qkv_copies(0):
                again.start()

    def in_sum(layer):
        swap(R.send, R.rh, 4 * layer + 3).wait()
        R.dh[...] += R.rh[...].astype(F32)

        @pl.when(c == 1 - x)
        def _():
            edge = rows_at(128 * c, 128)
            for core in range(2):
                landed(R.hr.at[layer, core], R.hrecv.at[layer, core])
                R.dh[edge] += R.hr[layer, core].astype(F32)

        halo_copy(layer).wait_send()
        if layer == 0:
            gx_copy.start()


    def small_copy(k):
        dev = (cdev, xdev, ydev, {"z": zp1}, {"z": zp2})[k]
        return remote(R.small, R.small_in.at[k], R.bs.at[k], R.br.at[k], dev)

    def small_give(k):
        small_copy(k).start()

    def small_sum(k):
        small_copy(k).wait()
        R.small[...] += R.small_in[k]


    total = R.seg.shape[1]
    number = lax.broadcasted_iota(jnp.int32, (SEGS, total), 0)
    before = (jnp.broadcast_to(R.seg[...], (SEGS, total)) < number).astype(F32)
    starts = jnp.sum(before, 1, keepdims=True).astype(jnp.int32)
    mine = lax.broadcasted_iota(jnp.int32, (SEGS, half), 1) + (2 * x + c) * half
    pick = (mine == starts).astype(F32)
    R.dh[...] = lax.dot_general(
        pick, R.gcls[...], (((0,), (0,)), ((), ())), precision=lax.Precision.HIGHEST, preferred_element_type=F32)

    gx_copy = pltpu.make_async_copy(R.dh, R.gx, R.gx_sem)
    def act(fn, *args):
        actions.append(functools.partial(fn, *args))

    actions = []
    for layer in range(2):
        act(ffn_norm, layer)
        act(ffn_wait, layer)
        for fn in (down_grad, units_back, up_grad):
            act(fn, layer, 0)
            act(fn, layer, 1)
        for fn in (mid_give, mid_own, mid_norm, proj_rows_back, proj_wait, proj_back, proj_grad):
            act(fn, layer)
        for fn in (attend_back, qkv_grad):
            act(fn, layer, 0)
            act(fn, layer, 1)
        for fn in (in_halo, in_give, in_own, in_sum):
            act(fn, layer)
    act(free_ffn, 1)
    for k in range(5):
        act(small_give, k)
    for k in range(5):
        act(small_sum, k)
    for b in GRADS:
        if b in CORNER:
            act(corner_first, b)
            for fn in (corner_out, corner_in, corner_join):
                act(fn, b)
        else:
            for fn in (plane_first, plane_second, plane_join):
                act(fn, b)
        act(finish, b)
    for step in BACKWARD_ORDER:
        actions[step]()
    R.o_small[...] = R.small[...]
    gx_copy.wait()
    for b in GRADS:
        sends_done(b)


def saved_shapes(half, width):
    head = width // 4
    return {
        "xw": ((640, width), BF),
        "q": ((2, 512, head), BF),
        "k": ((2, 640, head), BF),
        "v": ((2, 640, head), BF),
        "p": ((2, 4, 384, 384), BF),
        "att": ((2, 512, head), BF),
        "zf": ((512, width), BF),
        "gp": ((2, 512, width), BF),
        "act": ((2, 512, width), BF),
        "yh1": ((half, width), BF),
        "yh2": ((half, width), BF),
        "r1": ((half, 1), F32),
        "r2": ((half, 1), F32),
        "kp": ((2, half, width), BF),
    }


def run_forward(whole, wqkv, wout, up, down, b_in, biases, gains, pool_b, pairing, pool, tok, seg, drop):
    half, width = tok.shape
    rows = up.shape[1]
    cut = {n: up.shape[1:] for n in BLOCKS}
    cut["small"] = (32, 128)
    cut["qkv"] = (rows, 6 * wqkv.shape[3])
    cut["proj"] = (2 * wout.shape[1], width)
    saved = saved_shapes(half, width)
    head = width // 4
    dma = pltpu.SemaphoreType.DMA
    land = [(2, NZ, NY, *cut[n]) for n in BLOCKS]
    nb = len(BLOCKS)
    loss_outs, loss_scratch = loss_shapes(NZ * NY * SEGS, width)
    shape = jax.ShapeDtypeStruct
    outs = [shape(s, BF) for s in land[1:]]
    outs.append(shape((2, 32, width), F32))
    if whole:
        outs += loss_outs
    else:
        outs += [
            shape((NZ, NY, *pool.shape), BF),
            shape((NZ, NY, *cut["small"]), BF),
            shape((NZ, NY, SEGS, width), BF),
        ]
    outs += [shape((2, *s), t) for s, t in saved.values()]
    names = forward_out(whole)
    out_specs = [VMEM if n in LOSS_OUT + ("o_cls",) else ANY for n in names]
    scratch = [pltpu.VMEM(s, BF) for s in land]
    scratch += [
        pltpu.VMEM((NZ, NY, *pool.shape), BF),
        pltpu.VMEM((4, SEGS, width), BF),
        pltpu.VMEM((NZ, NY, SEGS, width), BF),
    ]
    scratch += [pltpu.VMEM((2, *s), t) for s, t in saved.values()]
    scratch += [
        pltpu.VMEM(drop.shape, drop.dtype),
        pltpu.VMEM((4, 128, 384), F32),
        pltpu.VMEM((2, 2, head, width), BF),
        pltpu.VMEM((2, 32, width), F32),
        pltpu.VMEM((2, 32, head), F32),
        pltpu.VMEM((half, width), F32),
        pltpu.VMEM((half, width), F32),
    ]
    scratch += [pltpu.VMEM((2, half, width), BF)] * 4
    scratch += [
        dma((nb, 4 * NZ)), dma((nb, 2 * NZ)), dma((nb, 2 * NZ)), dma((nb, 2, NZ, NY)), dma((nb,)),
        dma((3 * NZ,)), dma((NZ, NY)), dma, dma((2,)),
        dma((8,)), dma((8,)), dma((2, 2)), dma((2,)), dma, dma((len(SAVED), 2)), dma((nb,)), dma((3,)),
        dma((3,)), dma((3,)), dma((NZ * NY,)), dma((NZ * NY,)),
        pltpu.VMEM(cut["small"], F32),
        pltpu.VMEM(cut["small"], BF),
        pltpu.VMEM(cut["qkv"], BF),
        pltpu.VMEM(cut["proj"], BF),
        pltpu.VMEM((NZ * NY * SEGS, width), BF),
    ]
    if whole:
        scratch += loss_scratch
    res = pl.pallas_call(
        functools.partial(forward_kernel, whole),
        out_shape=outs,
        in_specs=[VMEM, VMEM, ANY, ANY] + [VMEM] * 5 + [ANY, VMEM, VMEM, ANY],
        out_specs=out_specs,
        scratch_shapes=scratch,
        compiler_params=pltpu.CompilerParams(collective_id=1, has_side_effects=True, vmem_limit_bytes=60 << 20),
        name="forward",
    )(wqkv, wout, up, down, b_in, biases, gains, pool_b, pairing, pool, tok, seg, drop)
    return dict(zip(names, res))


def run_backward(weights, saved, vec, seg, gcls):
    width = vec.shape[2]
    half = saved[SAVED.index("yh1")].shape[1]
    head = width // 4
    dma = pltpu.SemaphoreType.DMA
    by_name = dict(zip(BLOCKS[1:], weights))
    rows, wide = by_name["up0"].shape[3:]
    thin = by_name["proj"].shape[3]
    cut = {n: (rows, wide) for n in GRADS}
    cut["proj"] = (thin, width)
    cut["qk1"] = (rows, 2 * head)
    cut["last"] = (rows, 4 * head)
    nb = len(GRADS)
    shape = jax.ShapeDtypeStruct
    outs = [
        shape((half, width), F32),
        shape((2, rows, wide), F32),
        shape((2, rows, wide), F32),
        shape((2, thin // 2, width), F32),
        shape((2, 3, rows, head), F32),
        shape((24, width), F32),
    ]

    def low(*dims):
        return pltpu.VMEM(dims, BF)

    def full(*dims):
        return pltpu.VMEM(dims, F32)

    scratch = [low(2, NZ, NY, *cut[n]) for n in GRADS]
    scratch += [low(NZ - 1, *cut[n]) for n in GRADS]
    split = {n: cut[n][0] // 48 * 16 for n in GRADS}
    for n in GRADS:
        r, w = cut[n]
        scratch.append(low(NZ, r, w) if n in CORNER else low(NZ, NY, split[n], w))
    for n in GRADS:
        r, w = cut[n]
        scratch.append(low(NZ, r, w) if n in CORNER else low(2, NZ, r - split[n], w))
    for n in GRADS:
        r, w = cut[n]
        if n in CORNER:
            scratch += [low(r, w), low(NZ - 1, r, w)]
        else:
            scratch += [low(NZ, r - split[n], w), low(NZ, split[n], w)]
    scratch += [full(rows, wide), full(*cut["proj"]), full(2, 3, rows, head)]
    scratch += [pltpu.VMEM(s, t) for s, t in saved_shapes(half, width).values()]
    scratch += [
        low(2, NZ, NY, rows, 3 * head + 64),
        low(*by_name["proj"].shape),
        low(*by_name["up0"].shape),
        low(*by_name["down0"].shape),
        low(2, head, width),
        low(512, width),
        low(512, width),
        low(half, width),
        low(half, width),
        low(half, width),
        low(128, width),
        low(2, 2, 128, width),
        low(2, 512, head),
        full(640, head),
        full(640, head),
        full(640, head),
        low(2, 640, 2 * head),
        low(2, 640, head + 64),
        low(2, head, width),
        full(half, width),
        full(half, width),
        full(24, width),
        full(5, 24, width),
    ]
    scratch += [
        dma((5,)), dma((len(SAVED),)), dma((nb, 4)), dma((8,)), dma((8,)), dma((2,)), dma((2, 2)),
        dma((nb, NZ + 2)), dma((nb, NZ)), dma((nb, NZ)), dma((nb,)), dma((nb, 2)), dma((nb, 2)),
        dma((nb, 2, NZ - 1)), dma((nb, 2, NZ - 1)), dma((5,)), dma((5,)), dma,
    ]
    return pl.pallas_call(
        backward_kernel,
        out_shape=outs,
        in_specs=[ANY] * (len(weights) + len(saved)) + [VMEM] * 3,
        out_specs=[ANY] * 5 + [VMEM],
        scratch_shapes=scratch,
        compiler_params=pltpu.CompilerParams(collective_id=2, has_side_effects=True, vmem_limit_bytes=63 << 20),
        name="backward",
    )(*weights, *saved, vec, seg, gcls)


def hand_over_kernel(*refs):
    ins, outs, held, sem = refs[:11], refs[11:24], refs[24:30], refs[30]
    loads = [pltpu.make_async_copy(ins[k], held[k], sem.at[0, k]) for k in range(6)]
    moves = [pltpu.make_async_copy(held[k], outs[k], sem.at[1, k]) for k in range(6)]
    for cp in loads:
        cp.start()
    for k in range(6, 10):
        outs[k][...] = ins[k][...]
    sums = ins[10]
    z, y, x, c = position()
    m, dp = 2 * x + c, z * NY + y
    b_in, biases, gains = outs[10:]
    width = sums.shape[1]
    thin, part = biases.shape[2], b_in.shape[1]
    turned = pltpu.roll(sums[0:16], lax.rem(width - (dp * part + m * thin), width), 1)
    for layer in range(2):
        biases[layer] = turned[6 * layer : 6 * layer + 6, 0:thin]
        gains[layer] = turned[12 + 2 * layer : 14 + 2 * layer, 0:thin]
    turned = pltpu.roll(sums[16:24], lax.rem(width - dp * part, width), 1)
    for layer in range(2):
        total = jnp.zeros((1, part), F32)
        for k in range(4):
            total = total + turned[4 * layer + k : 4 * layer + k + 1, 0:part] * jnp.where(m == k, 1.0, 0.0)
        b_in[layer : layer + 1] = total
    for load, move in zip(loads, moves):
        load.wait()
        move.start()
    for cp in moves:
        cp.wait()


def hand_over(large, small, sums):
    shape = jax.ShapeDtypeStruct
    width = sums.shape[1]
    part = width // (NZ * NY)
    outs = [shape(v.shape, v.dtype) for v in large + small]
    outs += [shape((2, part), F32), shape((2, 6, part // 4), F32), shape((2, 2, part // 4), F32)]
    return pl.pallas_call(
        hand_over_kernel,
        out_shape=outs,
        in_specs=[ANY] * len(large) + [VMEM] * (len(small) + 1),
        out_specs=[ANY] * len(large) + [VMEM] * (len(small) + 3),
        scratch_shapes=[pltpu.VMEM(v.shape, v.dtype) for v in large] + [pltpu.SemaphoreType.DMA((2, len(large)))],
        name="hand_over",
    )(*large, *small, sums)


def per_device(tokens_in, segments, pairing, drop_masks, w_qkv, w_out, w_in, w_back, b_in, biases,
               gains, pool_w, pool_b):
    inner = lax.axis_size("g")
    layers = w_qkv.shape[0]
    width = tokens_in.shape[1]
    z, y, x, c = position()
    m = 2 * x + c
    dp = (z * NY + y) * inner + lax.axis_index("g")

    def group(arr, dim):
        return arr if inner == 1 else lax.all_gather(arr, "g", axis=dim, tiled=True)

    w_qkv, w_out, w_in, w_back = group(w_qkv, 2), group(w_out, 1), group(w_in, 1), group(w_back, 1)
    b_in, biases, gains = group(b_in, 1), group(biases, 2), group(gains, 2)
    pool_w, pool_b, pairing = group(pool_w, 0), group(pool_b, 0), group(pairing, 0)
    rows = w_in.shape[1]
    named = run_forward(
        inner == 1, w_qkv, w_out, w_in, w_back, b_in, biases, gains, pool_b[None], pairing[None], pool_w,
        tokens_in, segments, drop_masks)
    if inner == 1:
        loss, align, unif, grad_pool_w, grad_pool_b, gcls = (named[n] for n in LOSS_OUT)
    else:
        cls = named["o_cls"].reshape(NZ * NY, SEGS, width)
        cls = lax.all_gather(cls, "g", axis=1, tiled=True).reshape(-1, width)
        loss, align, unif, grad_pool_w, grad_pool_b, gcls = pooled_loss(
            cls, named["o_pool"], named["o_vec"], named["o_piece"])
    weights = [named["o_" + n] for n in BLOCKS[1:]]
    saved = [named["o_" + n] for n in SAVED]
    grad_x, down, up, proj, qkv, sums = run_backward(weights, saved, named["o_vec"], segments, gcls)

    if inner == 1:
        large = [grad_x, qkv, proj, up, down, grad_pool_w]
        small = [loss, align, unif, grad_pool_b]
        res = hand_over(large, small, sums)
        grad_x, qkv, proj, up, down, grad_pool_w, loss, align, unif, grad_pool_b, out_b_in, out_biases, out_gains = res
        return (
            loss[0], align[0], unif[0], grad_x, qkv, proj, up, down, out_b_in, out_biases, out_gains, grad_pool_w,
            grad_pool_b[0],
        )

    def spread(values, dim):
        return lax.psum_scatter(values, "g", scatter_dimension=dim, tiled=True)

    sums = lax.psum(sums, "g")
    thin = rows // (4 * inner)
    here = lax.dynamic_slice_in_dim(sums[:16], dp * 4 * thin + m * thin, thin, 1)
    up_sums = sums[16:24].reshape(layers, 4 * width)
    n_up = rows // inner
    out_b_in = lax.dynamic_slice_in_dim(up_sums, m * width + dp * n_up, n_up, 1)
    n_pool = pool_w.shape[0] // inner
    g = lax.axis_index("g")
    grad_pool_w = lax.dynamic_slice_in_dim(grad_pool_w, g * n_pool, n_pool, 0)
    return (
        loss[0],
        align[0],
        unif[0],
        grad_x,
        spread(qkv, 2),
        spread(proj, 1),
        spread(up, 1),
        spread(down, 1),
        out_b_in,
        here[:12].reshape(layers, 6, thin),
        here[12:].reshape(layers, 2, thin),
        grad_pool_w,
        grad_pool_b[0],
    )


def solution(mesh):
    count = mesh.shape["dp"]
    fine = Mesh(
        mesh.devices.reshape(NZ, NY, count // (NZ * NY), 2, 2), ("z", "y", "g", "x", "c")
    )
    dp, mp = ("z", "y", "g"), ("x", "c")
    in_specs = (
        P(dp + mp, None),
        P(dp, None),
        P(dp),
        P(None, None, dp + mp, None),
        P(None, None, dp, mp),
        P(None, mp + dp, None),
        P(None, dp, mp),
        P(None, mp + dp, None),
        P(None, mp + dp),
        P(None, None, dp),
        P(None, None, dp),
        P(dp, None),
        P(dp),
    )
    out_specs = (
        P(dp),
        P(dp),
        P(dp),
        P(dp + mp, None),
        P(None, None, dp, mp),
        P(None, mp + dp, None),
        P(None, dp, mp),
        P(None, mp + dp, None),
        P(None, mp + dp),
        P(None, None, dp + mp),
        P(None, None, dp + mp),
        P(dp, None),
        P(dp),
    )
    return jax.shard_map(
        per_device, mesh=fine, in_specs=in_specs, out_specs=out_specs, check_vma=False
    )
```

```python
import functools
from typing import NamedTuple

import jax
import jax.numpy as jnp
from jax import lax
from jax.experimental import pallas as pl
from jax.experimental.pallas import tpu as pltpu
from jax.sharding import Mesh
from jax.sharding import PartitionSpec as P

HEAD_DIM = 64
SEGS = 16
TEMP = 0.05
EPS = 1e-06
KEEP = 0.9
MESH = pl.DeviceIdType.MESH
ANY = pl.BlockSpec(memory_space=pl.ANY)
VMEM = pl.BlockSpec(memory_space=pltpu.VMEM)
BF = jnp.bfloat16
F32 = jnp.float32
NZ = 4
NY = 2


class Names:
    def __init__(self, names, refs):
        for name, ref in zip(names, refs, strict=True):
            setattr(self, name, ref)


def contract(left_side, right_side, left_dim, right_dim):
    return lax.dot_general(
        left_side,
        right_side,
        (((left_dim,), (right_dim,)), ((), ())),
        preferred_element_type=F32,
    )


def mm(a, b):
    return jnp.dot(a, b, preferred_element_type=F32)


def position():
    return tuple(lax.axis_index(name) for name in ("z", "y", "x", "c"))


def signal(sem, device):
    pl.semaphore_signal(sem, inc=1, device_id=device, device_id_type=MESH)


def remote(src, dst, send_sem, recv_sem, device):
    return pltpu.make_async_remote_copy(
        src_ref=src,
        dst_ref=dst,
        send_sem=send_sem,
        recv_sem=recv_sem,
        device_id=device,
        device_id_type=MESH,
    )


def landed(ref, sem):
    pltpu.make_async_copy(ref, ref, sem).wait()


def rows_at(start, count):
    return pl.ds(pl.multiple_of(start, 128), count)


def flat(ref):
    value = ref[...]
    return value.reshape(-1, value.shape[-1])


class ForwardArgs(NamedTuple):
    wqkv: object
    wout: object
    up: object
    down: object
    b_in: object
    biases: object
    gains: object
    pool_b: object
    pairing: object
    pool: object
    tok: object
    seg: object
    drop: object


class ForwardScratch(NamedTuple):
    keep: object
    bias: object
    wo: object
    vec: object
    qv: object
    h: object
    z: object
    sa: object
    ra: object
    sf: object
    rf: object
    zsend: object
    xsend: object
    ysend: object
    recv: object
    own_sem: object
    pool_send: object
    pool_recv: object
    pool_own: object
    pool_core: object
    core_send: object
    core_recv: object
    halo_send: object
    halo_recv: object
    drop_sem: object
    out_sem: object
    w_sem: object
    misc_sem: object
    s1: object
    r1s: object
    s2: object
    r2s: object
    wide: object
    sm: object
    sq: object
    sp: object
    cls: object


SMALL, QKV, PROJ, UP0, DOWN0, UP1, DOWN1 = range(7)
BLOCKS = ("small", "qkv", "proj", "up0", "down0", "up1", "down1")
SAVED = ("xw", "q", "k", "v", "p", "att", "zf", "gp", "act", "yh1", "yh2", "r1", "r2", "kp")
FWD_IN = ForwardArgs._fields
LOSS_OUT = ("loss", "align", "unif", "gw", "gb", "gcls")
LOSS_SCR = ("u", "nb", "rn", "dn", "dpre", "table", "gw_all")


def forward_out(whole):
    after = LOSS_OUT if whole else ("o_pool", "o_piece", "o_cls")
    return tuple("o_" + n for n in BLOCKS[1:]) + ("o_vec",) + after + tuple("o_" + n for n in SAVED)


FWD_SCR = (
    tuple("w_" + n for n in BLOCKS) + ("w_pool", "cls_part", "cls_all") + SAVED
    + ForwardScratch._fields
)


FORWARD_ORDER = (
    0, 6, 1, 3, 4, 39, 73, 5, 67, 45, 44, 14, 2, 17, 18, 43, 52, 19, 15, 20, 68, 21, 16, 22, 36, 47, 40, 38,
    58, 37, 59, 69, 42, 41, 35, 51, 23, 26, 27, 53, 32, 60, 55, 24, 7, 33, 70, 29, 71, 28, 74, 8, 77, 78, 56,
    79, 61, 57, 46, 80, 81, 9, 75, 62, 25, 63, 82, 72, 83, 30, 10, 11, 54, 34, 84, 85, 86, 49, 87, 48, 64, 88,
    65, 31, 89, 90, 91, 50, 92, 66, 93, 94, 12, 95, 13, 96, 97, 98, 76,
)


def forward_kernel(whole, *refs):
    R = Names(FWD_IN + forward_out(whole) + FWD_SCR + (LOSS_SCR if whole else ()), refs)
    z, y, x, c = position()
    up, down = z < NZ - 1, z > 0
    xdev, ydev, cdev, xcdev = {"x": 1 - x}, {"y": 1 - y}, {"c": 1 - c}, {"x": 1 - x, "c": 1 - c}
    half = R.tok.shape[0]
    ins = [R.sm, R.sq, R.sp, R.up.at[0], R.down.at[0], R.up.at[1], R.down.at[1]]
    lands = [getattr(R, "w_" + n) for n in BLOCKS]

    peers = [(k * NY + flip, k, flip) for k in range(NZ) for flip in range(NY) if k or flip]

    def peer(k, flip):
        return {"z": lax.rem(z + k, NZ), "y": y if flip == 0 else 1 - y}

    R.wide[...] = jnp.zeros_like(R.wide)
    n = R.b_in.shape[1]
    row = 0
    biases = [R.biases[k] for k in range(R.biases.shape[0])]
    shifts = [value[layer : layer + 1] for layer in range(2) for value in biases]
    for value in (R.b_in[...], *shifts, R.gains[0], R.gains[1], R.pool_b[...]):
        R.wide[row : row + value.shape[0], 0:n] = value.astype(F32)
        row += value.shape[0]
    pair = R.pairing[...]
    R.wide[row : row + 1, 0 : pair.shape[1]] = (pair // 32).astype(F32)
    R.wide[row + 1 : row + 2, 0 : pair.shape[1]] = lax.rem(pair, 32).astype(F32)
    R.sm[...] = R.wide[...].astype(BF)
    parts = [R.wqkv[layer, k].astype(F32) for layer, k in ((0, 0), (0, 1), (1, 0), (1, 1), (0, 2), (1, 2))]
    R.sq[...] = jnp.concatenate(parts, 1).astype(BF)
    R.sp[...] = jnp.concatenate([R.wout[0].astype(F32), R.wout[1].astype(F32)], 0).astype(BF)

    bar = pltpu.get_barrier_semaphore()
    for dev in (xdev, cdev, xcdev):
        signal(bar, dev)
    for _, k, flip in peers:
        signal(bar, peer(k, flip))
    pl.semaphore_wait(bar, 3 + len(peers))


    def copy(b, src, slot, device, sem):
        return remote(src, lands[b].at[slot], sem, R.recv.at[(b, *slot)], device)

    def arrived(b, slot):
        landed(lands[b].at[slot], R.recv.at[(b, *slot)])

    def by_z(b):
        return b in (PROJ, UP0, DOWN0, UP1)

    def over_y(b):
        return b in (SMALL, UP0, UP1, DOWN1)

    def sideways(b, src, slot, k):
        copy(b, src, slot, xdev, R.xsend.at[b, k]).start()
        copy(b, src, slot, ydev, R.ysend.at[b, k]).start()

    def launch(b):
        src, mine = ins[b], (x, z, y)
        pl.when(up)(lambda: copy(b, src, mine, {"z": z + 1}, R.zsend.at[b, 0]).start())
        pl.when(down)(lambda: copy(b, src, mine, {"z": z - 1}, R.zsend.at[b, 1]).start())
        sideways(b, src, mine, 0)
        pltpu.make_async_copy(src, lands[b].at[mine], R.own_sem.at[b]).start()

    def z_relay(b, d):
        @pl.when(z >= d)
        def _():
            slot = (x, z - d, y)
            arrived(b, slot)
            pl.when(up)(lambda: copy(b, lands[b].at[slot], slot, {"z": z + 1}, R.zsend.at[b, 2 * d]).start())
            sideways(b, lands[b].at[slot], slot, NZ - d)

        @pl.when(z < NZ - d)
        def _():
            slot = (x, z + d, y)
            arrived(b, slot)
            pl.when(down)(lambda: copy(b, lands[b].at[slot], slot, {"z": z - 1}, R.zsend.at[b, 2 * d + 1]).start())
            sideways(b, lands[b].at[slot], slot, d)

    def xy_relay(b, k):
        zp = lax.rem(z + k, NZ)
        sx, sy = (1 - x, zp, y), (x, zp, 1 - y)
        if over_y(b):
            arrived(b, sx)
            copy(b, lands[b].at[sx], sx, ydev, R.ysend.at[b, NZ + k]).start()
        else:
            arrived(b, sy)
            copy(b, lands[b].at[sy], sy, xdev, R.xsend.at[b, NZ + k]).start()

    def corner_launch(b):
        slot = (1 - x, z, 1 - y)
        arrived(b, slot)
        pl.when(up)(lambda: copy(b, lands[b].at[slot], slot, {"z": z + 1}, R.zsend.at[b, 2 * NZ]).start())
        pl.when(down)(lambda: copy(b, lands[b].at[slot], slot, {"z": z - 1}, R.zsend.at[b, 2 * NZ + 1]).start())

    def corner_relay(b, d):
        @pl.when(z >= d)
        def _():
            slot = (1 - x, z - d, 1 - y)
            arrived(b, slot)
            pl.when(up)(lambda: copy(b, lands[b].at[slot], slot, {"z": z + 1}, R.zsend.at[b, 2 * NZ + 2 * d]).start())

        @pl.when(z < NZ - d)
        def _():
            slot = (1 - x, z + d, 1 - y)
            arrived(b, slot)
            pl.when(down)(lambda: copy(b, lands[b].at[slot], slot, {"z": z - 1}, R.zsend.at[b, 2 * NZ + 2 * d + 1]).start())

    def complete(b):
        relays = 1 if by_z(b) else NZ
        for k in range(NZ):
            zp = lax.rem(z + k, NZ)
            if k >= relays or not over_y(b):
                arrived(b, (1 - x, zp, y))
            if k >= relays or over_y(b):
                arrived(b, (x, zp, 1 - y))
            if not by_z(b):
                arrived(b, (1 - x, zp, 1 - y))
        pltpu.make_async_copy(ins[b], lands[b].at[x, z, y], R.own_sem.at[b]).wait()
        if b != SMALL:
            w_copy(b).start()

    def sends_done(b):
        src, mine = ins[b], (x, z, y)
        for k in range(NZ):
            copy(b, src, mine, xdev, R.xsend.at[b, k]).wait_send()
            copy(b, src, mine, ydev, R.ysend.at[b, k]).wait_send()
        for k in range(1 if by_z(b) else NZ):
            if over_y(b):
                copy(b, src, mine, ydev, R.ysend.at[b, NZ + k]).wait_send()
            else:
                copy(b, src, mine, xdev, R.xsend.at[b, NZ + k]).wait_send()
        for d in range(NZ):
            for base in (0, 2 * NZ) if by_z(b) else (0,):
                pl.when(up & (z >= d))(lambda: copy(b, src, mine, {"z": z + 1}, R.zsend.at[b, base + 2 * d]).wait_send())
                pl.when(down & (z < NZ - d))(lambda: copy(b, src, mine, {"z": z - 1}, R.zsend.at[b, base + 2 * d + 1]).wait_send())

    prow = R.pool.shape[0] // 2
    pool_rows = pl.ds(pl.multiple_of(c * prow, 16), prow)

    def pool_slot(zp, yp):
        return R.w_pool.at[zp, yp, pool_rows]

    def pool_copy(src, zp, yp, device, k):
        return remote(src, pool_slot(zp, yp), R.pool_send.at[k], R.pool_recv.at[zp, yp], device)

    def pool_launch():
        src = R.pool.at[pool_rows]
        pl.when(up)(lambda: pool_copy(src, z, y, {"z": z + 1}, 0).start())
        pl.when(down)(lambda: pool_copy(src, z, y, {"z": z - 1}, 1).start())
        pool_copy(src, z, y, ydev, 2 * NZ).start()
        pltpu.make_async_copy(src, pool_slot(z, y), R.pool_own).start()

    def pool_relay(d):
        @pl.when(z >= d)
        def _():
            here = pool_slot(z - d, y)
            landed(here, R.pool_recv.at[z - d, y])
            pl.when(up)(lambda: pool_copy(here, z - d, y, {"z": z + 1}, 2 * d).start())
            pool_copy(here, z - d, y, ydev, 2 * NZ + NZ - d).start()

        @pl.when(z < NZ - d)
        def _():
            here = pool_slot(z + d, y)
            landed(here, R.pool_recv.at[z + d, y])
            pl.when(down)(lambda: pool_copy(here, z + d, y, {"z": z - 1}, 2 * d + 1).start())
            pool_copy(here, z + d, y, ydev, 2 * NZ + d).start()

    def pool_core():
        halves = R.w_pool.at[:, :, pool_rows]
        return remote(halves, halves, R.pool_core.at[0], R.pool_core.at[1], cdev)

    def pool_swap():
        pltpu.make_async_copy(R.pool.at[pool_rows], pool_slot(z, y), R.pool_own).wait()
        for k in range(NZ):
            zp = lax.rem(z + k, NZ)
            landed(pool_slot(zp, 1 - y), R.pool_recv.at[zp, 1 - y])
        pool_core().start()

    def pool_done():
        there = R.w_pool.at[:, :, pl.ds(pl.multiple_of((1 - c) * prow, 16), prow)]
        landed(there, R.pool_core.at[1])
        pool_core().wait_send()
        src = R.pool.at[pool_rows]
        for d in range(NZ):
            pl.when(up & (z >= d))(lambda: pool_copy(src, z, y, {"z": z + 1}, 2 * d).wait_send())
            pl.when(down & (z < NZ - d))(lambda: pool_copy(src, z, y, {"z": z - 1}, 2 * d + 1).wait_send())
            pool_copy(src, z, y, ydev, 2 * NZ + d).wait_send()
        for cp in misc_copies():
            cp.start()


    def win(core):
        return rows_at(x * 128 + core * half, half)

    def chip(core):
        return rows_at(core * half, half)

    def swap(src, dst, n):
        return remote(src, dst, R.core_send.at[n], R.core_recv.at[n], cdev)

    def rows_swap(layer):
        here = R.xw.at[layer, win(c)]
        return swap(here, here, 4 * layer)

    def edge_copies(layer):
        src = R.xw.at[layer, rows_at(x * 128 + c * half + 128 * c, 128)]
        dst = R.xw.at[layer, rows_at(x * 512, 128)]
        return [
            remote(src, dst, R.halo_send.at[layer, i], R.halo_recv.at[layer], dev)
            for i, dev in enumerate(({"x": 1 - x, "c": c}, {"x": 1 - x, "c": 1 - c}))
        ]

    def send_rows(layer):
        rows_swap(layer).start()

        @pl.when(c == 1 - x)
        def _():
            for cp in edge_copies(layer):
                cp.start()

    def partner_rows_here(layer):
        landed(R.xw.at[layer, win(1 - c)], R.core_recv.at[4 * layer])

    def edge_here(layer):
        landed(R.xw.at[layer, rows_at((1 - x) * 512, 128)], R.halo_recv.at[layer])


    def vec(layer, k):
        return R.vec[0, 2 + 6 * layer + k : 3 + 6 * layer + k, :]

    def gain(layer, k):
        return R.vec[0, 14 + 2 * layer + k : 15 + 2 * layer + k, :]

    def spread_params():
        width = R.vec.shape[2]
        part = width // (NZ * NY)
        lane = lax.broadcasted_iota(jnp.int32, (128, width), 0)
        col = lax.broadcasted_iota(jnp.int32, (128, width), 1)
        for j in range(2):
            total = jnp.zeros((R.vec.shape[1], width), F32)
            for dp in range(NZ * NY):
                place = ((lane < part) & (col == lane + dp * part)).astype(F32).astype(BF)
                total = total + mm(R.w_small[j, dp // NY, dp % NY], place)
            R.vec[j] = total
        head = R.qv.shape[2]
        lane = lax.broadcasted_iota(jnp.int32, (width, head), 0)
        col = lax.broadcasted_iota(jnp.int32, (width, head), 1)
        low = R.vec[0].astype(BF)
        for j in range(2):
            place = (lane == col + (2 * j + c) * head).astype(F32).astype(BF)
            R.qv[j] = mm(low, place)

    def masks():
        for i in range(4):
            mine = R.seg[0:1, rows_at(x * 512 + i * 128, 128)]
            start = (3 * (x + i) + 1) // 5 * 128
            keys = R.seg[0:1, rows_at(x * 384 + start, 384)]
            column = jnp.transpose(jnp.broadcast_to(mine, (128, 128)))
            for t in range(3):
                same = column == jnp.broadcast_to(keys[:, t * 128 : t * 128 + 128], (128, 128))
                R.bias[i, :, t * 128 : t * 128 + 128] = jnp.where(same, 0.0, -1000000000.0)

    def proj_rows():
        for layer in range(2):
            for j in range(2):
                value = R.w_proj[j].astype(F32)
                rows = value.shape[2] // 2
                value = value[:, :, layer * rows : (layer + 1) * rows].reshape(-1, value.shape[3])
                R.wo[layer, j] = value.astype(BF)

    def project(layer, wrow, count, crow):
        xx = R.xw[layer, wrow]
        head = R.q.shape[3]
        for j in range(2):
            w = R.w_qkv.at[j]
            wqk = w[:, :, :, layer * 2 * head : (layer + 1) * 2 * head].reshape(-1, 2 * head)
            yqk = mm(xx, wqk)
            if crow is not None:
                bq = R.qv[j, 2 + 6 * layer : 3 + 6 * layer, :]
                R.q[layer, j, crow] = (yqk[:, :head] + bq).astype(BF) * jnp.asarray(0.125, BF)
            R.k[layer, j, wrow] = yqk[:, head:].astype(BF)
            bv = R.qv[j, 3 + 6 * layer : 4 + 6 * layer, :]
            if layer == 0:
                yv = mm(xx, w[:, :, :, 4 * head : 5 * head].reshape(-1, head))
            else:
                yv = mm(xx, w[:, :, :, 5 * head - 64 : 6 * head].reshape(-1, head + 64))[:, 64:]
            R.v[layer, j, wrow] = (yv + bv).astype(BF)

    def attend(layer, j):
        head = R.q.shape[3]
        lane = lax.broadcasted_iota(jnp.int32, (1, head), 1) // HEAD_DIM
        picks = [(lane == n).astype(F32) for n in range(head // HEAD_DIM)]
        count = len(picks)

        @pl.loop(0, 4)
        def _(i):
            keys = rows_at((3 * (x + i) + 1) // 5 * 128, 384)
            mine = rows_at(i * 128, 128)
            qq = R.q[layer, j, mine]
            q3 = jnp.concatenate([qq * pick.astype(BF) for pick in picks], 0)
            scores = contract(q3, R.k[layer, j, keys], 1, 1)
            bias = R.bias[i]
            scores = scores.reshape(count, 128, 384) + bias[None]
            peak = jnp.max(scores, -1, keepdims=True)
            e = jnp.exp(scores - peak)
            p = (e * (1.0 / jnp.sum(e, -1, keepdims=True))).astype(BF).reshape(count * 128, 384)
            R.p[layer, j, i] = p
            o = mm(p, R.v[layer, j, keys])
            total = o[0:128] * picks[0]
            for n in range(1, count):
                total = total + o[n * 128 : (n + 1) * 128] * picks[n]
            R.att[layer, j, mine] = total.astype(BF)

        if j == 1:
            save(layer, "p", "att")

    def proj_part(layer, rows):
        return mm(R.att[layer, 0, rows], R.wo[layer, 0]) + mm(R.att[layer, 1, rows], R.wo[layer, 1])

    def norm(value, g, s):
        center = jnp.mean(value, 1, keepdims=True)
        spread = lax.rsqrt(jnp.mean(value * value, 1, keepdims=True) - center * center + EPS)
        hat = (value - center) * spread
        return hat * g + s, hat, spread

    def attention_give(layer):
        R.sa[layer] = proj_part(layer, chip(1 - c)).astype(BF)
        swap(R.sa.at[layer], R.ra.at[layer], 4 * layer + 1).start()

    def attention_out(layer):
        if layer == 0:
            drop.wait()
            for n in range(2):
                for k in range(2):
                    R.kp[n, k] = R.keep[n, k].astype(F32).astype(BF)
                save(n, "kp")
        a = proj_part(layer, chip(c))
        swap(R.sa.at[layer], R.ra.at[layer], 4 * layer + 1).wait_recv()
        a = a + R.ra[layer].astype(F32) + vec(layer, 2)
        out, hat, spread = norm(R.h[...] + R.kp[layer, 0].astype(F32) * a * (1.0 / KEEP), gain(layer, 0), vec(layer, 3))
        R.z[...] = out
        R.yh1[layer] = hat.astype(BF)
        R.r1[layer] = spread
        R.zf[layer, chip(c)] = out.astype(BF)
        here = R.zf.at[layer, chip(c)]
        swap(here, here, 4 * layer + 2).start()
        save(layer, "yh1", "r1")

    def ffn_up(layer, own):
        if not own:
            landed(R.zf.at[layer, chip(1 - c)], R.core_recv.at[4 * layer + 2])
        rows = chip(c if own else 1 - c)
        w = R.w_up0 if layer == 0 else R.w_up1
        zz = R.zf[layer, rows]
        for j in range(2):
            hid = mm(zz, flat(w.at[j])) + R.vec[j, layer : layer + 1, :]
            cdf = 0.5 + 0.5 * lax.erf(hid * 0.7071067811865476)
            R.act[layer, j, rows] = (hid * cdf).astype(BF)
            R.gp[layer, j, rows] = (cdf + hid * jnp.exp(-0.5 * hid * hid) * 0.3989422804014327).astype(BF)
        if not own:
            save(layer, "zf", "gp", "act")

    def ffn_part(layer, rows):
        w = R.w_down0 if layer == 0 else R.w_down1
        return mm(R.act[layer, 0, rows], flat(w.at[0])) + mm(R.act[layer, 1, rows], flat(w.at[1]))

    def ffn_give(layer):
        R.sf[layer] = ffn_part(layer, chip(1 - c)).astype(BF)
        swap(R.sf.at[layer], R.rf.at[layer], 4 * layer + 3).start()

    def ffn_down(layer):
        f = ffn_part(layer, chip(c))
        swap(R.sf.at[layer], R.rf.at[layer], 4 * layer + 3).wait_recv()
        f = f + R.rf[layer].astype(F32) + vec(layer, 4)
        out, hat, spread = norm(R.z[...] + R.kp[layer, 1].astype(F32) * f * (1.0 / KEEP), gain(layer, 1), vec(layer, 5))
        R.h[...] = out
        R.yh2[layer] = hat.astype(BF)
        R.r2[layer] = spread
        if layer == 0:
            R.xw[1, win(c)] = out.astype(BF)
            send_rows(1)
        save(layer, "yh2", "r2")

    def project_part(layer, part):
        if part == 0:
            project(layer, win(c), half, chip(c))
        elif part == 1:
            partner_rows_here(layer)
            project(layer, win(1 - c), half, chip(1 - c))
        else:
            edge_here(layer)
            project(layer, rows_at((1 - x) * 512, 128), 128, None)
            save(layer, "xw", "q", "k", "v")


    def out_copy(k, layer):
        name = SAVED[k]
        return pltpu.make_async_copy(getattr(R, name).at[layer], getattr(R, "o_" + name).at[layer], R.out_sem.at[k, layer])

    def save(layer, *names):
        for name in names:
            out_copy(SAVED.index(name), layer).start()

    def w_copy(b):
        return pltpu.make_async_copy(lands[b], getattr(R, "o_" + BLOCKS[b]), R.w_sem.at[b])

    def misc_copies():
        copies = [pltpu.make_async_copy(R.vec, R.o_vec, R.misc_sem.at[0])]
        if not whole:
            copies.append(pltpu.make_async_copy(R.w_pool, R.o_pool, R.misc_sem.at[1]))
            copies.append(pltpu.make_async_copy(R.w_small.at[0], R.o_piece, R.misc_sem.at[2]))
        return copies


    def pooled():
        total = R.seg.shape[1]
        number = lax.broadcasted_iota(jnp.int32, (SEGS, total), 0)
        before = (jnp.broadcast_to(R.seg[...], (SEGS, total)) < number).astype(F32)
        starts = jnp.sum(before, 1, keepdims=True).astype(jnp.int32)
        mine = lax.broadcasted_iota(jnp.int32, (SEGS, half), 1) + (2 * x + c) * half
        pick = (mine == starts).astype(F32).astype(BF)
        row = mm(pick, R.h[...].astype(BF))
        R.cls_part[0] = row.astype(BF)
        first = [
            remote(R.cls_part.at[0], R.cls_part.at[1 + i], R.s1.at[i], R.r1s.at[i], dev)
            for i, dev in enumerate((xdev, cdev, xcdev))
        ]
        for cp in first:
            cp.start()
        for i, cp in enumerate(first):
            cp.wait_recv()
            row = row + R.cls_part[1 + i].astype(F32)
        here = R.cls_all.at[z, y]
        here[...] = row.astype(BF)
        second = [remote(here, here, R.s2.at[i], R.r2s.at[i], peer(k, flip)) for i, k, flip in peers]
        for cp in second:
            cp.start()
        for i, k, flip in peers:
            landed(R.cls_all.at[lax.rem(z + NZ - k, NZ), y if flip == 0 else 1 - y], R.r2s.at[i])
        if whole:
            R.cls[...] = R.cls_all[...].reshape(R.cls.shape)
            work_out_loss(R.cls, R.w_pool, R.vec, R.w_small.at[0], *[getattr(R, n) for n in LOSS_OUT + LOSS_SCR])
        else:
            R.o_cls[...] = R.cls_all[...]
        for cp in first + second:
            cp.wait_send()


    R.xw[0, win(c)] = R.tok[...]
    send_rows(0)
    drop = pltpu.make_async_copy(R.drop, R.keep, R.drop_sem)
    drop.start()
    R.h[...] = R.tok[...].astype(F32)
    def act(fn, *args):
        actions.append(functools.partial(fn, *args))

    actions = []
    every = range(len(BLOCKS))
    along = [b for b in every if by_z(b)]
    for b in every:
        act(launch, b)
    for b in every:
        act(complete, b)
    for b in every:
        for d in range(1, NZ):
            act(z_relay, b, d)
    for b in every:
        for k in range(1 if by_z(b) else NZ):
            act(xy_relay, b, k)
    for b in along:
        act(corner_launch, b)
    for b in along:
        for d in range(1, NZ):
            act(corner_relay, b, d)
    act(pool_launch)
    for d in range(1, NZ):
        act(pool_relay, d)
    for fn in (pool_swap, pool_done, masks, spread_params, proj_rows, pooled):
        act(fn)
    for layer in range(2):
        for k in range(3):
            act(project_part, layer, k)
        for j in range(2):
            act(attend, layer, j)
        act(attention_give, layer)
        act(attention_out, layer)
        act(ffn_up, layer, True)
        act(ffn_up, layer, False)
        act(ffn_give, layer)
        act(ffn_down, layer)
    for step in FORWARD_ORDER:
        actions[step]()

    for b in range(len(BLOCKS)):
        sends_done(b)
        if b != SMALL:
            w_copy(b).wait()
    for cp in misc_copies():
        cp.wait()
    for layer in range(2):
        for k in range(len(SAVED)):
            out_copy(k, layer).wait()
        rows_swap(layer).wait_send()
        swap(R.sa.at[layer], R.ra.at[layer], 4 * layer + 1).wait_send()
        swap(R.zf.at[layer, chip(c)], R.zf.at[layer, chip(c)], 4 * layer + 2).wait_send()
        swap(R.sf.at[layer], R.rf.at[layer], 4 * layer + 3).wait_send()

        @pl.when(c == 1 - x)
        def _():
            for cp in edge_copies(layer):
                cp.wait_send()


def work_out_loss(cls, pool, vec, piece, loss, align, unif, gw, gb, gcls, u, nb, rn, dn, dpre, table, gw_all):
    z, y = lax.axis_index("z"), lax.axis_index("y")
    inner = lax.axis_size("g")
    count, width = cls.shape
    per = SEGS * inner
    pre = mm(cls[...], pool[...].reshape(width, width)) + vec[0, 18:19, :]
    value = jnp.tanh(pre)
    u[...] = value
    scale = lax.rsqrt(jnp.sum(value * value, 1, keepdims=True) + EPS)
    rn[...] = scale
    nb[...] = (value * scale).astype(BF)
    low = nb[...].astype(F32)
    squares_row = lax.dot_general(
        jnp.ones((8, width), F32), low * low, (((1,), (1,)), ((), ())),
        precision=lax.Precision.HIGHEST, preferred_element_type=F32)[0:1]
    dn[...] = jnp.zeros_like(dn)

    @pl.loop(0, count // 128)
    def _(blk):
        rows = rows_at(blk * 128, 128)
        ids = lax.broadcasted_iota(jnp.int32, (128, 1), 0) + blk * 128
        cols = lax.broadcasted_iota(jnp.int32, (1, count), 1)
        pair = jnp.zeros((128, 1), F32)
        lane = lax.broadcasted_iota(jnp.int32, (1, 128), 1)
        for o in range(NZ * NY):
            got = piece[o // NY, o % NY]
            number = got[19:20].astype(F32) * 32.0 + got[20:21].astype(F32)
            here = (ids == o * per + lane) & (lane < per)
            pair = pair + jnp.sum(jnp.where(here, number, 0.0), 1, keepdims=True)
        mine = nb[rows]
        gram = contract(mine, nb[...], 1, 1)
        logits = gram * (1.0 / TEMP)
        own = cols == ids
        twin = cols == pair.astype(jnp.int32)
        masked = jnp.where(own, -1000000000.0, logits)
        peak = jnp.max(masked, 1, keepdims=True)
        e = jnp.exp(masked - peak)
        total = jnp.sum(e, 1, keepdims=True)
        low_mine = mine.astype(F32)
        squares = jnp.sum(low_mine * low_mine, 1, keepdims=True)
        distance = squares + squares_row - 2.0 * gram
        terms = (
            peak + jnp.log(total) - jnp.sum(jnp.where(twin, logits, 0.0), 1, keepdims=True),
            jnp.sum(jnp.where(twin, distance, 0.0), 1, keepdims=True),
            jnp.log(jnp.sum(jnp.where(own, 0.0, jnp.exp(-2.0 * distance)), 1, keepdims=True) * (1.0 / (count - 1))),
        )
        for t in range(3):
            table[t, rows] = jnp.broadcast_to(terms[t], (128, 128))
        dg = ((e * (1.0 / total) - jnp.where(twin, 1.0, 0.0)) * (1.0 / TEMP)).astype(BF)
        dn[rows] += mm(dg, nb[...])
        dn[...] += contract(dg, mine, 0, 0)

    grad = dn[...]
    value = u[...]
    unit = value * rn[...]
    du = rn[...] * (grad - unit * jnp.sum(grad * unit, 1, keepdims=True))
    dpre[...] = (du * (1.0 - value * value)).astype(BF)
    dp = (z * NY + y) * inner + lax.axis_index("g")
    mine = pl.ds(pl.multiple_of(dp * SEGS, SEGS), SEGS)
    gcls[...] = contract(dpre[mine], pool[...].reshape(width, width), 1, 1)
    thin = gb.shape[1]
    columns = jnp.sum(dpre[...].astype(F32), 0, keepdims=True)
    gb[...] = pltpu.roll(jnp.broadcast_to(columns, (8, width)), lax.rem(width - dp * thin, width), 1)[0:1, 0:thin]
    gw_all[...] = contract(cls[...], dpre[...], 0, 0)
    part = gw.shape[0]
    gw[...] = gw_all[pl.ds(pl.multiple_of((z * NY + y) * part, 8), part)]
    for t, ref in enumerate((loss, align, unif)):
        lines = [jnp.transpose(table[t, n * 128 : (n + 1) * 128])[0:8] for n in range(count // 128)]
        line = jnp.concatenate(lines, 1)
        ref[...] = pltpu.roll(line, lax.rem(count - dp * SEGS, count), 1)[0:1, 0:SEGS]


def loss_shapes(count, width):
    one = jax.ShapeDtypeStruct((1, SEGS), F32)
    outs = [
        one, one, one,
        jax.ShapeDtypeStruct((width // (NZ * NY), width), F32),
        jax.ShapeDtypeStruct((1, width * SEGS // count), F32),
        jax.ShapeDtypeStruct((SEGS, width), F32),
    ]
    scratch = [
        pltpu.VMEM((count, width), F32),
        pltpu.VMEM((count, width), BF),
        pltpu.VMEM((count, 1), F32),
        pltpu.VMEM((count, width), F32),
        pltpu.VMEM((count, width), BF),
        pltpu.VMEM((3, count, 128), F32),
        pltpu.VMEM((width, width), F32),
    ]
    return outs, scratch


def pooled_loss(cls, pool, vec, piece):
    outs, scratch = loss_shapes(*cls.shape)
    return pl.pallas_call(
        work_out_loss,
        out_shape=outs,
        in_specs=[VMEM] * 4,
        out_specs=[VMEM] * 6,
        scratch_shapes=scratch,
        compiler_params=pltpu.CompilerParams(vmem_limit_bytes=48 << 20),
        name="pooled_loss",
    )(cls, pool, vec, piece)


class BackwardScratch(NamedTuple):
    w_qkv: object
    w_proj: object
    w_up: object
    w_down: object
    wo: object
    dff: object
    daf: object
    send: object
    rz: object
    rh: object
    hs: object
    hr: object
    datt: object
    dq: object
    dk: object
    dv: object
    dqk: object
    dvp: object
    dwo: object
    dh: object
    dy: object
    small: object
    small_in: object
    w_sem: object
    v_sem: object
    out_sem: object
    csend: object
    crecv: object
    hsend: object
    hrecv: object
    s1: object
    rx: object
    ry: object
    rd: object
    s2: object
    r2s: object
    zs: object
    zrs: object
    bs: object
    br: object
    gx_sem: object


GRADS = ("down1", "up1", "qk1", "down0", "up0", "proj", "last")
CORNER = {"down1": "x", "up1": "y", "down0": "x"}
BWD_IN = BLOCKS[1:] + SAVED + ("vec", "seg", "gcls")
BWD_OUT = ("gx", "o_down", "o_up", "o_proj", "o_qkv", "o_small")
BWD_SCR = (
    tuple("g_" + n for n in GRADS) + tuple("zr_" + n for n in GRADS)
    + tuple("px_" + n for n in GRADS) + tuple("py_" + n for n in GRADS)
    + tuple(t + n for n in GRADS for t in (("pd_", "zd_") if n in CORNER else ("qx_", "qy_")))
    + ("st_ffn", "st_proj", "st_qkv") + tuple("v_" + n for n in SAVED)
    + BackwardScratch._fields
)
BACKWARD_ORDER = (
    23, 34, 24, 25, 26, 57, 27, 28, 31, 32, 33, 35, 29, 30, 62, 36, 38, 39, 42, 40, 58, 41, 43, 67, 44, 45, 0,
    11, 63, 37, 1, 2, 59, 3, 71, 46, 4, 68, 5, 8, 64, 60, 6, 9, 10, 12, 7, 76, 69, 13, 15, 72, 65, 16, 73, 17,
    77, 74, 18, 84, 14, 78, 47, 52, 48, 85, 80, 86, 81, 66, 19, 20, 75, 53, 49, 82, 54, 50, 70, 79, 21, 22,
    55, 87, 51, 61, 83, 56,
)


def backward_kernel(*refs):
    R = Names(BWD_IN + BWD_OUT + BWD_SCR, refs)
    z, y, x, c = position()
    up, down = z < NZ - 1, z > 0
    xdev, ydev, cdev = {"x": 1 - x}, {"y": 1 - y}, {"c": 1 - c}
    half = R.gx.shape[0]
    head = R.q.shape[3]
    width = R.gx.shape[1]


    def v_copy(name, layer):
        k = SAVED.index(name)
        return pltpu.make_async_copy(getattr(R, name).at[layer], getattr(R, "v_" + name), R.v_sem.at[k])

    def load(layer, *names):
        for name in names:
            v_copy(name, layer).start()

    def need(layer, *names):
        for name in names:
            v_copy(name, layer).wait()

    def qkv_copies(layer):
        src, dst = R.qkv, R.w_qkv
        low = 4 * head if layer == 0 else 5 * head - 64
        return [
            pltpu.make_async_copy(src.at[:, :, :, :, layer * 2 * head : (layer + 1) * 2 * head],
                                  dst.at[:, :, :, :, 0 : 2 * head], R.w_sem.at[0]),
            pltpu.make_async_copy(src.at[:, :, :, :, low : low + head + 64],
                                  dst.at[:, :, :, :, 2 * head : 3 * head + 64], R.w_sem.at[1]),
        ]

    def up_copy(layer):
        return pltpu.make_async_copy(R.up0 if layer == 0 else R.up1, R.w_up, R.w_sem.at[2])

    def down_copy(layer):
        return pltpu.make_async_copy(R.down0 if layer == 0 else R.down1, R.w_down, R.w_sem.at[3])

    def proj_copy():
        return pltpu.make_async_copy(R.proj, R.w_proj, R.w_sem.at[4])

    load(1, "yh2", "r2", "kp", "act")
    down_copy(1).start()
    load(1, "gp", "zf")
    up_copy(1).start()
    load(1, "yh1", "r1", "att")
    proj_copy().start()
    load(1, "p", "q", "k", "v", "xw")
    for cp in qkv_copies(1):
        cp.start()

    zp1 = z + 1 - 2 * lax.rem(z, 2)
    zp2 = lax.rem(z + 2, NZ)
    bar = pltpu.get_barrier_semaphore()
    for dev in (xdev, ydev, cdev, {"x": 1 - x, "c": 1 - c}):
        signal(bar, dev)
    for k in range(1, NZ):
        signal(bar, {"z": lax.rem(z + k, NZ)})
    pl.semaphore_wait(bar, 4 + NZ - 1)


    def part(prefix, b):
        return getattr(R, prefix + b)

    def add_into(ref, *others):
        total = ref[...].astype(F32)
        for other in others:
            total = total + other.astype(F32)
        ref[...] = total.astype(BF)

    def column(kind):
        return (x, y) if kind == 0 else (1 - x, 1 - y)

    def z_copy(b, kind, k):
        n, (cx, cy), zt = GRADS.index(b), column(kind), lax.rem(z + k, NZ)
        return remote(part("g_", b).at[cx, zt, cy], part(("zr_", "zd_")[kind], b).at[k - 1],
                      R.zs.at[n, kind, k - 1], R.zrs.at[n, kind, k - 1], {"z": zt})

    def z_start(b, kind):
        for k in range(1, NZ):
            z_copy(b, kind, k).start()

    def z_landed(b, kind):
        ref = part(("zr_", "zd_")[kind], b)
        for k in range(NZ - 1):
            landed(ref.at[k], R.zrs.at[GRADS.index(b), kind, k])
        return [ref[k] for k in range(NZ - 1)]

    def wide(b):
        n = GRADS.index(b)
        if CORNER[b] == "x":
            return remote(part("g_", b).at[1 - x, :, y], part("px_", b), R.s1.at[n, 0], R.rx.at[n, 0], xdev)
        return remote(part("g_", b).at[x, :, 1 - y], part("py_", b), R.s1.at[n, 0], R.ry.at[n, 0], ydev)

    def narrow(b, k):
        n, zk = GRADS.index(b), lax.rem(z + k, NZ)
        if CORNER[b] == "x":
            return remote(part("g_", b).at[x, zk, 1 - y], part("py_", b).at[zk], R.s1.at[n, 1 + k], R.ry.at[n, zk], ydev)
        return remote(part("g_", b).at[1 - x, zk, y], part("px_", b).at[zk], R.s1.at[n, 1 + k], R.rx.at[n, zk], xdev)

    def corner_share(b):
        n = GRADS.index(b)
        return remote(part("g_", b).at[1 - x, z, 1 - y], part("pd_", b), R.s1.at[n, 1 + NZ], R.rd.at[n],
                      xdev if CORNER[b] == "x" else ydev)

    def corner_first(b):
        wide(b).start()
        for k in range(1, NZ):
            narrow(b, k).start()
        z_start(b, 1)

    def corner_out(b):
        add_into(part("g_", b).at[1 - x, z, 1 - y], *z_landed(b, 1))
        corner_share(b).start()

    def corner_in(b):
        corner_share(b).wait_recv()
        here = part("g_", b).at[x, z, 1 - y] if CORNER[b] == "x" else part("g_", b).at[1 - x, z, y]
        add_into(here, part("pd_", b)[...])
        narrow(b, 0).start()

    def corner_join(b):
        n = GRADS.index(b)
        px, py = part("px_", b), part("py_", b)
        wide(b).wait_recv()
        for k in range(NZ):
            if CORNER[b] == "x":
                landed(py.at[k], R.ry.at[n, k])
            else:
                landed(px.at[k], R.rx.at[n, k])

        @pl.loop(0, NZ)
        def _(k):
            add_into(part("g_", b).at[x, k, y], px[k], py[k])

        z_start(b, 0)

    def split(b):
        return part("g_", b).shape[3] // 48 * 16

    def first(b):
        n, h, g = GRADS.index(b), split(b), part("g_", b)
        return (
            remote(g.at[1 - x, :, :, 0:h], part("px_", b), R.s1.at[n, 0], R.rx.at[n, 0], xdev),
            remote(g.at[:, :, 1 - y, h:], part("py_", b), R.s1.at[n, 1], R.ry.at[n, 0], ydev),
        )

    def second(b):
        n, h, g = GRADS.index(b), split(b), part("g_", b)
        return (
            remote(g.at[x, :, 1 - y, 0:h], part("qy_", b), R.s2.at[n, 0], R.r2s.at[n, 0], ydev),
            remote(g.at[1 - x, :, y, h:], part("qx_", b), R.s2.at[n, 1], R.r2s.at[n, 1], xdev),
        )

    def plane_first(b):
        for cp in first(b):
            cp.start()

    def plane_second(b):
        h, g = split(b), part("g_", b)
        px, py = part("px_", b), part("py_", b)
        for cp in first(b):
            cp.wait_recv()

        @pl.loop(0, NZ)
        def _(k):
            for yy in range(NY):
                add_into(g.at[x, k, yy, 0:h], px[k, yy])
            for xx in range(2):
                add_into(g.at[xx, k, y, h:], py[xx, k])

        for cp in second(b):
            cp.start()

    def plane_join(b):
        h, g = split(b), part("g_", b)
        qx, qy = part("qx_", b), part("qy_", b)
        for cp in second(b):
            cp.wait_recv()

        @pl.loop(0, NZ)
        def _(k):
            add_into(g.at[x, k, y, 0:h], qy[k])
            add_into(g.at[x, k, y, h:], qx[k])

        z_start(b, 0)

    def out_copies(b):
        sem = R.out_sem.at[GRADS.index(b)]
        if b[:-1] in ("down", "up"):
            return [pltpu.make_async_copy(R.st_ffn, part("o_", b[:-1]).at[int(b[-1])], sem.at[0])]
        if b == "proj":
            rows = R.o_proj.shape[1]
            return [pltpu.make_async_copy(R.st_proj.at[n * rows : (n + 1) * rows], R.o_proj.at[n], sem.at[n]) for n in range(2)]
        places = ((1, 0), (1, 1)) if b == "qk1" else ((0, 0), (0, 1), (0, 2), (1, 2))
        return [pltpu.make_async_copy(R.st_qkv.at[p], R.o_qkv.at[p], sem.at[k]) for k, p in enumerate(places)]

    ffn_done = []

    def finish(b):
        if b[:-1] in ("down", "up"):
            if ffn_done:
                for cp in out_copies(ffn_done[-1]):
                    cp.wait()
            ffn_done.append(b)
        total = part("g_", b)[x, z, y].astype(F32)
        for other in z_landed(b, 0):
            total = total + other.astype(F32)
        if b[:-1] in ("down", "up"):
            R.st_ffn[...] = total
        elif b == "proj":
            R.st_proj[...] = total
        else:
            places = ((1, 0), (1, 1)) if b == "qk1" else ((0, 0), (0, 1), (0, 2), (1, 2))
            for k, p in enumerate(places):
                R.st_qkv[p] = total[:, k * head : (k + 1) * head]
        for cp in out_copies(b):
            cp.start()

    def sends_done(b):
        if b in CORNER:
            copies = [wide(b), corner_share(b)] + [narrow(b, k) for k in range(NZ)]
        else:
            copies = first(b) + second(b)
        for cp in copies:
            cp.wait_send()
        for kind in (0, 1) if b in CORNER else (0,):
            for k in range(1, NZ):
                z_copy(b, kind, k).wait_send()
        if not (b[:-1] in ("down", "up") and b != ffn_done[-1]):
            for cp in out_copies(b):
                cp.wait()


    def chip(core):
        return rows_at(core * half, half)

    def win(core):
        return rows_at(x * 128 + core * half, half)

    def swap(src, dst, n):
        return remote(src, dst, R.csend.at[n], R.crecv.at[n], cdev)

    def gain(layer, k):
        return R.vec[0, 14 + 2 * layer + k : 15 + 2 * layer + k, :]

    def note(row, value):
        R.small[row : row + 1, :] = value

    def norm_back(grad, g_row, hat, spread):
        scaled = grad * g_row
        first_mean = jnp.mean(scaled, 1, keepdims=True)
        second_mean = jnp.mean(scaled * hat, 1, keepdims=True)
        return spread * (scaled - first_mean - hat * second_mean)

    def ffn_norm(layer):
        need(layer, "yh2", "r2", "kp")
        grad, hat = R.dh[...], R.v_yh2[...].astype(F32)
        note(12 + 2 * layer + 1, jnp.sum(grad * hat, 0, keepdims=True))
        note(6 * layer + 5, jnp.sum(grad, 0, keepdims=True))
        dy = norm_back(grad, gain(layer, 1), hat, R.v_r2[...])
        R.dy[...] = dy
        df = dy * R.v_kp[1].astype(F32) * (1.0 / KEEP)
        note(6 * layer + 4, jnp.sum(df, 0, keepdims=True))
        R.dff[chip(c)] = df.astype(BF)
        here = R.dff.at[chip(c)]
        swap(here, here, 4 * layer).start()
        if layer == 1:
            load(0, "yh2", "r2")

    def ffn_wait(layer):
        here = R.dff.at[chip(c)]
        swap(here, here, 4 * layer).wait_send()
        landed(R.dff.at[chip(1 - c)], R.crecv.at[4 * layer])

    def as_block(value):
        return value.astype(BF).reshape(NZ, NY, -1, value.shape[1])

    def down_grad(layer, j):
        if j == 0:
            need(layer, "act")
        (R.g_down1 if layer else R.g_down0)[j] = as_block(contract(R.v_act[j], R.dff[...], 0, 0))
        if layer == 1 and j == 1:
            load(0, "act")

    def units_back(layer, j):
        if j == 0:
            need(layer, "gp")
            down_copy(layer).wait()
        total = jnp.zeros((1, width), F32)
        for core in range(2):
            rows = pl.ds(core * half, half)
            dact = contract(R.dff[rows], flat(R.w_down.at[j]), 1, 1)
            dhid = (dact * R.v_gp[j, rows].astype(F32)).astype(BF)
            R.v_gp[j, rows] = dhid
            total = total + jnp.sum(dhid.astype(F32), 0, keepdims=True)
        keep_row = jnp.where(c == 0, 1.0, 0.0)
        note(16 + 4 * layer + 2 * j, total * keep_row)
        note(16 + 4 * layer + 2 * j + 1, total * (1.0 - keep_row))
        if layer == 1 and j == 1:
            down_copy(0).start()

    def up_grad(layer, j):
        if j == 0:
            need(layer, "zf")
        (R.g_up1 if layer else R.g_up0)[j] = as_block(contract(R.v_zf[...], R.v_gp[j], 0, 0))
        if layer == 1 and j == 1:
            load(0, "zf")

    def mid_part(rows):
        return contract(R.v_gp[0, rows], flat(R.w_up.at[0]), 1, 1) + contract(R.v_gp[1, rows], flat(R.w_up.at[1]), 1, 1)

    def mid_give(layer):
        up_copy(layer).wait()
        R.send[...] = mid_part(chip(1 - c)).astype(BF)
        swap(R.send, R.rz, 4 * layer + 1).start()

    def mid_own(layer):
        R.dy[...] += mid_part(chip(c))

    def mid_norm(layer):
        need(layer, "yh1", "r1")
        swap(R.send, R.rz, 4 * layer + 1).wait()
        grad, hat = R.dy[...] + R.rz[...].astype(F32), R.v_yh1[...].astype(F32)
        note(12 + 2 * layer, jnp.sum(grad * hat, 0, keepdims=True))
        note(6 * layer + 3, jnp.sum(grad, 0, keepdims=True))
        dy = norm_back(grad, gain(layer, 0), hat, R.v_r1[...])
        R.dy[...] = dy
        da = dy * R.v_kp[0].astype(F32) * (1.0 / KEEP)
        note(6 * layer + 2, jnp.sum(da, 0, keepdims=True))
        R.daf[chip(c)] = da.astype(BF)
        here = R.daf.at[chip(c)]
        swap(here, here, 4 * layer + 2).start()
        if layer == 1:
            load(0, "yh1", "r1", "kp")

    def free_ffn(layer):
        up_copy(0).start()
        load(0, "gp")

    def proj_rows_back(layer):
        if layer == 1:
            proj_copy().wait()
        for j in range(2):
            value = R.w_proj[j].astype(F32)
            rows = value.shape[2] // 2
            value = value[:, :, layer * rows : (layer + 1) * rows].reshape(-1, value.shape[3])
            R.wo[j] = value.astype(BF)

    def proj_wait(layer):
        here = R.daf.at[chip(c)]
        swap(here, here, 4 * layer + 2).wait_send()
        landed(R.daf.at[chip(1 - c)], R.crecv.at[4 * layer + 2])

    def proj_back(layer):
        for j in range(2):
            for core in range(2):
                rows = pl.ds(core * half, half)
                R.datt[j, rows] = contract(R.daf[rows], R.wo[j], 1, 1).astype(BF)

    def proj_grad(layer):
        need(layer, "att")
        for j in range(2):
            grad = contract(R.v_att[j], R.daf[...], 0, 0)
            if layer == 1:
                R.dwo[j] = grad.astype(BF)
            else:
                both = [v.reshape(NZ * NY, -1, width) for v in (grad, R.dwo[j].astype(F32))]
                R.g_proj[j] = as_block(jnp.concatenate(both, 1).reshape(-1, width))
        if layer == 1:
            load(0, "att")

    def attend_back(layer, j):
        if j == 0:
            need(layer, "p", "q", "k", "v")
        lane = lax.broadcasted_iota(jnp.int32, (1, head), 1) // HEAD_DIM
        picks = [(lane == n).astype(F32) for n in range(head // HEAD_DIM)]
        count = len(picks)
        R.dk[...] = jnp.zeros_like(R.dk)
        R.dv[...] = jnp.zeros_like(R.dv)
        R.dq[...] = jnp.zeros_like(R.dq)

        @pl.loop(0, 4)
        def _(i):
            keys = rows_at((3 * (x + i) + 1) // 5 * 128, 384)
            mine = rows_at(i * 128, 128)
            kk = R.v_k[j, keys]
            qq, dd = R.v_q[j, mine], R.datt[j, mine]
            q3 = jnp.concatenate([qq * pick.astype(BF) for pick in picks], 0)
            d3 = jnp.concatenate([dd * pick.astype(BF) for pick in picks], 0)
            p3 = R.v_p[j, i]
            dp = contract(d3, R.v_v[j, keys], 1, 1)
            pf = p3.astype(F32)
            ds = (pf * (dp - jnp.sum(pf * dp, 1, keepdims=True))).astype(BF)
            R.dv[keys] += contract(p3, d3, 0, 0)
            R.dk[keys] += contract(ds, q3, 0, 0)
            dq = mm(ds, kk)
            total = dq[0:128] * picks[0]
            for n in range(1, count):
                total = total + dq[n * 128 : (n + 1) * 128] * picks[n]
            R.dq[rows_at(x * 128 + i * 128, 128)] = total * 0.125

        dq, dk, dv = (v[...].astype(BF).astype(F32) for v in (R.dq, R.dk, R.dv))
        R.dqk[j] = jnp.concatenate([dq, dk], 1).astype(BF)
        gap = jnp.zeros((dv.shape[0], 64), F32)
        R.dvp[j] = jnp.concatenate([dv, gap] if layer == 0 else [gap, dv], 1).astype(BF)
        own = jnp.where(c == 0, 1.0, 0.0)
        for row, value in ((0, dq), (1, dv)):
            line = jnp.sum(value, 0, keepdims=True)
            pair = [line * own, line * (1.0 - own)]
            zero = jnp.zeros((1, 2 * head), F32)
            if j == 0:
                note(6 * layer + row, jnp.concatenate(pair + [zero], 1))
            else:
                R.small[6 * layer + row : 6 * layer + row + 1, :] += jnp.concatenate([zero] + pair, 1)
        if layer == 1 and j == 1:
            load(0, "p", "q", "k", "v")

    def qkv_grad(layer, j):
        if j == 0:
            need(layer, "xw")
        gqk = as_block(contract(R.v_xw[...], R.dqk[j], 0, 0))
        gv = as_block(contract(R.v_xw[...], R.dvp[j], 0, 0))
        if layer == 1:
            R.g_qk1[j] = gqk
            R.g_last[j, :, :, :, 3 * head - 64 :] = gv
        else:
            R.g_last[j, :, :, :, 0 : 2 * head] = gqk
            R.g_last[j, :, :, :, 2 * head : 2 * head + 128] = gv[..., 0:128]
            R.g_last[j, :, :, :, 2 * head + 128 : 3 * head + 64] += gv[..., 128:]
        if layer == 1 and j == 1:
            load(0, "xw")

    def in_part(rows):
        total = None
        for j in range(2):
            w = R.w_qkv.at[j]
            wqk = w[:, :, :, 0 : 2 * head].reshape(width, 2 * head)
            wv = w[:, :, :, 2 * head :].reshape(width, head + 64)
            term = contract(R.dqk[j, rows], wqk, 1, 1) + contract(R.dvp[j, rows], wv, 1, 1)
            total = term if total is None else total + term
        return total

    def halo_copy(layer):
        return remote(R.hs, R.hr.at[layer, c], R.hsend.at[layer], R.hrecv.at[layer, c], {"x": 1 - x, "c": x})

    def in_halo(layer):
        for cp in qkv_copies(layer):
            cp.wait()
        R.hs[...] = in_part(rows_at((1 - x) * 512, 128)).astype(BF)
        halo_copy(layer).start()

    def in_give(layer):
        R.send[...] = in_part(win(1 - c)).astype(BF)
        swap(R.send, R.rh, 4 * layer + 3).start()

    def in_own(layer):
        R.dh[...] = R.dy[...] + in_part(win(c))
        if layer == 1:
            for again in qkv_copies(0):
                again.start()

    def in_sum(layer):
        swap(R.send, R.rh, 4 * layer + 3).wait()
        R.dh[...] += R.rh[...].astype(F32)

        @pl.when(c == 1 - x)
        def _():
            edge = rows_at(128 * c, 128)
            for core in range(2):
                landed(R.hr.at[layer, core], R.hrecv.at[layer, core])
                R.dh[edge] += R.hr[layer, core].astype(F32)

        halo_copy(layer).wait_send()
        if layer == 0:
            gx_copy.start()


    def small_copy(k):
        dev = (cdev, xdev, ydev, {"z": zp1}, {"z": zp2})[k]
        return remote(R.small, R.small_in.at[k], R.bs.at[k], R.br.at[k], dev)

    def small_give(k):
        small_copy(k).start()

    def small_sum(k):
        small_copy(k).wait()
        R.small[...] += R.small_in[k]


    total = R.seg.shape[1]
    number = lax.broadcasted_iota(jnp.int32, (SEGS, total), 0)
    before = (jnp.broadcast_to(R.seg[...], (SEGS, total)) < number).astype(F32)
    starts = jnp.sum(before, 1, keepdims=True).astype(jnp.int32)
    mine = lax.broadcasted_iota(jnp.int32, (SEGS, half), 1) + (2 * x + c) * half
    pick = (mine == starts).astype(F32)
    R.dh[...] = lax.dot_general(
        pick, R.gcls[...], (((0,), (0,)), ((), ())), precision=lax.Precision.HIGHEST, preferred_element_type=F32)

    gx_copy = pltpu.make_async_copy(R.dh, R.gx, R.gx_sem)
    def act(fn, *args):
        actions.append(functools.partial(fn, *args))

    actions = []
    for layer in range(2):
        act(ffn_norm, layer)
        act(ffn_wait, layer)
        for fn in (down_grad, units_back, up_grad):
            act(fn, layer, 0)
            act(fn, layer, 1)
        for fn in (mid_give, mid_own, mid_norm, proj_rows_back, proj_wait, proj_back, proj_grad):
            act(fn, layer)
        for fn in (attend_back, qkv_grad):
            act(fn, layer, 0)
            act(fn, layer, 1)
        for fn in (in_halo, in_give, in_own, in_sum):
            act(fn, layer)
    act(free_ffn, 1)
    for k in range(5):
        act(small_give, k)
    for k in range(5):
        act(small_sum, k)
    for b in GRADS:
        if b in CORNER:
            act(corner_first, b)
            for fn in (corner_out, corner_in, corner_join):
                act(fn, b)
        else:
            for fn in (plane_first, plane_second, plane_join):
                act(fn, b)
        act(finish, b)
    for step in BACKWARD_ORDER:
        actions[step]()
    R.o_small[...] = R.small[...]
    gx_copy.wait()
    for b in GRADS:
        sends_done(b)


def saved_shapes(half, width):
    head = width // 4
    return {
        "xw": ((640, width), BF),
        "q": ((2, 512, head), BF),
        "k": ((2, 640, head), BF),
        "v": ((2, 640, head), BF),
        "p": ((2, 4, 384, 384), BF),
        "att": ((2, 512, head), BF),
        "zf": ((512, width), BF),
        "gp": ((2, 512, width), BF),
        "act": ((2, 512, width), BF),
        "yh1": ((half, width), BF),
        "yh2": ((half, width), BF),
        "r1": ((half, 1), F32),
        "r2": ((half, 1), F32),
        "kp": ((2, half, width), BF),
    }


def run_forward(whole, wqkv, wout, up, down, b_in, biases, gains, pool_b, pairing, pool, tok, seg, drop):
    half, width = tok.shape
    rows = up.shape[1]
    cut = {n: up.shape[1:] for n in BLOCKS}
    cut["small"] = (32, 128)
    cut["qkv"] = (rows, 6 * wqkv.shape[3])
    cut["proj"] = (2 * wout.shape[1], width)
    saved = saved_shapes(half, width)
    head = width // 4
    dma = pltpu.SemaphoreType.DMA
    land = [(2, NZ, NY, *cut[n]) for n in BLOCKS]
    nb = len(BLOCKS)
    loss_outs, loss_scratch = loss_shapes(NZ * NY * SEGS, width)
    shape = jax.ShapeDtypeStruct
    outs = [shape(s, BF) for s in land[1:]]
    outs.append(shape((2, 32, width), F32))
    if whole:
        outs += loss_outs
    else:
        outs += [
            shape((NZ, NY, *pool.shape), BF),
            shape((NZ, NY, *cut["small"]), BF),
            shape((NZ, NY, SEGS, width), BF),
        ]
    outs += [shape((2, *s), t) for s, t in saved.values()]
    names = forward_out(whole)
    out_specs = [VMEM if n in LOSS_OUT + ("o_cls",) else ANY for n in names]
    scratch = [pltpu.VMEM(s, BF) for s in land]
    scratch += [
        pltpu.VMEM((NZ, NY, *pool.shape), BF),
        pltpu.VMEM((4, SEGS, width), BF),
        pltpu.VMEM((NZ, NY, SEGS, width), BF),
    ]
    scratch += [pltpu.VMEM((2, *s), t) for s, t in saved.values()]
    scratch += [
        pltpu.VMEM(drop.shape, drop.dtype),
        pltpu.VMEM((4, 128, 384), F32),
        pltpu.VMEM((2, 2, head, width), BF),
        pltpu.VMEM((2, 32, width), F32),
        pltpu.VMEM((2, 32, head), F32),
        pltpu.VMEM((half, width), F32),
        pltpu.VMEM((half, width), F32),
    ]
    scratch += [pltpu.VMEM((2, half, width), BF)] * 4
    scratch += [
        dma((nb, 4 * NZ)), dma((nb, 2 * NZ)), dma((nb, 2 * NZ)), dma((nb, 2, NZ, NY)), dma((nb,)),
        dma((3 * NZ,)), dma((NZ, NY)), dma, dma((2,)),
        dma((8,)), dma((8,)), dma((2, 2)), dma((2,)), dma, dma((len(SAVED), 2)), dma((nb,)), dma((3,)),
        dma((3,)), dma((3,)), dma((NZ * NY,)), dma((NZ * NY,)),
        pltpu.VMEM(cut["small"], F32),
        pltpu.VMEM(cut["small"], BF),
        pltpu.VMEM(cut["qkv"], BF),
        pltpu.VMEM(cut["proj"], BF),
        pltpu.VMEM((NZ * NY * SEGS, width), BF),
    ]
    if whole:
        scratch += loss_scratch
    res = pl.pallas_call(
        functools.partial(forward_kernel, whole),
        out_shape=outs,
        in_specs=[VMEM, VMEM, ANY, ANY] + [VMEM] * 5 + [ANY, VMEM, VMEM, ANY],
        out_specs=out_specs,
        scratch_shapes=scratch,
        compiler_params=pltpu.CompilerParams(collective_id=1, has_side_effects=True, vmem_limit_bytes=60 << 20),
        name="forward",
    )(wqkv, wout, up, down, b_in, biases, gains, pool_b, pairing, pool, tok, seg, drop)
    return dict(zip(names, res))


def run_backward(weights, saved, vec, seg, gcls):
    width = vec.shape[2]
    half = saved[SAVED.index("yh1")].shape[1]
    head = width // 4
    dma = pltpu.SemaphoreType.DMA
    by_name = dict(zip(BLOCKS[1:], weights))
    rows, wide = by_name["up0"].shape[3:]
    thin = by_name["proj"].shape[3]
    cut = {n: (rows, wide) for n in GRADS}
    cut["proj"] = (thin, width)
    cut["qk1"] = (rows, 2 * head)
    cut["last"] = (rows, 4 * head)
    nb = len(GRADS)
    shape = jax.ShapeDtypeStruct
    outs = [
        shape((half, width), F32),
        shape((2, rows, wide), F32),
        shape((2, rows, wide), F32),
        shape((2, thin // 2, width), F32),
        shape((2, 3, rows, head), F32),
        shape((24, width), F32),
    ]

    def low(*dims):
        return pltpu.VMEM(dims, BF)

    def full(*dims):
        return pltpu.VMEM(dims, F32)

    scratch = [low(2, NZ, NY, *cut[n]) for n in GRADS]
    scratch += [low(NZ - 1, *cut[n]) for n in GRADS]
    split = {n: cut[n][0] // 48 * 16 for n in GRADS}
    for n in GRADS:
        r, w = cut[n]
        scratch.append(low(NZ, r, w) if n in CORNER else low(NZ, NY, split[n], w))
    for n in GRADS:
        r, w = cut[n]
        scratch.append(low(NZ, r, w) if n in CORNER else low(2, NZ, r - split[n], w))
    for n in GRADS:
        r, w = cut[n]
        if n in CORNER:
            scratch += [low(r, w), low(NZ - 1, r, w)]
        else:
            scratch += [low(NZ, r - split[n], w), low(NZ, split[n], w)]
    scratch += [full(rows, wide), full(*cut["proj"]), full(2, 3, rows, head)]
    scratch += [pltpu.VMEM(s, t) for s, t in saved_shapes(half, width).values()]
    scratch += [
        low(2, NZ, NY, rows, 3 * head + 64),
        low(*by_name["proj"].shape),
        low(*by_name["up0"].shape),
        low(*by_name["down0"].shape),
        low(2, head, width),
        low(512, width),
        low(512, width),
        low(half, width),
        low(half, width),
        low(half, width),
        low(128, width),
        low(2, 2, 128, width),
        low(2, 512, head),
        full(640, head),
        full(640, head),
        full(640, head),
        low(2, 640, 2 * head),
        low(2, 640, head + 64),
        low(2, head, width),
        full(half, width),
        full(half, width),
        full(24, width),
        full(5, 24, width),
    ]
    scratch += [
        dma((5,)), dma((len(SAVED),)), dma((nb, 4)), dma((8,)), dma((8,)), dma((2,)), dma((2, 2)),
        dma((nb, NZ + 2)), dma((nb, NZ)), dma((nb, NZ)), dma((nb,)), dma((nb, 2)), dma((nb, 2)),
        dma((nb, 2, NZ - 1)), dma((nb, 2, NZ - 1)), dma((5,)), dma((5,)), dma,
    ]
    return pl.pallas_call(
        backward_kernel,
        out_shape=outs,
        in_specs=[ANY] * (len(weights) + len(saved)) + [VMEM] * 3,
        out_specs=[ANY] * 5 + [VMEM],
        scratch_shapes=scratch,
        compiler_params=pltpu.CompilerParams(collective_id=2, has_side_effects=True, vmem_limit_bytes=63 << 20),
        name="backward",
    )(*weights, *saved, vec, seg, gcls)


def hand_over_kernel(*refs):
    ins, outs, held, sem = refs[:11], refs[11:24], refs[24:30], refs[30]
    loads = [pltpu.make_async_copy(ins[k], held[k], sem.at[0, k]) for k in range(6)]
    moves = [pltpu.make_async_copy(held[k], outs[k], sem.at[1, k]) for k in range(6)]
    for cp in loads:
        cp.start()
    for k in range(6, 10):
        outs[k][...] = ins[k][...]
    sums = ins[10]
    z, y, x, c = position()
    m, dp = 2 * x + c, z * NY + y
    b_in, biases, gains = outs[10:]
    width = sums.shape[1]
    thin, part = biases.shape[2], b_in.shape[1]
    turned = pltpu.roll(sums[0:16], lax.rem(width - (dp * part + m * thin), width), 1)
    for layer in range(2):
        for k in range(6):
            biases[k, layer : layer + 1] = turned[6 * layer + k : 6 * layer + k + 1, 0:thin]
        gains[layer] = turned[12 + 2 * layer : 14 + 2 * layer, 0:thin]
    turned = pltpu.roll(sums[16:24], lax.rem(width - dp * part, width), 1)
    for layer in range(2):
        total = jnp.zeros((1, part), F32)
        for k in range(4):
            total = total + turned[4 * layer + k : 4 * layer + k + 1, 0:part] * jnp.where(m == k, 1.0, 0.0)
        b_in[layer : layer + 1] = total
    for load, move in zip(loads, moves):
        load.wait()
        move.start()
    for cp in moves:
        cp.wait()


def hand_over(large, small, sums):
    shape = jax.ShapeDtypeStruct
    width = sums.shape[1]
    part = width // (NZ * NY)
    outs = [shape(v.shape, v.dtype) for v in large + small]
    outs += [shape((2, part), F32), shape((6, 2, part // 4), F32), shape((2, 2, part // 4), F32)]
    return pl.pallas_call(
        hand_over_kernel,
        out_shape=outs,
        in_specs=[ANY] * len(large) + [VMEM] * (len(small) + 1),
        out_specs=[ANY] * len(large) + [VMEM] * (len(small) + 3),
        scratch_shapes=[pltpu.VMEM(v.shape, v.dtype) for v in large] + [pltpu.SemaphoreType.DMA((2, len(large)))],
        name="hand_over",
    )(*large, *small, sums)


def per_device(tokens_in, segments, pairing, drop_masks, w_qkv, w_out, w_in, w_back, b_in, biases,
               gains, pool_w, pool_b):
    inner = lax.axis_size("g")
    layers = w_qkv.shape[0]
    width = tokens_in.shape[1]
    z, y, x, c = position()
    m = 2 * x + c
    dp = (z * NY + y) * inner + lax.axis_index("g")

    def group(arr, dim):
        return arr if inner == 1 else lax.all_gather(arr, "g", axis=dim, tiled=True)

    w_qkv, w_out, w_in, w_back = group(w_qkv, 2), group(w_out, 1), group(w_in, 1), group(w_back, 1)
    b_in, biases, gains = group(b_in, 1), group(biases, 2), group(gains, 2)
    pool_w, pool_b, pairing = group(pool_w, 0), group(pool_b, 0), group(pairing, 0)
    rows = w_in.shape[1]
    named = run_forward(
        inner == 1, w_qkv, w_out, w_in, w_back, b_in, jnp.transpose(biases, (1, 0, 2)), gains, pool_b[None], pairing[None], pool_w,
        tokens_in, segments, drop_masks)
    if inner == 1:
        loss, align, unif, grad_pool_w, grad_pool_b, gcls = (named[n] for n in LOSS_OUT)
    else:
        cls = named["o_cls"].reshape(NZ * NY, SEGS, width)
        cls = lax.all_gather(cls, "g", axis=1, tiled=True).reshape(-1, width)
        loss, align, unif, grad_pool_w, grad_pool_b, gcls = pooled_loss(
            cls, named["o_pool"], named["o_vec"], named["o_piece"])
    weights = [named["o_" + n] for n in BLOCKS[1:]]
    saved = [named["o_" + n] for n in SAVED]
    grad_x, down, up, proj, qkv, sums = run_backward(weights, saved, named["o_vec"], segments, gcls)

    if inner == 1:
        large = [grad_x, qkv, proj, up, down, grad_pool_w]
        small = [loss, align, unif, grad_pool_b]
        res = hand_over(large, small, sums)
        grad_x, qkv, proj, up, down, grad_pool_w, loss, align, unif, grad_pool_b, out_b_in, out_biases, out_gains = res
        return (
            loss[0], align[0], unif[0], grad_x, qkv, proj, up, down, out_b_in,
            jnp.transpose(out_biases, (1, 0, 2)), out_gains, grad_pool_w, grad_pool_b[0],
        )

    def spread(values, dim):
        return lax.psum_scatter(values, "g", scatter_dimension=dim, tiled=True)

    sums = lax.psum(sums, "g")
    thin = rows // (4 * inner)
    here = lax.dynamic_slice_in_dim(sums[:16], dp * 4 * thin + m * thin, thin, 1)
    up_sums = sums[16:24].reshape(layers, 4 * width)
    n_up = rows // inner
    out_b_in = lax.dynamic_slice_in_dim(up_sums, m * width + dp * n_up, n_up, 1)
    n_pool = pool_w.shape[0] // inner
    g = lax.axis_index("g")
    grad_pool_w = lax.dynamic_slice_in_dim(grad_pool_w, g * n_pool, n_pool, 0)
    return (
        loss[0],
        align[0],
        unif[0],
        grad_x,
        spread(qkv, 2),
        spread(proj, 1),
        spread(up, 1),
        spread(down, 1),
        out_b_in,
        here[:12].reshape(layers, 6, thin),
        here[12:].reshape(layers, 2, thin),
        grad_pool_w,
        grad_pool_b[0],
    )


def solution(mesh):
    count = mesh.shape["dp"]
    fine = Mesh(
        mesh.devices.reshape(NZ, NY, count // (NZ * NY), 2, 2), ("z", "y", "g", "x", "c")
    )
    dp, mp = ("z", "y", "g"), ("x", "c")
    in_specs = (
        P(dp + mp, None),
        P(dp, None),
        P(dp),
        P(None, None, dp + mp, None),
        P(None, None, dp, mp),
        P(None, mp + dp, None),
        P(None, dp, mp),
        P(None, mp + dp, None),
        P(None, mp + dp),
        P(None, None, dp),
        P(None, None, dp),
        P(dp, None),
        P(dp),
    )
    out_specs = (
        P(dp),
        P(dp),
        P(dp),
        P(dp + mp, None),
        P(None, None, dp, mp),
        P(None, mp + dp, None),
        P(None, dp, mp),
        P(None, mp + dp, None),
        P(None, mp + dp),
        P(None, None, dp + mp),
        P(None, None, dp + mp),
        P(dp, None),
        P(dp),
    )
    return jax.shard_map(
        per_device, mesh=fine, in_specs=in_specs, out_specs=out_specs, check_vma=False
    )
```

```python
import functools
from typing import NamedTuple

import jax
import jax.numpy as jnp
from jax import lax
from jax.experimental import pallas as pl
from jax.experimental.pallas import tpu as pltpu
from jax.sharding import Mesh
from jax.sharding import PartitionSpec as P

HEAD_DIM = 64
SEGS = 16
TEMP = 0.05
EPS = 1e-06
KEEP = 0.9
MESH = pl.DeviceIdType.MESH
ANY = pl.BlockSpec(memory_space=pl.ANY)
VMEM = pl.BlockSpec(memory_space=pltpu.VMEM)
BF = jnp.bfloat16
F32 = jnp.float32
NZ = 4
NY = 2


class Names:
    def __init__(self, names, refs):
        for name, ref in zip(names, refs, strict=True):
            setattr(self, name, ref)


def contract(left_side, right_side, left_dim, right_dim):
    return lax.dot_general(
        left_side,
        right_side,
        (((left_dim,), (right_dim,)), ((), ())),
        preferred_element_type=F32,
    )


def mm(a, b):
    return jnp.dot(a, b, preferred_element_type=F32)


def position():
    return tuple(lax.axis_index(name) for name in ("z", "y", "x", "c"))


def signal(sem, device):
    pl.semaphore_signal(sem, inc=1, device_id=device, device_id_type=MESH)


def remote(src, dst, send_sem, recv_sem, device):
    return pltpu.make_async_remote_copy(
        src_ref=src,
        dst_ref=dst,
        send_sem=send_sem,
        recv_sem=recv_sem,
        device_id=device,
        device_id_type=MESH,
    )


def landed(ref, sem):
    pltpu.make_async_copy(ref, ref, sem).wait()


def rows_at(start, count):
    return pl.ds(pl.multiple_of(start, 128), count)


def flat(ref):
    value = ref[...]
    return value.reshape(-1, value.shape[-1])


class ForwardArgs(NamedTuple):
    wqkv: object
    wout: object
    up: object
    down: object
    b_in: object
    biases: object
    gains: object
    pool_b: object
    pairing: object
    pool: object
    tok: object
    seg: object
    drop: object


class ForwardScratch(NamedTuple):
    keep: object
    bias: object
    wo: object
    vec: object
    qv: object
    h: object
    z: object
    sa: object
    ra: object
    sf: object
    rf: object
    zsend: object
    xsend: object
    ysend: object
    recv: object
    own_sem: object
    pool_send: object
    pool_recv: object
    pool_own: object
    pool_core: object
    core_send: object
    core_recv: object
    halo_send: object
    halo_recv: object
    drop_sem: object
    out_sem: object
    w_sem: object
    misc_sem: object
    s1: object
    r1s: object
    s2: object
    r2s: object
    wide: object
    sm: object
    sq: object
    sp: object
    cls: object
    pick: object


SMALL, QKV, PROJ, UP0, DOWN0, UP1, DOWN1 = range(7)
BLOCKS = ("small", "qkv", "proj", "up0", "down0", "up1", "down1")
SAVED = ("xw", "q", "k", "v", "p", "att", "zf", "gp", "act", "yh1", "yh2", "r1", "r2", "kp")
FWD_IN = ForwardArgs._fields
LOSS_OUT = ("loss", "align", "unif", "gw", "gb", "gcls")
LOSS_SCR = ("u", "nb", "rn", "dn", "dpre", "table")


def forward_out(whole):
    after = LOSS_OUT if whole else ("o_pool", "o_piece", "o_cls")
    return tuple("o_" + n for n in BLOCKS[1:]) + ("o_vec",) + after + tuple("o_" + n for n in SAVED)


FWD_SCR = (
    tuple("w_" + n for n in BLOCKS) + ("w_pool", "cls_part", "cls_all") + SAVED
    + ForwardScratch._fields
)


FORWARD_ORDER = (
    0, 6, 1, 3, 4, 39, 73, 5, 67, 45, 44, 14, 2, 17, 18, 43, 52, 19, 15, 20, 68, 21, 16, 22, 36, 47, 40, 38,
    58, 37, 59, 69, 42, 41, 35, 51, 23, 26, 27, 53, 32, 60, 55, 24, 7, 33, 70, 29, 71, 28, 74, 8, 77, 78, 56,
    79, 61, 57, 46, 80, 81, 9, 75, 62, 25, 63, 82, 72, 83, 30, 10, 11, 54, 34, 84, 85, 86, 49, 87, 48, 64, 88,
    65, 31, 89, 90, 91, 50, 92, 66, 93, 94, 12, 95, 13, 96, 97, 98, 76,
)


def forward_kernel(whole, *refs):
    R = Names(FWD_IN + forward_out(whole) + FWD_SCR + (LOSS_SCR if whole else ()), refs)
    z, y, x, c = position()
    up, down = z < NZ - 1, z > 0
    xdev, ydev, cdev, xcdev = {"x": 1 - x}, {"y": 1 - y}, {"c": 1 - c}, {"x": 1 - x, "c": 1 - c}
    half = R.tok.shape[0]
    ins = [R.sm, R.sq, R.sp, R.up.at[0], R.down.at[0], R.up.at[1], R.down.at[1]]
    lands = [getattr(R, "w_" + n) for n in BLOCKS]

    peers = [(k * NY + flip, k, flip) for k in range(NZ) for flip in range(NY) if k or flip]

    def peer(k, flip):
        return {"z": lax.rem(z + k, NZ), "y": y if flip == 0 else 1 - y}

    R.wide[...] = jnp.zeros_like(R.wide)
    n = R.b_in.shape[1]
    row = 0
    biases = [R.biases[k] for k in range(R.biases.shape[0])]
    shifts = [value[layer : layer + 1] for layer in range(2) for value in biases]
    for value in (R.b_in[...], *shifts, R.gains[0], R.gains[1], R.pool_b[...]):
        R.wide[row : row + value.shape[0], 0:n] = value.astype(F32)
        row += value.shape[0]
    pair = R.pairing[...]
    R.wide[row : row + 1, 0 : pair.shape[1]] = (pair // 32).astype(F32)
    R.wide[row + 1 : row + 2, 0 : pair.shape[1]] = lax.rem(pair, 32).astype(F32)
    R.sm[...] = R.wide[...].astype(BF)
    parts = [R.wqkv[layer, k].astype(F32) for layer, k in ((0, 0), (0, 1), (1, 0), (1, 1), (0, 2), (1, 2))]
    R.sq[...] = jnp.concatenate(parts, 1).astype(BF)
    R.sp[...] = jnp.concatenate([R.wout[0].astype(F32), R.wout[1].astype(F32)], 0).astype(BF)

    bar = pltpu.get_barrier_semaphore()
    for dev in (xdev, cdev, xcdev):
        signal(bar, dev)
    for _, k, flip in peers:
        signal(bar, peer(k, flip))
    drop = pltpu.make_async_copy(R.drop, R.keep, R.drop_sem)
    drop.start()
    R.xw[0, rows_at(x * 128 + c * half, half)] = R.tok[...]
    R.h[...] = R.tok[...].astype(F32)
    pl.semaphore_wait(bar, 3 + len(peers))


    def copy(b, src, slot, device, sem):
        return remote(src, lands[b].at[slot], sem, R.recv.at[(b, *slot)], device)

    def arrived(b, slot):
        landed(lands[b].at[slot], R.recv.at[(b, *slot)])

    def by_z(b):
        return b in (PROJ, UP0, DOWN0, UP1)

    def over_y(b):
        return b in (SMALL, UP0, UP1, DOWN1)

    def sideways(b, src, slot, k):
        copy(b, src, slot, xdev, R.xsend.at[b, k]).start()
        copy(b, src, slot, ydev, R.ysend.at[b, k]).start()

    def launch(b):
        src, mine = ins[b], (x, z, y)
        pl.when(up)(lambda: copy(b, src, mine, {"z": z + 1}, R.zsend.at[b, 0]).start())
        pl.when(down)(lambda: copy(b, src, mine, {"z": z - 1}, R.zsend.at[b, 1]).start())
        sideways(b, src, mine, 0)
        pltpu.make_async_copy(src, lands[b].at[mine], R.own_sem.at[b]).start()

    def z_relay(b, d):
        @pl.when(z >= d)
        def _():
            slot = (x, z - d, y)
            arrived(b, slot)
            pl.when(up)(lambda: copy(b, lands[b].at[slot], slot, {"z": z + 1}, R.zsend.at[b, 2 * d]).start())
            sideways(b, lands[b].at[slot], slot, NZ - d)

        @pl.when(z < NZ - d)
        def _():
            slot = (x, z + d, y)
            arrived(b, slot)
            pl.when(down)(lambda: copy(b, lands[b].at[slot], slot, {"z": z - 1}, R.zsend.at[b, 2 * d + 1]).start())
            sideways(b, lands[b].at[slot], slot, d)

    def xy_relay(b, k):
        zp = lax.rem(z + k, NZ)
        sx, sy = (1 - x, zp, y), (x, zp, 1 - y)
        if over_y(b):
            arrived(b, sx)
            copy(b, lands[b].at[sx], sx, ydev, R.ysend.at[b, NZ + k]).start()
        else:
            arrived(b, sy)
            copy(b, lands[b].at[sy], sy, xdev, R.xsend.at[b, NZ + k]).start()

    def corner_launch(b):
        slot = (1 - x, z, 1 - y)
        arrived(b, slot)
        pl.when(up)(lambda: copy(b, lands[b].at[slot], slot, {"z": z + 1}, R.zsend.at[b, 2 * NZ]).start())
        pl.when(down)(lambda: copy(b, lands[b].at[slot], slot, {"z": z - 1}, R.zsend.at[b, 2 * NZ + 1]).start())

    def corner_relay(b, d):
        @pl.when(z >= d)
        def _():
            slot = (1 - x, z - d, 1 - y)
            arrived(b, slot)
            pl.when(up)(lambda: copy(b, lands[b].at[slot], slot, {"z": z + 1}, R.zsend.at[b, 2 * NZ + 2 * d]).start())

        @pl.when(z < NZ - d)
        def _():
            slot = (1 - x, z + d, 1 - y)
            arrived(b, slot)
            pl.when(down)(lambda: copy(b, lands[b].at[slot], slot, {"z": z - 1}, R.zsend.at[b, 2 * NZ + 2 * d + 1]).start())

    def complete(b):
        relays = 1 if by_z(b) else NZ
        for k in range(NZ):
            zp = lax.rem(z + k, NZ)
            if k >= relays or not over_y(b):
                arrived(b, (1 - x, zp, y))
            if k >= relays or over_y(b):
                arrived(b, (x, zp, 1 - y))
            if not by_z(b):
                arrived(b, (1 - x, zp, 1 - y))
        pltpu.make_async_copy(ins[b], lands[b].at[x, z, y], R.own_sem.at[b]).wait()
        if b != SMALL:
            w_copy(b).start()

    def sends_done(b):
        src, mine = ins[b], (x, z, y)
        for k in range(NZ):
            copy(b, src, mine, xdev, R.xsend.at[b, k]).wait_send()
            copy(b, src, mine, ydev, R.ysend.at[b, k]).wait_send()
        for k in range(1 if by_z(b) else NZ):
            if over_y(b):
                copy(b, src, mine, ydev, R.ysend.at[b, NZ + k]).wait_send()
            else:
                copy(b, src, mine, xdev, R.xsend.at[b, NZ + k]).wait_send()
        for d in range(NZ):
            for base in (0, 2 * NZ) if by_z(b) else (0,):
                pl.when(up & (z >= d))(lambda: copy(b, src, mine, {"z": z + 1}, R.zsend.at[b, base + 2 * d]).wait_send())
                pl.when(down & (z < NZ - d))(lambda: copy(b, src, mine, {"z": z - 1}, R.zsend.at[b, base + 2 * d + 1]).wait_send())

    prow = R.pool.shape[0] // 2
    pool_rows = pl.ds(pl.multiple_of(c * prow, 16), prow)

    def pool_slot(zp, yp):
        return R.w_pool.at[zp, yp, pool_rows]

    def pool_copy(src, zp, yp, device, k):
        return remote(src, pool_slot(zp, yp), R.pool_send.at[k], R.pool_recv.at[zp, yp], device)

    def pool_launch():
        src = R.pool.at[pool_rows]
        pl.when(up)(lambda: pool_copy(src, z, y, {"z": z + 1}, 0).start())
        pl.when(down)(lambda: pool_copy(src, z, y, {"z": z - 1}, 1).start())
        pool_copy(src, z, y, ydev, 2 * NZ).start()
        pltpu.make_async_copy(src, pool_slot(z, y), R.pool_own).start()

    def pool_relay(d):
        @pl.when(z >= d)
        def _():
            here = pool_slot(z - d, y)
            landed(here, R.pool_recv.at[z - d, y])
            pl.when(up)(lambda: pool_copy(here, z - d, y, {"z": z + 1}, 2 * d).start())
            pool_copy(here, z - d, y, ydev, 2 * NZ + NZ - d).start()

        @pl.when(z < NZ - d)
        def _():
            here = pool_slot(z + d, y)
            landed(here, R.pool_recv.at[z + d, y])
            pl.when(down)(lambda: pool_copy(here, z + d, y, {"z": z - 1}, 2 * d + 1).start())
            pool_copy(here, z + d, y, ydev, 2 * NZ + d).start()

    def pool_core():
        halves = R.w_pool.at[:, :, pool_rows]
        return remote(halves, halves, R.pool_core.at[0], R.pool_core.at[1], cdev)

    def pool_swap():
        pltpu.make_async_copy(R.pool.at[pool_rows], pool_slot(z, y), R.pool_own).wait()
        for k in range(NZ):
            zp = lax.rem(z + k, NZ)
            landed(pool_slot(zp, 1 - y), R.pool_recv.at[zp, 1 - y])
        pool_core().start()

    def pool_done():
        there = R.w_pool.at[:, :, pl.ds(pl.multiple_of((1 - c) * prow, 16), prow)]
        landed(there, R.pool_core.at[1])
        pool_core().wait_send()
        src = R.pool.at[pool_rows]
        for d in range(NZ):
            pl.when(up & (z >= d))(lambda: pool_copy(src, z, y, {"z": z + 1}, 2 * d).wait_send())
            pl.when(down & (z < NZ - d))(lambda: pool_copy(src, z, y, {"z": z - 1}, 2 * d + 1).wait_send())
            pool_copy(src, z, y, ydev, 2 * NZ + d).wait_send()
        for cp in misc_copies():
            cp.start()


    def win(core):
        return rows_at(x * 128 + core * half, half)

    def chip(core):
        return rows_at(core * half, half)

    def swap(src, dst, n):
        return remote(src, dst, R.core_send.at[n], R.core_recv.at[n], cdev)

    def rows_swap(layer):
        here = R.xw.at[layer, win(c)]
        return swap(here, here, 4 * layer)

    def edge_copies(layer):
        src = R.xw.at[layer, rows_at(x * 128 + c * half + 128 * c, 128)]
        dst = R.xw.at[layer, rows_at(x * 512, 128)]
        return [
            remote(src, dst, R.halo_send.at[layer, i], R.halo_recv.at[layer], dev)
            for i, dev in enumerate(({"x": 1 - x, "c": c}, {"x": 1 - x, "c": 1 - c}))
        ]

    def send_rows(layer):
        rows_swap(layer).start()

        @pl.when(c == 1 - x)
        def _():
            for cp in edge_copies(layer):
                cp.start()

    def partner_rows_here(layer):
        landed(R.xw.at[layer, win(1 - c)], R.core_recv.at[4 * layer])

    def edge_here(layer):
        landed(R.xw.at[layer, rows_at((1 - x) * 512, 128)], R.halo_recv.at[layer])


    def vec(layer, k):
        return R.vec[0, 2 + 6 * layer + k : 3 + 6 * layer + k, :]

    def gain(layer, k):
        return R.vec[0, 14 + 2 * layer + k : 15 + 2 * layer + k, :]

    def spread_params():
        width = R.vec.shape[2]
        part = width // (NZ * NY)
        lane = lax.broadcasted_iota(jnp.int32, (128, width), 0)
        col = lax.broadcasted_iota(jnp.int32, (128, width), 1)
        for j in range(2):
            total = jnp.zeros((R.vec.shape[1], width), F32)
            for dp in range(NZ * NY):
                place = ((lane < part) & (col == lane + dp * part)).astype(F32).astype(BF)
                total = total + mm(R.w_small[j, dp // NY, dp % NY], place)
            R.vec[j] = total
        head = R.qv.shape[2]
        lane = lax.broadcasted_iota(jnp.int32, (width, head), 0)
        col = lax.broadcasted_iota(jnp.int32, (width, head), 1)
        low = R.vec[0].astype(BF)
        for j in range(2):
            place = (lane == col + (2 * j + c) * head).astype(F32).astype(BF)
            R.qv[j] = mm(low, place)

    def masks():
        total = R.seg.shape[1]
        number = lax.broadcasted_iota(jnp.int32, (SEGS, total), 0)
        before = (jnp.broadcast_to(R.seg[...], (SEGS, total)) < number).astype(F32)
        starts = jnp.sum(before, 1, keepdims=True).astype(jnp.int32)
        own = lax.broadcasted_iota(jnp.int32, (SEGS, half), 1) + (2 * x + c) * half
        R.pick[...] = (own == starts).astype(F32).astype(BF)
        for i in range(4):
            mine = R.seg[0:1, rows_at(x * 512 + i * 128, 128)]
            start = (3 * (x + i) + 1) // 5 * 128
            keys = R.seg[0:1, rows_at(x * 384 + start, 384)]
            column = jnp.transpose(jnp.broadcast_to(mine, (128, 128)))
            for t in range(3):
                same = column == jnp.broadcast_to(keys[:, t * 128 : t * 128 + 128], (128, 128))
                R.bias[i, :, t * 128 : t * 128 + 128] = jnp.where(same, 0.0, -1000000000.0)

    def proj_rows():
        for layer in range(2):
            for j in range(2):
                value = R.w_proj[j].astype(F32)
                rows = value.shape[2] // 2
                value = value[:, :, layer * rows : (layer + 1) * rows].reshape(-1, value.shape[3])
                R.wo[layer, j] = value.astype(BF)

    def project(layer, wrow, count, crow):
        xx = R.xw[layer, wrow]
        head = R.q.shape[3]
        for j in range(2):
            w = R.w_qkv.at[j]
            wqk = w[:, :, :, layer * 2 * head : (layer + 1) * 2 * head].reshape(-1, 2 * head)
            yqk = mm(xx, wqk)
            if crow is not None:
                bq = R.qv[j, 2 + 6 * layer : 3 + 6 * layer, :]
                R.q[layer, j, crow] = (yqk[:, :head] + bq).astype(BF) * jnp.asarray(0.125, BF)
            R.k[layer, j, wrow] = yqk[:, head:].astype(BF)
            bv = R.qv[j, 3 + 6 * layer : 4 + 6 * layer, :]
            if layer == 0:
                yv = mm(xx, w[:, :, :, 4 * head : 5 * head].reshape(-1, head))
            else:
                yv = mm(xx, w[:, :, :, 5 * head - 64 : 6 * head].reshape(-1, head + 64))[:, 64:]
            R.v[layer, j, wrow] = (yv + bv).astype(BF)

    def attend(layer, j):
        head = R.q.shape[3]
        lane = lax.broadcasted_iota(jnp.int32, (1, head), 1) // HEAD_DIM
        picks = [(lane == n).astype(F32) for n in range(head // HEAD_DIM)]
        count = len(picks)

        @pl.loop(0, 4)
        def _(i):
            keys = rows_at((3 * (x + i) + 1) // 5 * 128, 384)
            mine = rows_at(i * 128, 128)
            qq = R.q[layer, j, mine]
            q3 = jnp.concatenate([qq * pick.astype(BF) for pick in picks], 0)
            scores = contract(q3, R.k[layer, j, keys], 1, 1)
            bias = R.bias[i]
            scores = scores.reshape(count, 128, 384) + bias[None]
            peak = jnp.max(scores, -1, keepdims=True)
            e = jnp.exp(scores - peak)
            p = (e * (1.0 / jnp.sum(e, -1, keepdims=True))).astype(BF).reshape(count * 128, 384)
            R.p[layer, j, i] = p
            o = mm(p, R.v[layer, j, keys])
            total = o[0:128] * picks[0]
            for n in range(1, count):
                total = total + o[n * 128 : (n + 1) * 128] * picks[n]
            R.att[layer, j, mine] = total.astype(BF)

        if j == 1:
            save(layer, "p", "att")

    def proj_part(layer, rows):
        return mm(R.att[layer, 0, rows], R.wo[layer, 0]) + mm(R.att[layer, 1, rows], R.wo[layer, 1])

    def norm(value, g, s):
        center = jnp.mean(value, 1, keepdims=True)
        spread = lax.rsqrt(jnp.mean(value * value, 1, keepdims=True) - center * center + EPS)
        hat = (value - center) * spread
        return hat * g + s, hat, spread

    def attention_give(layer):
        R.sa[layer] = proj_part(layer, chip(1 - c)).astype(BF)
        swap(R.sa.at[layer], R.ra.at[layer], 4 * layer + 1).start()

    def attention_out(layer):
        if layer == 0:
            drop.wait()
            for n in range(2):
                for k in range(2):
                    R.kp[n, k] = R.keep[n, k].astype(F32).astype(BF)
                save(n, "kp")
        a = proj_part(layer, chip(c))
        swap(R.sa.at[layer], R.ra.at[layer], 4 * layer + 1).wait_recv()
        a = a + R.ra[layer].astype(F32) + vec(layer, 2)
        out, hat, spread = norm(R.h[...] + R.kp[layer, 0].astype(F32) * a * (1.0 / KEEP), gain(layer, 0), vec(layer, 3))
        R.z[...] = out
        R.yh1[layer] = hat.astype(BF)
        R.r1[layer] = spread
        R.zf[layer, chip(c)] = out.astype(BF)
        here = R.zf.at[layer, chip(c)]
        swap(here, here, 4 * layer + 2).start()
        save(layer, "yh1", "r1")

    def ffn_up(layer, own):
        if not own:
            landed(R.zf.at[layer, chip(1 - c)], R.core_recv.at[4 * layer + 2])
        rows = chip(c if own else 1 - c)
        w = R.w_up0 if layer == 0 else R.w_up1
        zz = R.zf[layer, rows]
        for j in range(2):
            hid = mm(zz, flat(w.at[j])) + R.vec[j, layer : layer + 1, :]
            cdf = 0.5 + 0.5 * lax.erf(hid * 0.7071067811865476)
            R.act[layer, j, rows] = (hid * cdf).astype(BF)
            R.gp[layer, j, rows] = (cdf + hid * jnp.exp(-0.5 * hid * hid) * 0.3989422804014327).astype(BF)
        if not own:
            save(layer, "zf", "gp", "act")

    def ffn_part(layer, rows):
        w = R.w_down0 if layer == 0 else R.w_down1
        return mm(R.act[layer, 0, rows], flat(w.at[0])) + mm(R.act[layer, 1, rows], flat(w.at[1]))

    def ffn_give(layer):
        R.sf[layer] = ffn_part(layer, chip(1 - c)).astype(BF)
        swap(R.sf.at[layer], R.rf.at[layer], 4 * layer + 3).start()

    def ffn_down(layer):
        f = ffn_part(layer, chip(c))
        swap(R.sf.at[layer], R.rf.at[layer], 4 * layer + 3).wait_recv()
        f = f + R.rf[layer].astype(F32) + vec(layer, 4)
        out, hat, spread = norm(R.z[...] + R.kp[layer, 1].astype(F32) * f * (1.0 / KEEP), gain(layer, 1), vec(layer, 5))
        R.h[...] = out
        R.yh2[layer] = hat.astype(BF)
        R.r2[layer] = spread
        if layer == 0:
            R.xw[1, win(c)] = out.astype(BF)
            send_rows(1)
        save(layer, "yh2", "r2")

    def project_part(layer, part):
        if part == 0:
            project(layer, win(c), half, chip(c))
        elif part == 1:
            partner_rows_here(layer)
            project(layer, win(1 - c), half, chip(1 - c))
        else:
            edge_here(layer)
            project(layer, rows_at((1 - x) * 512, 128), 128, None)
            save(layer, "xw", "q", "k", "v")


    def out_copy(k, layer):
        name = SAVED[k]
        return pltpu.make_async_copy(getattr(R, name).at[layer], getattr(R, "o_" + name).at[layer], R.out_sem.at[k, layer])

    def save(layer, *names):
        for name in names:
            out_copy(SAVED.index(name), layer).start()

    def w_copy(b):
        return pltpu.make_async_copy(lands[b], getattr(R, "o_" + BLOCKS[b]), R.w_sem.at[b])

    def misc_copies():
        copies = [pltpu.make_async_copy(R.vec, R.o_vec, R.misc_sem.at[0])]
        if not whole:
            copies.append(pltpu.make_async_copy(R.w_pool, R.o_pool, R.misc_sem.at[1]))
            copies.append(pltpu.make_async_copy(R.w_small.at[0], R.o_piece, R.misc_sem.at[2]))
        return copies


    def pooled():
        row = mm(R.pick[...], R.h[...].astype(BF))
        R.cls_part[0] = row.astype(BF)
        first = [
            remote(R.cls_part.at[0], R.cls_part.at[1 + i], R.s1.at[i], R.r1s.at[i], dev)
            for i, dev in enumerate((xdev, cdev, xcdev))
        ]
        for cp in first:
            cp.start()
        for i, cp in enumerate(first):
            cp.wait_recv()
            row = row + R.cls_part[1 + i].astype(F32)
        here = R.cls_all.at[z, y]
        here[...] = row.astype(BF)
        second = [remote(here, here, R.s2.at[i], R.r2s.at[i], peer(k, flip)) for i, k, flip in peers]
        for cp in second:
            cp.start()
        for i, k, flip in peers:
            landed(R.cls_all.at[lax.rem(z + NZ - k, NZ), y if flip == 0 else 1 - y], R.r2s.at[i])
        if whole:
            R.cls[...] = R.cls_all[...].reshape(R.cls.shape)
            work_out_loss(R.cls, R.w_pool, R.vec, R.w_small.at[0], *[getattr(R, n) for n in LOSS_OUT + LOSS_SCR])
        else:
            R.o_cls[...] = R.cls_all[...]
        for cp in first + second:
            cp.wait_send()


    send_rows(0)
    def act(fn, *args):
        actions.append(functools.partial(fn, *args))

    actions = []
    every = range(len(BLOCKS))
    along = [b for b in every if by_z(b)]
    for b in every:
        act(launch, b)
    for b in every:
        act(complete, b)
    for b in every:
        for d in range(1, NZ):
            act(z_relay, b, d)
    for b in every:
        for k in range(1 if by_z(b) else NZ):
            act(xy_relay, b, k)
    for b in along:
        act(corner_launch, b)
    for b in along:
        for d in range(1, NZ):
            act(corner_relay, b, d)
    act(pool_launch)
    for d in range(1, NZ):
        act(pool_relay, d)
    for fn in (pool_swap, pool_done, masks, spread_params, proj_rows, pooled):
        act(fn)
    for layer in range(2):
        for k in range(3):
            act(project_part, layer, k)
        for j in range(2):
            act(attend, layer, j)
        act(attention_give, layer)
        act(attention_out, layer)
        act(ffn_up, layer, True)
        act(ffn_up, layer, False)
        act(ffn_give, layer)
        act(ffn_down, layer)
    for step in FORWARD_ORDER:
        actions[step]()

    for b in range(len(BLOCKS)):
        sends_done(b)
        if b != SMALL:
            w_copy(b).wait()
    for cp in misc_copies():
        cp.wait()
    for layer in range(2):
        for k in range(len(SAVED)):
            out_copy(k, layer).wait()
        rows_swap(layer).wait_send()
        swap(R.sa.at[layer], R.ra.at[layer], 4 * layer + 1).wait_send()
        swap(R.zf.at[layer, chip(c)], R.zf.at[layer, chip(c)], 4 * layer + 2).wait_send()
        swap(R.sf.at[layer], R.rf.at[layer], 4 * layer + 3).wait_send()

        @pl.when(c == 1 - x)
        def _():
            for cp in edge_copies(layer):
                cp.wait_send()


def work_out_loss(cls, pool, vec, piece, loss, align, unif, gw, gb, gcls, u, nb, rn, dn, dpre, table):
    z, y = lax.axis_index("z"), lax.axis_index("y")
    inner = lax.axis_size("g")
    count, width = cls.shape
    per = SEGS * inner
    pre = mm(cls[...], pool[...].reshape(width, width)) + vec[0, 18:19, :]
    value = jnp.tanh(pre)
    u[...] = value
    scale = lax.rsqrt(jnp.sum(value * value, 1, keepdims=True) + EPS)
    rn[...] = scale
    nb[...] = (value * scale).astype(BF)
    low = nb[...].astype(F32)
    squares_row = lax.dot_general(
        jnp.ones((8, width), F32), low * low, (((1,), (1,)), ((), ())),
        precision=lax.Precision.HIGHEST, preferred_element_type=F32)[0:1]
    dn[...] = jnp.zeros_like(dn)

    @pl.loop(0, count // 128)
    def _(blk):
        rows = rows_at(blk * 128, 128)
        ids = lax.broadcasted_iota(jnp.int32, (128, 1), 0) + blk * 128
        cols = lax.broadcasted_iota(jnp.int32, (1, count), 1)
        pair = jnp.zeros((128, 1), F32)
        lane = lax.broadcasted_iota(jnp.int32, (1, 128), 1)
        for o in range(NZ * NY):
            got = piece[o // NY, o % NY]
            number = got[19:20].astype(F32) * 32.0 + got[20:21].astype(F32)
            here = (ids == o * per + lane) & (lane < per)
            pair = pair + jnp.sum(jnp.where(here, number, 0.0), 1, keepdims=True)
        mine = nb[rows]
        gram = contract(mine, nb[...], 1, 1)
        logits = gram * (1.0 / TEMP)
        own = cols == ids
        twin = cols == pair.astype(jnp.int32)
        masked = jnp.where(own, -1000000000.0, logits)
        peak = jnp.max(masked, 1, keepdims=True)
        e = jnp.exp(masked - peak)
        total = jnp.sum(e, 1, keepdims=True)
        low_mine = mine.astype(F32)
        squares = jnp.sum(low_mine * low_mine, 1, keepdims=True)
        distance = squares + squares_row - 2.0 * gram
        terms = (
            peak + jnp.log(total) - jnp.sum(jnp.where(twin, logits, 0.0), 1, keepdims=True),
            jnp.sum(jnp.where(twin, distance, 0.0), 1, keepdims=True),
            jnp.log(jnp.sum(jnp.where(own, 0.0, jnp.exp(-2.0 * distance)), 1, keepdims=True) * (1.0 / (count - 1))),
        )
        for t in range(3):
            table[t, rows] = jnp.broadcast_to(terms[t], (128, 128))
        dg = ((e * (1.0 / total) - jnp.where(twin, 1.0, 0.0)) * (1.0 / TEMP)).astype(BF)
        dn[rows] += mm(dg, nb[...])
        dn[...] += contract(dg, mine, 0, 0)

    grad = dn[...]
    value = u[...]
    unit = value * rn[...]
    du = rn[...] * (grad - unit * jnp.sum(grad * unit, 1, keepdims=True))
    dpre[...] = (du * (1.0 - value * value)).astype(BF)
    dp = (z * NY + y) * inner + lax.axis_index("g")
    mine = pl.ds(pl.multiple_of(dp * SEGS, SEGS), SEGS)
    gcls[...] = contract(dpre[mine], pool[...].reshape(width, width), 1, 1)
    thin = gb.shape[1]
    columns = jnp.sum(dpre[...].astype(F32), 0, keepdims=True)
    gb[...] = pltpu.roll(jnp.broadcast_to(columns, (8, width)), lax.rem(width - dp * thin, width), 1)[0:1, 0:thin]
    part = gw.shape[0]
    turned = pltpu.roll(cls[...].astype(F32), lax.rem(width - (z * NY + y) * part, width), 1)
    gw[...] = contract(turned[:, 0:128].astype(BF), dpre[...], 0, 0)[0:part]
    for t, ref in enumerate((loss, align, unif)):
        lines = [jnp.transpose(table[t, n * 128 : (n + 1) * 128])[0:8] for n in range(count // 128)]
        line = jnp.concatenate(lines, 1)
        ref[...] = pltpu.roll(line, lax.rem(count - dp * SEGS, count), 1)[0:1, 0:SEGS]


def loss_shapes(count, width):
    one = jax.ShapeDtypeStruct((1, SEGS), F32)
    outs = [
        one, one, one,
        jax.ShapeDtypeStruct((width // (NZ * NY), width), F32),
        jax.ShapeDtypeStruct((1, width * SEGS // count), F32),
        jax.ShapeDtypeStruct((SEGS, width), F32),
    ]
    scratch = [
        pltpu.VMEM((count, width), F32),
        pltpu.VMEM((count, width), BF),
        pltpu.VMEM((count, 1), F32),
        pltpu.VMEM((count, width), F32),
        pltpu.VMEM((count, width), BF),
        pltpu.VMEM((3, count, 128), F32),
    ]
    return outs, scratch


def pooled_loss(cls, pool, vec, piece):
    outs, scratch = loss_shapes(*cls.shape)
    return pl.pallas_call(
        work_out_loss,
        out_shape=outs,
        in_specs=[VMEM] * 4,
        out_specs=[VMEM] * 6,
        scratch_shapes=scratch,
        compiler_params=pltpu.CompilerParams(vmem_limit_bytes=48 << 20),
        name="pooled_loss",
    )(cls, pool, vec, piece)


class BackwardScratch(NamedTuple):
    w_qkv: object
    w_proj: object
    w_up: object
    w_down: object
    wo: object
    dff: object
    daf: object
    send: object
    rz: object
    rh: object
    hs: object
    hr: object
    datt: object
    dq: object
    dk: object
    dv: object
    dqk: object
    dvp: object
    dwo: object
    dh: object
    dy: object
    small: object
    small_in: object
    w_sem: object
    v_sem: object
    out_sem: object
    csend: object
    crecv: object
    hsend: object
    hrecv: object
    s1: object
    rx: object
    ry: object
    rd: object
    s2: object
    r2s: object
    zs: object
    zrs: object
    bs: object
    br: object
    gx_sem: object


GRADS = ("down1", "up1", "qk1", "down0", "up0", "proj", "last")
CORNER = {"down1": "x", "up1": "y", "down0": "x"}
BWD_IN = BLOCKS[1:] + SAVED + ("vec", "seg", "gcls")
BWD_OUT = ("gx", "o_down", "o_up", "o_proj", "o_qkv", "o_small")
BWD_SCR = (
    tuple("g_" + n for n in GRADS) + tuple("zr_" + n for n in GRADS)
    + tuple("px_" + n for n in GRADS) + tuple("py_" + n for n in GRADS)
    + tuple(t + n for n in GRADS for t in (("pd_", "zd_") if n in CORNER else ("qx_", "qy_")))
    + ("st_ffn", "st_proj", "st_qkv") + tuple("v_" + n for n in SAVED)
    + BackwardScratch._fields
)
BACKWARD_ORDER = (
    23, 34, 24, 25, 26, 57, 27, 28, 31, 32, 33, 35, 29, 30, 62, 36, 38, 39, 42, 40, 58, 41, 43, 67, 44, 45, 0,
    11, 63, 37, 1, 2, 59, 3, 71, 46, 4, 68, 5, 8, 64, 60, 6, 9, 10, 12, 7, 76, 69, 13, 15, 72, 65, 16, 73, 17,
    77, 74, 18, 84, 14, 78, 47, 52, 48, 85, 80, 86, 81, 66, 19, 20, 75, 53, 49, 82, 54, 50, 70, 79, 21, 22,
    55, 87, 51, 61, 83, 56,
)


def backward_kernel(*refs):
    R = Names(BWD_IN + BWD_OUT + BWD_SCR, refs)
    z, y, x, c = position()
    up, down = z < NZ - 1, z > 0
    xdev, ydev, cdev = {"x": 1 - x}, {"y": 1 - y}, {"c": 1 - c}
    half = R.gx.shape[0]
    head = R.q.shape[3]
    width = R.gx.shape[1]


    def v_copy(name, layer):
        k = SAVED.index(name)
        return pltpu.make_async_copy(getattr(R, name).at[layer], getattr(R, "v_" + name), R.v_sem.at[k])

    def load(layer, *names):
        for name in names:
            v_copy(name, layer).start()

    def need(layer, *names):
        for name in names:
            v_copy(name, layer).wait()

    def qkv_copies(layer):
        src, dst = R.qkv, R.w_qkv
        low = 4 * head if layer == 0 else 5 * head - 64
        return [
            pltpu.make_async_copy(src.at[:, :, :, :, layer * 2 * head : (layer + 1) * 2 * head],
                                  dst.at[:, :, :, :, 0 : 2 * head], R.w_sem.at[0]),
            pltpu.make_async_copy(src.at[:, :, :, :, low : low + head + 64],
                                  dst.at[:, :, :, :, 2 * head : 3 * head + 64], R.w_sem.at[1]),
        ]

    def up_copy(layer):
        return pltpu.make_async_copy(R.up0 if layer == 0 else R.up1, R.w_up, R.w_sem.at[2])

    def down_copy(layer):
        return pltpu.make_async_copy(R.down0 if layer == 0 else R.down1, R.w_down, R.w_sem.at[3])

    def proj_copy():
        return pltpu.make_async_copy(R.proj, R.w_proj, R.w_sem.at[4])

    load(1, "yh2", "r2", "kp", "act")
    down_copy(1).start()
    load(1, "gp", "zf")
    up_copy(1).start()
    load(1, "yh1", "r1", "att")
    proj_copy().start()
    load(1, "p", "q", "k", "v", "xw")
    for cp in qkv_copies(1):
        cp.start()

    zp1 = z + 1 - 2 * lax.rem(z, 2)
    zp2 = lax.rem(z + 2, NZ)
    bar = pltpu.get_barrier_semaphore()
    for dev in (xdev, ydev, cdev, {"x": 1 - x, "c": 1 - c}):
        signal(bar, dev)
    for k in range(1, NZ):
        signal(bar, {"z": lax.rem(z + k, NZ)})


    def part(prefix, b):
        return getattr(R, prefix + b)

    def add_into(ref, *others):
        total = ref[...].astype(F32)
        for other in others:
            total = total + other.astype(F32)
        ref[...] = total.astype(BF)

    def column(kind):
        return (x, y) if kind == 0 else (1 - x, 1 - y)

    def z_copy(b, kind, k):
        n, (cx, cy), zt = GRADS.index(b), column(kind), lax.rem(z + k, NZ)
        return remote(part("g_", b).at[cx, zt, cy], part(("zr_", "zd_")[kind], b).at[k - 1],
                      R.zs.at[n, kind, k - 1], R.zrs.at[n, kind, k - 1], {"z": zt})

    def z_start(b, kind):
        for k in range(1, NZ):
            z_copy(b, kind, k).start()

    def z_landed(b, kind):
        ref = part(("zr_", "zd_")[kind], b)
        for k in range(NZ - 1):
            landed(ref.at[k], R.zrs.at[GRADS.index(b), kind, k])
        return [ref[k] for k in range(NZ - 1)]

    def wide(b):
        n = GRADS.index(b)
        if CORNER[b] == "x":
            return remote(part("g_", b).at[1 - x, :, y], part("px_", b), R.s1.at[n, 0], R.rx.at[n, 0], xdev)
        return remote(part("g_", b).at[x, :, 1 - y], part("py_", b), R.s1.at[n, 0], R.ry.at[n, 0], ydev)

    def narrow(b, k):
        n, zk = GRADS.index(b), lax.rem(z + k, NZ)
        if CORNER[b] == "x":
            return remote(part("g_", b).at[x, zk, 1 - y], part("py_", b).at[zk], R.s1.at[n, 1 + k], R.ry.at[n, zk], ydev)
        return remote(part("g_", b).at[1 - x, zk, y], part("px_", b).at[zk], R.s1.at[n, 1 + k], R.rx.at[n, zk], xdev)

    def corner_share(b):
        n = GRADS.index(b)
        return remote(part("g_", b).at[1 - x, z, 1 - y], part("pd_", b), R.s1.at[n, 1 + NZ], R.rd.at[n],
                      xdev if CORNER[b] == "x" else ydev)

    def corner_first(b):
        wide(b).start()
        for k in range(1, NZ):
            narrow(b, k).start()
        z_start(b, 1)

    def corner_out(b):
        add_into(part("g_", b).at[1 - x, z, 1 - y], *z_landed(b, 1))
        corner_share(b).start()

    def corner_in(b):
        corner_share(b).wait_recv()
        here = part("g_", b).at[x, z, 1 - y] if CORNER[b] == "x" else part("g_", b).at[1 - x, z, y]
        add_into(here, part("pd_", b)[...])
        narrow(b, 0).start()

    def corner_join(b):
        n = GRADS.index(b)
        px, py = part("px_", b), part("py_", b)
        wide(b).wait_recv()
        for k in range(NZ):
            if CORNER[b] == "x":
                landed(py.at[k], R.ry.at[n, k])
            else:
                landed(px.at[k], R.rx.at[n, k])

        @pl.loop(0, NZ)
        def _(k):
            add_into(part("g_", b).at[x, k, y], px[k], py[k])

        z_start(b, 0)

    def split(b):
        return part("g_", b).shape[3] // 48 * 16

    def first(b):
        n, h, g = GRADS.index(b), split(b), part("g_", b)
        return (
            remote(g.at[1 - x, :, :, 0:h], part("px_", b), R.s1.at[n, 0], R.rx.at[n, 0], xdev),
            remote(g.at[:, :, 1 - y, h:], part("py_", b), R.s1.at[n, 1], R.ry.at[n, 0], ydev),
        )

    def second(b):
        n, h, g = GRADS.index(b), split(b), part("g_", b)
        return (
            remote(g.at[x, :, 1 - y, 0:h], part("qy_", b), R.s2.at[n, 0], R.r2s.at[n, 0], ydev),
            remote(g.at[1 - x, :, y, h:], part("qx_", b), R.s2.at[n, 1], R.r2s.at[n, 1], xdev),
        )

    def plane_first(b):
        for cp in first(b):
            cp.start()

    def plane_second(b):
        h, g = split(b), part("g_", b)
        px, py = part("px_", b), part("py_", b)
        for cp in first(b):
            cp.wait_recv()

        @pl.loop(0, NZ)
        def _(k):
            for yy in range(NY):
                add_into(g.at[x, k, yy, 0:h], px[k, yy])
            for xx in range(2):
                add_into(g.at[xx, k, y, h:], py[xx, k])

        for cp in second(b):
            cp.start()

    def plane_join(b):
        h, g = split(b), part("g_", b)
        qx, qy = part("qx_", b), part("qy_", b)
        for cp in second(b):
            cp.wait_recv()

        @pl.loop(0, NZ)
        def _(k):
            add_into(g.at[x, k, y, 0:h], qy[k])
            add_into(g.at[x, k, y, h:], qx[k])

        z_start(b, 0)

    def out_copies(b):
        sem = R.out_sem.at[GRADS.index(b)]
        if b[:-1] in ("down", "up"):
            return [pltpu.make_async_copy(R.st_ffn, part("o_", b[:-1]).at[int(b[-1])], sem.at[0])]
        if b == "proj":
            rows = R.o_proj.shape[1]
            return [pltpu.make_async_copy(R.st_proj.at[n * rows : (n + 1) * rows], R.o_proj.at[n], sem.at[n]) for n in range(2)]
        places = ((1, 0), (1, 1)) if b == "qk1" else ((0, 0), (0, 1), (0, 2), (1, 2))
        return [pltpu.make_async_copy(R.st_qkv.at[p], R.o_qkv.at[p], sem.at[k]) for k, p in enumerate(places)]

    ffn_done = []

    def finish(b):
        if b[:-1] in ("down", "up"):
            if ffn_done:
                for cp in out_copies(ffn_done[-1]):
                    cp.wait()
            ffn_done.append(b)
        total = part("g_", b)[x, z, y].astype(F32)
        for other in z_landed(b, 0):
            total = total + other.astype(F32)
        if b[:-1] in ("down", "up"):
            R.st_ffn[...] = total
        elif b == "proj":
            R.st_proj[...] = total
        else:
            places = ((1, 0), (1, 1)) if b == "qk1" else ((0, 0), (0, 1), (0, 2), (1, 2))
            for k, p in enumerate(places):
                R.st_qkv[p] = total[:, k * head : (k + 1) * head]
        for cp in out_copies(b):
            cp.start()

    def sends_done(b):
        if b in CORNER:
            copies = [wide(b), corner_share(b)] + [narrow(b, k) for k in range(NZ)]
        else:
            copies = first(b) + second(b)
        for cp in copies:
            cp.wait_send()
        for kind in (0, 1) if b in CORNER else (0,):
            for k in range(1, NZ):
                z_copy(b, kind, k).wait_send()
        if not (b[:-1] in ("down", "up") and b != ffn_done[-1]):
            for cp in out_copies(b):
                cp.wait()


    def chip(core):
        return rows_at(core * half, half)

    def win(core):
        return rows_at(x * 128 + core * half, half)

    def swap(src, dst, n):
        return remote(src, dst, R.csend.at[n], R.crecv.at[n], cdev)

    def gain(layer, k):
        return R.vec[0, 14 + 2 * layer + k : 15 + 2 * layer + k, :]

    def note(row, value):
        R.small[row : row + 1, :] = value

    def norm_back(grad, g_row, hat, spread):
        scaled = grad * g_row
        first_mean = jnp.mean(scaled, 1, keepdims=True)
        second_mean = jnp.mean(scaled * hat, 1, keepdims=True)
        return spread * (scaled - first_mean - hat * second_mean)

    def ffn_norm(layer):
        need(layer, "yh2", "r2", "kp")
        grad, hat = R.dh[...], R.v_yh2[...].astype(F32)
        note(12 + 2 * layer + 1, jnp.sum(grad * hat, 0, keepdims=True))
        note(6 * layer + 5, jnp.sum(grad, 0, keepdims=True))
        dy = norm_back(grad, gain(layer, 1), hat, R.v_r2[...])
        R.dy[...] = dy
        df = dy * R.v_kp[1].astype(F32) * (1.0 / KEEP)
        note(6 * layer + 4, jnp.sum(df, 0, keepdims=True))
        R.dff[chip(c)] = df.astype(BF)
        here = R.dff.at[chip(c)]
        if layer == 1:
            pl.semaphore_wait(bar, 4 + NZ - 1)
        swap(here, here, 4 * layer).start()
        if layer == 1:
            load(0, "yh2", "r2")

    def ffn_wait(layer):
        here = R.dff.at[chip(c)]
        swap(here, here, 4 * layer).wait_send()
        landed(R.dff.at[chip(1 - c)], R.crecv.at[4 * layer])

    def as_block(value):
        return value.astype(BF).reshape(NZ, NY, -1, value.shape[1])

    def down_grad(layer, j):
        if j == 0:
            need(layer, "act")
        (R.g_down1 if layer else R.g_down0)[j] = as_block(contract(R.v_act[j], R.dff[...], 0, 0))
        if layer == 1 and j == 1:
            load(0, "act")

    def units_back(layer, j):
        if j == 0:
            need(layer, "gp")
            down_copy(layer).wait()
        total = jnp.zeros((1, width), F32)
        for core in range(2):
            rows = pl.ds(core * half, half)
            dact = contract(R.dff[rows], flat(R.w_down.at[j]), 1, 1)
            dhid = (dact * R.v_gp[j, rows].astype(F32)).astype(BF)
            R.v_gp[j, rows] = dhid
            total = total + jnp.sum(dhid.astype(F32), 0, keepdims=True)
        keep_row = jnp.where(c == 0, 1.0, 0.0)
        note(16 + 4 * layer + 2 * j, total * keep_row)
        note(16 + 4 * layer + 2 * j + 1, total * (1.0 - keep_row))
        if layer == 1 and j == 1:
            down_copy(0).start()

    def up_grad(layer, j):
        if j == 0:
            need(layer, "zf")
        (R.g_up1 if layer else R.g_up0)[j] = as_block(contract(R.v_zf[...], R.v_gp[j], 0, 0))
        if layer == 1 and j == 1:
            load(0, "zf")

    def mid_part(rows):
        return contract(R.v_gp[0, rows], flat(R.w_up.at[0]), 1, 1) + contract(R.v_gp[1, rows], flat(R.w_up.at[1]), 1, 1)

    def mid_give(layer):
        up_copy(layer).wait()
        R.send[...] = mid_part(chip(1 - c)).astype(BF)
        swap(R.send, R.rz, 4 * layer + 1).start()

    def mid_own(layer):
        R.dy[...] += mid_part(chip(c))

    def mid_norm(layer):
        need(layer, "yh1", "r1")
        swap(R.send, R.rz, 4 * layer + 1).wait()
        grad, hat = R.dy[...] + R.rz[...].astype(F32), R.v_yh1[...].astype(F32)
        note(12 + 2 * layer, jnp.sum(grad * hat, 0, keepdims=True))
        note(6 * layer + 3, jnp.sum(grad, 0, keepdims=True))
        dy = norm_back(grad, gain(layer, 0), hat, R.v_r1[...])
        R.dy[...] = dy
        da = dy * R.v_kp[0].astype(F32) * (1.0 / KEEP)
        note(6 * layer + 2, jnp.sum(da, 0, keepdims=True))
        R.daf[chip(c)] = da.astype(BF)
        here = R.daf.at[chip(c)]
        swap(here, here, 4 * layer + 2).start()
        if layer == 1:
            load(0, "yh1", "r1", "kp")

    def free_ffn(layer):
        up_copy(0).start()
        load(0, "gp")

    def proj_rows_back(layer):
        if layer == 1:
            proj_copy().wait()
        for j in range(2):
            value = R.w_proj[j].astype(F32)
            rows = value.shape[2] // 2
            value = value[:, :, layer * rows : (layer + 1) * rows].reshape(-1, value.shape[3])
            R.wo[j] = value.astype(BF)

    def proj_wait(layer):
        here = R.daf.at[chip(c)]
        swap(here, here, 4 * layer + 2).wait_send()
        landed(R.daf.at[chip(1 - c)], R.crecv.at[4 * layer + 2])

    def proj_back(layer):
        for j in range(2):
            for core in range(2):
                rows = pl.ds(core * half, half)
                R.datt[j, rows] = contract(R.daf[rows], R.wo[j], 1, 1).astype(BF)

    def proj_grad(layer):
        need(layer, "att")
        for j in range(2):
            grad = contract(R.v_att[j], R.daf[...], 0, 0)
            if layer == 1:
                R.dwo[j] = grad.astype(BF)
            else:
                both = [v.reshape(NZ * NY, -1, width) for v in (grad, R.dwo[j].astype(F32))]
                R.g_proj[j] = as_block(jnp.concatenate(both, 1).reshape(-1, width))
        if layer == 1:
            load(0, "att")

    def attend_back(layer, j):
        if j == 0:
            need(layer, "p", "q", "k", "v")
        lane = lax.broadcasted_iota(jnp.int32, (1, head), 1) // HEAD_DIM
        picks = [(lane == n).astype(F32) for n in range(head // HEAD_DIM)]
        count = len(picks)
        R.dk[...] = jnp.zeros_like(R.dk)
        R.dv[...] = jnp.zeros_like(R.dv)
        R.dq[...] = jnp.zeros_like(R.dq)

        @pl.loop(0, 4)
        def _(i):
            keys = rows_at((3 * (x + i) + 1) // 5 * 128, 384)
            mine = rows_at(i * 128, 128)
            kk = R.v_k[j, keys]
            qq, dd = R.v_q[j, mine], R.datt[j, mine]
            q3 = jnp.concatenate([qq * pick.astype(BF) for pick in picks], 0)
            d3 = jnp.concatenate([dd * pick.astype(BF) for pick in picks], 0)
            p3 = R.v_p[j, i]
            dp = contract(d3, R.v_v[j, keys], 1, 1)
            pf = p3.astype(F32)
            ds = (pf * (dp - jnp.sum(pf * dp, 1, keepdims=True))).astype(BF)
            R.dv[keys] += contract(p3, d3, 0, 0)
            R.dk[keys] += contract(ds, q3, 0, 0)
            dq = mm(ds, kk)
            total = dq[0:128] * picks[0]
            for n in range(1, count):
                total = total + dq[n * 128 : (n + 1) * 128] * picks[n]
            R.dq[rows_at(x * 128 + i * 128, 128)] = total * 0.125

        dq, dk, dv = (v[...].astype(BF).astype(F32) for v in (R.dq, R.dk, R.dv))
        R.dqk[j] = jnp.concatenate([dq, dk], 1).astype(BF)
        gap = jnp.zeros((dv.shape[0], 64), F32)
        R.dvp[j] = jnp.concatenate([dv, gap] if layer == 0 else [gap, dv], 1).astype(BF)
        own = jnp.where(c == 0, 1.0, 0.0)
        for row, value in ((0, dq), (1, dv)):
            line = jnp.sum(value, 0, keepdims=True)
            pair = [line * own, line * (1.0 - own)]
            zero = jnp.zeros((1, 2 * head), F32)
            if j == 0:
                note(6 * layer + row, jnp.concatenate(pair + [zero], 1))
            else:
                R.small[6 * layer + row : 6 * layer + row + 1, :] += jnp.concatenate([zero] + pair, 1)
        if layer == 1 and j == 1:
            load(0, "p", "q", "k", "v")

    def qkv_grad(layer, j):
        if j == 0:
            need(layer, "xw")
        gqk = as_block(contract(R.v_xw[...], R.dqk[j], 0, 0))
        gv = as_block(contract(R.v_xw[...], R.dvp[j], 0, 0))
        if layer == 1:
            R.g_qk1[j] = gqk
            R.g_last[j, :, :, :, 3 * head - 64 :] = gv
        else:
            R.g_last[j, :, :, :, 0 : 2 * head] = gqk
            R.g_last[j, :, :, :, 2 * head : 2 * head + 128] = gv[..., 0:128]
            R.g_last[j, :, :, :, 2 * head + 128 : 3 * head + 64] += gv[..., 128:]
        if layer == 1 and j == 1:
            load(0, "xw")

    def in_part(rows):
        total = None
        for j in range(2):
            w = R.w_qkv.at[j]
            wqk = w[:, :, :, 0 : 2 * head].reshape(width, 2 * head)
            wv = w[:, :, :, 2 * head :].reshape(width, head + 64)
            term = contract(R.dqk[j, rows], wqk, 1, 1) + contract(R.dvp[j, rows], wv, 1, 1)
            total = term if total is None else total + term
        return total

    def halo_copy(layer):
        return remote(R.hs, R.hr.at[layer, c], R.hsend.at[layer], R.hrecv.at[layer, c], {"x": 1 - x, "c": x})

    def in_halo(layer):
        for cp in qkv_copies(layer):
            cp.wait()
        R.hs[...] = in_part(rows_at((1 - x) * 512, 128)).astype(BF)
        halo_copy(layer).start()

    def in_give(layer):
        R.send[...] = in_part(win(1 - c)).astype(BF)
        swap(R.send, R.rh, 4 * layer + 3).start()

    def in_own(layer):
        R.dh[...] = R.dy[...] + in_part(win(c))
        if layer == 1:
            for again in qkv_copies(0):
                again.start()

    def in_sum(layer):
        swap(R.send, R.rh, 4 * layer + 3).wait()
        R.dh[...] += R.rh[...].astype(F32)

        @pl.when(c == 1 - x)
        def _():
            edge = rows_at(128 * c, 128)
            for core in range(2):
                landed(R.hr.at[layer, core], R.hrecv.at[layer, core])
                R.dh[edge] += R.hr[layer, core].astype(F32)

        halo_copy(layer).wait_send()
        if layer == 0:
            gx_copy.start()


    def small_copy(k):
        dev = (cdev, xdev, ydev, {"z": zp1}, {"z": zp2})[k]
        return remote(R.small, R.small_in.at[k], R.bs.at[k], R.br.at[k], dev)

    def small_give(k):
        small_copy(k).start()

    def small_sum(k):
        small_copy(k).wait()
        R.small[...] += R.small_in[k]


    total = R.seg.shape[1]
    number = lax.broadcasted_iota(jnp.int32, (SEGS, total), 0)
    before = (jnp.broadcast_to(R.seg[...], (SEGS, total)) < number).astype(F32)
    starts = jnp.sum(before, 1, keepdims=True).astype(jnp.int32)
    mine = lax.broadcasted_iota(jnp.int32, (SEGS, half), 1) + (2 * x + c) * half
    pick = (mine == starts).astype(F32)
    R.dh[...] = lax.dot_general(
        pick, R.gcls[...], (((0,), (0,)), ((), ())), precision=lax.Precision.HIGHEST, preferred_element_type=F32)

    gx_copy = pltpu.make_async_copy(R.dh, R.gx, R.gx_sem)
    def act(fn, *args):
        actions.append(functools.partial(fn, *args))

    actions = []
    for layer in range(2):
        act(ffn_norm, layer)
        act(ffn_wait, layer)
        for fn in (down_grad, units_back, up_grad):
            act(fn, layer, 0)
            act(fn, layer, 1)
        for fn in (mid_give, mid_own, mid_norm, proj_rows_back, proj_wait, proj_back, proj_grad):
            act(fn, layer)
        for fn in (attend_back, qkv_grad):
            act(fn, layer, 0)
            act(fn, layer, 1)
        for fn in (in_halo, in_give, in_own, in_sum):
            act(fn, layer)
    act(free_ffn, 1)
    for k in range(5):
        act(small_give, k)
    for k in range(5):
        act(small_sum, k)
    for b in GRADS:
        if b in CORNER:
            act(corner_first, b)
            for fn in (corner_out, corner_in, corner_join):
                act(fn, b)
        else:
            for fn in (plane_first, plane_second, plane_join):
                act(fn, b)
        act(finish, b)
    for step in BACKWARD_ORDER:
        actions[step]()
    R.o_small[...] = R.small[...]
    gx_copy.wait()
    for b in GRADS:
        sends_done(b)


def saved_shapes(half, width):
    head = width // 4
    return {
        "xw": ((640, width), BF),
        "q": ((2, 512, head), BF),
        "k": ((2, 640, head), BF),
        "v": ((2, 640, head), BF),
        "p": ((2, 4, 384, 384), BF),
        "att": ((2, 512, head), BF),
        "zf": ((512, width), BF),
        "gp": ((2, 512, width), BF),
        "act": ((2, 512, width), BF),
        "yh1": ((half, width), BF),
        "yh2": ((half, width), BF),
        "r1": ((half, 1), F32),
        "r2": ((half, 1), F32),
        "kp": ((2, half, width), BF),
    }


def run_forward(whole, wqkv, wout, up, down, b_in, biases, gains, pool_b, pairing, pool, tok, seg, drop):
    half, width = tok.shape
    rows = up.shape[1]
    cut = {n: up.shape[1:] for n in BLOCKS}
    cut["small"] = (32, 128)
    cut["qkv"] = (rows, 6 * wqkv.shape[3])
    cut["proj"] = (2 * wout.shape[1], width)
    saved = saved_shapes(half, width)
    head = width // 4
    dma = pltpu.SemaphoreType.DMA
    land = [(2, NZ, NY, *cut[n]) for n in BLOCKS]
    nb = len(BLOCKS)
    loss_outs, loss_scratch = loss_shapes(NZ * NY * SEGS, width)
    shape = jax.ShapeDtypeStruct
    outs = [shape(s, BF) for s in land[1:]]
    outs.append(shape((2, 32, width), F32))
    if whole:
        outs += loss_outs
    else:
        outs += [
            shape((NZ, NY, *pool.shape), BF),
            shape((NZ, NY, *cut["small"]), BF),
            shape((NZ, NY, SEGS, width), BF),
        ]
    outs += [shape((2, *s), t) for s, t in saved.values()]
    names = forward_out(whole)
    out_specs = [VMEM if n in LOSS_OUT + ("o_cls",) else ANY for n in names]
    scratch = [pltpu.VMEM(s, BF) for s in land]
    scratch += [
        pltpu.VMEM((NZ, NY, *pool.shape), BF),
        pltpu.VMEM((4, SEGS, width), BF),
        pltpu.VMEM((NZ, NY, SEGS, width), BF),
    ]
    scratch += [pltpu.VMEM((2, *s), t) for s, t in saved.values()]
    scratch += [
        pltpu.VMEM(drop.shape, drop.dtype),
        pltpu.VMEM((4, 128, 384), F32),
        pltpu.VMEM((2, 2, head, width), BF),
        pltpu.VMEM((2, 32, width), F32),
        pltpu.VMEM((2, 32, head), F32),
        pltpu.VMEM((half, width), F32),
        pltpu.VMEM((half, width), F32),
    ]
    scratch += [pltpu.VMEM((2, half, width), BF)] * 4
    scratch += [
        dma((nb, 4 * NZ)), dma((nb, 2 * NZ)), dma((nb, 2 * NZ)), dma((nb, 2, NZ, NY)), dma((nb,)),
        dma((3 * NZ,)), dma((NZ, NY)), dma, dma((2,)),
        dma((8,)), dma((8,)), dma((2, 2)), dma((2,)), dma, dma((len(SAVED), 2)), dma((nb,)), dma((3,)),
        dma((3,)), dma((3,)), dma((NZ * NY,)), dma((NZ * NY,)),
        pltpu.VMEM(cut["small"], F32),
        pltpu.VMEM(cut["small"], BF),
        pltpu.VMEM(cut["qkv"], BF),
        pltpu.VMEM(cut["proj"], BF),
        pltpu.VMEM((NZ * NY * SEGS, width), BF),
        pltpu.VMEM((SEGS, half), BF),
    ]
    if whole:
        scratch += loss_scratch
    res = pl.pallas_call(
        functools.partial(forward_kernel, whole),
        out_shape=outs,
        in_specs=[VMEM, VMEM, ANY, ANY] + [VMEM] * 5 + [ANY, VMEM, VMEM, ANY],
        out_specs=out_specs,
        scratch_shapes=scratch,
        compiler_params=pltpu.CompilerParams(collective_id=1, has_side_effects=True, vmem_limit_bytes=60 << 20),
        name="forward",
    )(wqkv, wout, up, down, b_in, biases, gains, pool_b, pairing, pool, tok, seg, drop)
    return dict(zip(names, res))


def run_backward(weights, saved, vec, seg, gcls):
    width = vec.shape[2]
    half = saved[SAVED.index("yh1")].shape[1]
    head = width // 4
    dma = pltpu.SemaphoreType.DMA
    by_name = dict(zip(BLOCKS[1:], weights))
    rows, wide = by_name["up0"].shape[3:]
    thin = by_name["proj"].shape[3]
    cut = {n: (rows, wide) for n in GRADS}
    cut["proj"] = (thin, width)
    cut["qk1"] = (rows, 2 * head)
    cut["last"] = (rows, 4 * head)
    nb = len(GRADS)
    shape = jax.ShapeDtypeStruct
    outs = [
        shape((half, width), F32),
        shape((2, rows, wide), F32),
        shape((2, rows, wide), F32),
        shape((2, thin // 2, width), F32),
        shape((2, 3, rows, head), F32),
        shape((24, width), F32),
    ]

    def low(*dims):
        return pltpu.VMEM(dims, BF)

    def full(*dims):
        return pltpu.VMEM(dims, F32)

    scratch = [low(2, NZ, NY, *cut[n]) for n in GRADS]
    scratch += [low(NZ - 1, *cut[n]) for n in GRADS]
    split = {n: cut[n][0] // 48 * 16 for n in GRADS}
    for n in GRADS:
        r, w = cut[n]
        scratch.append(low(NZ, r, w) if n in CORNER else low(NZ, NY, split[n], w))
    for n in GRADS:
        r, w = cut[n]
        scratch.append(low(NZ, r, w) if n in CORNER else low(2, NZ, r - split[n], w))
    for n in GRADS:
        r, w = cut[n]
        if n in CORNER:
            scratch += [low(r, w), low(NZ - 1, r, w)]
        else:
            scratch += [low(NZ, r - split[n], w), low(NZ, split[n], w)]
    scratch += [full(rows, wide), full(*cut["proj"]), full(2, 3, rows, head)]
    scratch += [pltpu.VMEM(s, t) for s, t in saved_shapes(half, width).values()]
    scratch += [
        low(2, NZ, NY, rows, 3 * head + 64),
        low(*by_name["proj"].shape),
        low(*by_name["up0"].shape),
        low(*by_name["down0"].shape),
        low(2, head, width),
        low(512, width),
        low(512, width),
        low(half, width),
        low(half, width),
        low(half, width),
        low(128, width),
        low(2, 2, 128, width),
        low(2, 512, head),
        full(640, head),
        full(640, head),
        full(640, head),
        low(2, 640, 2 * head),
        low(2, 640, head + 64),
        low(2, head, width),
        full(half, width),
        full(half, width),
        full(24, width),
        full(5, 24, width),
    ]
    scratch += [
        dma((5,)), dma((len(SAVED),)), dma((nb, 4)), dma((8,)), dma((8,)), dma((2,)), dma((2, 2)),
        dma((nb, NZ + 2)), dma((nb, NZ)), dma((nb, NZ)), dma((nb,)), dma((nb, 2)), dma((nb, 2)),
        dma((nb, 2, NZ - 1)), dma((nb, 2, NZ - 1)), dma((5,)), dma((5,)), dma,
    ]
    return pl.pallas_call(
        backward_kernel,
        out_shape=outs,
        in_specs=[ANY] * (len(weights) + len(saved)) + [VMEM] * 3,
        out_specs=[ANY] * 5 + [VMEM],
        scratch_shapes=scratch,
        compiler_params=pltpu.CompilerParams(collective_id=2, has_side_effects=True, vmem_limit_bytes=63 << 20),
        name="backward",
    )(*weights, *saved, vec, seg, gcls)


def hand_over_kernel(*refs):
    ins, outs, held, sem = refs[:11], refs[11:24], refs[24:30], refs[30]
    loads = [pltpu.make_async_copy(ins[k], held[k], sem.at[0, k]) for k in range(6)]
    moves = [pltpu.make_async_copy(held[k], outs[k], sem.at[1, k]) for k in range(6)]
    for cp in loads:
        cp.start()
    for k in range(6, 10):
        outs[k][...] = ins[k][...]
    sums = ins[10]
    z, y, x, c = position()
    m, dp = 2 * x + c, z * NY + y
    b_in, biases, gains = outs[10:]
    width = sums.shape[1]
    thin, part = biases.shape[2], b_in.shape[1]
    turned = pltpu.roll(sums[0:16], lax.rem(width - (dp * part + m * thin), width), 1)
    for layer in range(2):
        for k in range(6):
            biases[k, layer : layer + 1] = turned[6 * layer + k : 6 * layer + k + 1, 0:thin]
        gains[layer] = turned[12 + 2 * layer : 14 + 2 * layer, 0:thin]
    turned = pltpu.roll(sums[16:24], lax.rem(width - dp * part, width), 1)
    for layer in range(2):
        total = jnp.zeros((1, part), F32)
        for k in range(4):
            total = total + turned[4 * layer + k : 4 * layer + k + 1, 0:part] * jnp.where(m == k, 1.0, 0.0)
        b_in[layer : layer + 1] = total
    for load, move in zip(loads, moves):
        load.wait()
        move.start()
    for cp in moves:
        cp.wait()


def hand_over(large, small, sums):
    shape = jax.ShapeDtypeStruct
    width = sums.shape[1]
    part = width // (NZ * NY)
    outs = [shape(v.shape, v.dtype) for v in large + small]
    outs += [shape((2, part), F32), shape((6, 2, part // 4), F32), shape((2, 2, part // 4), F32)]
    return pl.pallas_call(
        hand_over_kernel,
        out_shape=outs,
        in_specs=[ANY] * len(large) + [VMEM] * (len(small) + 1),
        out_specs=[ANY] * len(large) + [VMEM] * (len(small) + 3),
        scratch_shapes=[pltpu.VMEM(v.shape, v.dtype) for v in large] + [pltpu.SemaphoreType.DMA((2, len(large)))],
        name="hand_over",
    )(*large, *small, sums)


def per_device(tokens_in, segments, pairing, drop_masks, w_qkv, w_out, w_in, w_back, b_in, biases,
               gains, pool_w, pool_b):
    inner = lax.axis_size("g")
    layers = w_qkv.shape[0]
    width = tokens_in.shape[1]
    z, y, x, c = position()
    m = 2 * x + c
    dp = (z * NY + y) * inner + lax.axis_index("g")

    def group(arr, dim):
        return arr if inner == 1 else lax.all_gather(arr, "g", axis=dim, tiled=True)

    w_qkv, w_out, w_in, w_back = group(w_qkv, 2), group(w_out, 1), group(w_in, 1), group(w_back, 1)
    b_in, biases, gains = group(b_in, 1), group(biases, 2), group(gains, 2)
    pool_w, pool_b, pairing = group(pool_w, 0), group(pool_b, 0), group(pairing, 0)
    rows = w_in.shape[1]
    named = run_forward(
        inner == 1, w_qkv, w_out, w_in, w_back, b_in, jnp.transpose(biases, (1, 0, 2)), gains, pool_b[None], pairing[None], pool_w,
        tokens_in, segments, drop_masks)
    if inner == 1:
        loss, align, unif, grad_pool_w, grad_pool_b, gcls = (named[n] for n in LOSS_OUT)
    else:
        cls = named["o_cls"].reshape(NZ * NY, SEGS, width)
        cls = lax.all_gather(cls, "g", axis=1, tiled=True).reshape(-1, width)
        loss, align, unif, grad_pool_w, grad_pool_b, gcls = pooled_loss(
            cls, named["o_pool"], named["o_vec"], named["o_piece"])
    weights = [named["o_" + n] for n in BLOCKS[1:]]
    saved = [named["o_" + n] for n in SAVED]
    grad_x, down, up, proj, qkv, sums = run_backward(weights, saved, named["o_vec"], segments, gcls)

    if inner == 1:
        large = [grad_x, qkv, proj, up, down, grad_pool_w]
        small = [loss, align, unif, grad_pool_b]
        res = hand_over(large, small, sums)
        grad_x, qkv, proj, up, down, grad_pool_w, loss, align, unif, grad_pool_b, out_b_in, out_biases, out_gains = res
        return (
            loss[0], align[0], unif[0], grad_x, qkv, proj, up, down, out_b_in,
            jnp.transpose(out_biases, (1, 0, 2)), out_gains, grad_pool_w, grad_pool_b[0],
        )

    def spread(values, dim):
        return lax.psum_scatter(values, "g", scatter_dimension=dim, tiled=True)

    sums = lax.psum(sums, "g")
    thin = rows // (4 * inner)
    here = lax.dynamic_slice_in_dim(sums[:16], dp * 4 * thin + m * thin, thin, 1)
    up_sums = sums[16:24].reshape(layers, 4 * width)
    n_up = rows // inner
    out_b_in = lax.dynamic_slice_in_dim(up_sums, m * width + dp * n_up, n_up, 1)
    n_pool = pool_w.shape[0] // inner
    g = lax.axis_index("g")
    grad_pool_w = lax.dynamic_slice_in_dim(grad_pool_w, g * n_pool, n_pool, 0)
    return (
        loss[0],
        align[0],
        unif[0],
        grad_x,
        spread(qkv, 2),
        spread(proj, 1),
        spread(up, 1),
        spread(down, 1),
        out_b_in,
        here[:12].reshape(layers, 6, thin),
        here[12:].reshape(layers, 2, thin),
        grad_pool_w,
        grad_pool_b[0],
    )


def solution(mesh):
    count = mesh.shape["dp"]
    fine = Mesh(
        mesh.devices.reshape(NZ, NY, count // (NZ * NY), 2, 2), ("z", "y", "g", "x", "c")
    )
    dp, mp = ("z", "y", "g"), ("x", "c")
    in_specs = (
        P(dp + mp, None),
        P(dp, None),
        P(dp),
        P(None, None, dp + mp, None),
        P(None, None, dp, mp),
        P(None, mp + dp, None),
        P(None, dp, mp),
        P(None, mp + dp, None),
        P(None, mp + dp),
        P(None, None, dp),
        P(None, None, dp),
        P(dp, None),
        P(dp),
    )
    out_specs = (
        P(dp),
        P(dp),
        P(dp),
        P(dp + mp, None),
        P(None, None, dp, mp),
        P(None, mp + dp, None),
        P(None, dp, mp),
        P(None, mp + dp, None),
        P(None, mp + dp),
        P(None, None, dp + mp),
        P(None, None, dp + mp),
        P(dp, None),
        P(dp),
    )
    return jax.shard_map(
        per_device, mesh=fine, in_specs=in_specs, out_specs=out_specs, check_vma=False
    )
```
